32 devices in a mesh: dp: 8 (over z, core), seq: 4 (over y, x).
Axes of the slice: x: 2, y: 2, z: 4, core: 2. Of those that a mesh axis runs over, the one named last changes fastest.
Arguments:
- inputs: bfloat16 [16, 1024, 1024], P('dp', 'seq'), may hold values from -6 to 6
- cotangent: bfloat16 [16, 1024, 1024], P('dp', 'seq'), may hold values from -6 to 6
- segments: int32 [16, 1024], P('dp', 'seq'), may hold values from 0 to 4, as said below
- w_in: float32 [1024, 3072], P(('dp', 'seq')), may hold values from -0.1875 to 0.1875
- w_out: float32 [1024, 1024], P(('dp', 'seq')), may hold values from -0.1875 to 0.1875
- conv_w: float32 [3, 1024], P(None, ('dp', 'seq')), may hold values from -3.5 to 3.5
- w_gate: float32 [1024, 4608], P(('dp', 'seq')), may hold values from -0.1875 to 0.1875
- w_up: float32 [1024, 4608], P(('dp', 'seq')), may hold values from -0.1875 to 0.1875
- w_down: float32 [4608, 1024], P(('dp', 'seq')), may hold values from -0.09375 to 0.09375
- gains: float32 [2, 1024], P(None, ('dp', 'seq')), may hold values from 0.5 to 1.5
- m_in: float32 [1024, 3072], P(('dp', 'seq')), may hold values from -80 to 80
- m_out: float32 [1024, 1024], P(('dp', 'seq')), may hold values from -96 to 96
- m_conv: float32 [3, 1024], P(None, ('dp', 'seq')), may hold values from -80 to 80
- m_gate: float32 [1024, 4608], P(('dp', 'seq')), may hold values from -24 to 24
- m_up: float32 [1024, 4608], P(('dp', 'seq')), may hold values from -24 to 24
- m_down: float32 [4608, 1024], P(('dp', 'seq')), may hold values from -48 to 48
- m_gains: float32 [2, 1024], P(None, ('dp', 'seq')), may hold values from -80 to 80
- v_in: float32 [1024, 3072], P(('dp', 'seq')), may hold values from 868.352 to 3440.64
- v_out: float32 [1024, 1024], P(('dp', 'seq')), may hold values from 1245.184 to 4915.2
- v_conv: float32 [3, 1024], P(None, ('dp', 'seq')), may hold values from 868.352 to 3440.64
- v_gate: float32 [1024, 4608], P(('dp', 'seq')), may hold values from 78.6432 to 311.296
- v_up: float32 [1024, 4608], P(('dp', 'seq')), may hold values from 78.6432 to 311.296
- v_down: float32 [4608, 1024], P(('dp', 'seq')), may hold values from 311.296 to 1245.184
- v_gains: float32 [2, 1024], P(None, ('dp', 'seq')), may hold values from 868.352 to 3440.64
Outputs:
- output: bfloat16 [16, 1024, 1024], P('dp', 'seq')
- input_grad: float32 [16, 1024, 1024], P('dp', 'seq')
- new_w_in: float32 [1024, 3072], P(('dp', 'seq'))
- new_w_out: float32 [1024, 1024], P(('dp', 'seq'))
- new_conv_w: float32 [3, 1024], P(None, ('dp', 'seq'))
- new_w_gate: float32 [1024, 4608], P(('dp', 'seq'))
- new_w_up: float32 [1024, 4608], P(('dp', 'seq'))
- new_w_down: float32 [4608, 1024], P(('dp', 'seq'))
- new_gains: float32 [2, 1024], P(None, ('dp', 'seq'))
- new_m_in: float32 [1024, 3072], P(('dp', 'seq'))
- new_m_out: float32 [1024, 1024], P(('dp', 'seq'))
- new_m_conv: float32 [3, 1024], P(None, ('dp', 'seq'))
- new_m_gate: float32 [1024, 4608], P(('dp', 'seq'))
- new_m_up: float32 [1024, 4608], P(('dp', 'seq'))
- new_m_down: float32 [4608, 1024], P(('dp', 'seq'))
- new_m_gains: float32 [2, 1024], P(None, ('dp', 'seq'))
- new_v_in: float32 [1024, 3072], P(('dp', 'seq'))
- new_v_out: float32 [1024, 1024], P(('dp', 'seq'))
- new_v_conv: float32 [3, 1024], P(None, ('dp', 'seq'))
- new_v_gate: float32 [1024, 4608], P(('dp', 'seq'))
- new_v_up: float32 [1024, 4608], P(('dp', 'seq'))
- new_v_down: float32 [4608, 1024], P(('dp', 'seq'))
- new_v_gains: float32 [2, 1024], P(None, ('dp', 'seq'))
The draws below stay inside these ranges and needn't reach their ends.
Inputs may be any that keep to these rules, and one draw needn't show every extreme that they name: `segments`: within each sequence the numbers never fall. In each group of 2 sequences on one index of dp, one sequence has a single document covering positions 255 to 768.
All inputs are finite; a program needn't handle non-finite values.
Results may differ from the reference program's by a relative error of at most 0.012.
The reference program's roundings to bfloat16 on the way count: a program that leaves them out, or rounds other values in their place, can miss the bound.
Values may be sent and summed in bfloat16 or wider, within the bound.
No kernel may reach another device: no remote copies, remote signals or barrier semaphores. Data moves between devices by JAX's collectives and lax.ppermute only.
A program may use at most 192 MiB of HBM per device.

```python
import math
import jax
import jax.numpy as jnp
from jax import lax

D = 1024
FF = 4608
STRETCH = 256
SEQS = 2
STEP = 10
LEN = 1024
NSEQ = 16
TOKENS = 16384


def draw_segments(key, part):
    key = jax.random.fold_in(key, 7)
    keys = jax.random.split(key, 7)
    cuts = jax.random.randint(keys[0], (NSEQ, 4), 1, LEN)
    groups = NSEQ // SEQS
    picked = jax.random.randint(keys[1], (groups,), 0, SEQS)
    chosen = jnp.arange(NSEQ) % SEQS == jnp.repeat(picked, SEQS)
    early_cut = jax.random.randint(keys[2], (NSEQ, 4), 1, STRETCH)
    late_cut = jax.random.randint(keys[3], (NSEQ, 4), LEN - STRETCH + 1, LEN)
    side = jax.random.randint(keys[4], (NSEQ, 4), 0, 2)
    edge = jnp.where(side == 0, early_cut, late_cut)
    border_block = jax.random.randint(keys[5], (NSEQ, 2), 1, LEN // STRETCH)
    border_step = jax.random.randint(keys[6], (NSEQ, 2), 0, 2)
    border = STRETCH * border_block + border_step
    drawn = jnp.concatenate([border, cuts[:, 2:]], 1)
    cuts = jnp.where(chosen[:, None], edge, drawn)
    positions = jnp.arange(LEN)
    return jnp.sum((positions[None, :, None] >= cuts[:, None, :]).astype(jnp.int32), -1).astype(jnp.int32)


def levels(stream_key, shape, shards, low, top_value):
    level = 1.0
    for position, shards_of in shards:
        steps = jax.random.uniform(jax.random.fold_in(jax.random.fold_in(stream_key, 6), position), (shards_of,), jnp.float32, low / len(shards), top_value / len(shards))
        level = level * jnp.repeat(jnp.exp(steps), shape[position] // shards_of).reshape((-1,) + (1,) * (len(shape) - 1 - position))
    return level


def centred(key, extent, deviation, most, pieces=(), held_as=jnp.bfloat16):
    values = deviation * jax.random.normal(key, extent, jnp.float32)
    if pieces:
        values = values * levels(key, extent, pieces, -0.22, 0.18)
    return jnp.clip(values, -most, most).astype(held_as)


def setup_inputs(seed: int = 0) -> dict:
    key_list = jax.random.split(jax.random.key(seed), 25)
    return {
        "inputs": centred(key_list[0], (NSEQ, LEN, D), 1.0, 6.0, ((0, 8), (1, 4))),
        "cotangent": centred(key_list[1], (NSEQ, LEN, D), 1.0, 6.0, ((0, 8), (1, 4))),
        "segments": draw_segments(jax.random.fold_in(key_list[24], 71), 0),
        "w_in": centred(key_list[3], (D, 3 * D), D ** -0.5, 0.1875, ((0, 32),), jnp.float32),
        "w_out": centred(key_list[4], (D, D), D ** -0.5, 0.1875, ((0, 32),), jnp.float32),
        "conv_w": centred(key_list[5], (3, D), 3 ** -0.5, 3.5, ((1, 32),), jnp.float32),
        "w_gate": centred(key_list[6], (D, FF), D ** -0.5, 0.1875, ((0, 32),), jnp.float32),
        "w_up": centred(key_list[7], (D, FF), D ** -0.5, 0.1875, ((0, 32),), jnp.float32),
        "w_down": centred(key_list[8], (FF, D), FF ** -0.5, 0.09375, ((0, 32),), jnp.float32),
        "gains": jnp.clip(1.0 + 0.1 * jax.random.normal(key_list[9], (2, D), jnp.float32), 0.5, 1.5),
        "m_in": centred(key_list[10], (D, 3 * D), (0.11 * TOKENS ** 0.5), 80.0, ((0, 32),), jnp.float32),
        "m_out": centred(key_list[11], (D, D), (0.13 * TOKENS ** 0.5), 96.0, ((0, 32),), jnp.float32),
        "m_conv": centred(key_list[12], (3, D), (0.11 * TOKENS ** 0.5), 80.0, ((1, 32),), jnp.float32),
        "m_gate": centred(key_list[13], (D, FF), (0.033 * TOKENS ** 0.5), 24.0, ((0, 32),), jnp.float32),
        "m_up": centred(key_list[14], (D, FF), (0.033 * TOKENS ** 0.5), 24.0, ((0, 32),), jnp.float32),
        "m_down": centred(key_list[15], (FF, D), (0.066 * TOKENS ** 0.5), 48.0, ((0, 32),), jnp.float32),
        "m_gains": centred(key_list[16], (2, D), (0.11 * TOKENS ** 0.5), 80.0, ((1, 32),), jnp.float32),
        "v_in": jnp.clip(jnp.exp(math.log(3440.64) - 1.3768156 * jax.random.uniform(key_list[17], (D, 3 * D), jnp.float32) ** levels(key_list[17], (D, 3 * D), ((0, 32),), -0.2, 0.2)), 868.352, 3440.64),
        "v_out": jnp.clip(jnp.exp(math.log(4915.2) - 1.3730492 * jax.random.uniform(key_list[18], (D, D), jnp.float32) ** levels(key_list[18], (D, D), ((0, 32),), -0.2, 0.2)), 1245.184, 4915.2),
        "v_conv": jnp.clip(jnp.exp(math.log(3440.64) - 1.3768156 * jax.random.uniform(key_list[19], (3, D), jnp.float32) ** levels(key_list[19], (3, D), ((1, 32),), -0.2, 0.2)), 868.352, 3440.64),
        "v_gate": jnp.clip(jnp.exp(math.log(311.296) - 1.375823 * jax.random.uniform(key_list[20], (D, FF), jnp.float32) ** levels(key_list[20], (D, FF), ((0, 32),), -0.2, 0.2)), 78.6432, 311.296),
        "v_up": jnp.clip(jnp.exp(math.log(311.296) - 1.375823 * jax.random.uniform(key_list[21], (D, FF), jnp.float32) ** levels(key_list[21], (D, FF), ((0, 32),), -0.2, 0.2)), 78.6432, 311.296),
        "v_down": jnp.clip(jnp.exp(math.log(1245.184) - 1.3862944 * jax.random.uniform(key_list[22], (FF, D), jnp.float32) ** levels(key_list[22], (FF, D), ((0, 32),), -0.2, 0.2)), 311.296, 1245.184),
        "v_gains": jnp.clip(jnp.exp(math.log(3440.64) - 1.3768156 * jax.random.uniform(key_list[23], (2, D), jnp.float32) ** levels(key_list[23], (2, D), ((1, 32),), -0.2, 0.2)), 868.352, 3440.64),
    }


@jax.custom_vjp
def low(v):
    return lax.optimization_barrier(v.astype(jnp.bfloat16)).astype(jnp.float32)

@jax.custom_vjp
def low_back(v):
    return v

def low_keep(v):
    return (low(v), None)

def low_pass(kept, grad):
    return (grad,)

def back_keep(v):
    return (v, None)

def back_low(kept, grad):
    return (low(grad),)
low.defvjp(low_keep, low_pass)
low_back.defvjp(back_keep, back_low)
norm_eps = 1e-05
learn_rate = 0.02
small_rate = 1.0
beta_one = 0.9
beta_two = 0.95
adam_eps = 1e-08
weight_decay = 0.1

def matmul(left, right):
    return jnp.dot(left, right, precision=lax.Precision.HIGHEST, preferred_element_type=jnp.float32)

def rms_norm(values, gain):
    return values * lax.rsqrt(lax.optimization_barrier(jnp.mean(values * values, -1, keepdims=True)) + norm_eps) * gain

def convolve(conv_in, taps, doc_ids):
    padded = jnp.pad(conv_in, ((2, 0), (0, 0)))
    padded_ids = jnp.pad(doc_ids, (2, 0), constant_values=-1)
    near_one = (padded_ids[1:-1] == doc_ids).astype(jnp.float32)[:, None]
    near_two = (padded_ids[:-2] == doc_ids).astype(jnp.float32)[:, None]
    return taps[2] * conv_in + taps[1] * padded[1:-1] * near_one + taps[0] * padded[:-2] * near_two

def forward(params, rows, doc_ids):
    w_in, w_out, conv_w, w_gate, w_up, w_down, gains = [low(item) for item in params]
    width = rows.shape[1]
    norm_one = low(rms_norm(rows, gains[0]))
    projected = low_back(matmul(norm_one, w_in))
    b_gate = projected[:, :width]
    c_gate = projected[:, width:2 * width]
    x_part = projected[:, 2 * width:]
    conv_in = low(b_gate * x_part)
    conv_out = convolve(conv_in, conv_w, doc_ids)
    mixed_in = low(c_gate * conv_out)
    branch = low_back(matmul(mixed_in, w_out))
    middle = rows + branch
    norm_two = low(rms_norm(middle, gains[1]))
    gate = low_back(matmul(norm_two, w_gate))
    up_part = low_back(matmul(norm_two, w_up))
    hidden = low(jax.nn.silu(gate) * up_part)
    return middle + low_back(matmul(hidden, w_down))

def adamw(master, first, second, grad, rate, decay):
    first_new = beta_one * first + (1.0 - beta_one) * grad
    second_new = beta_two * second + (1.0 - beta_two) * grad * grad
    first_hat = first_new / (1.0 - beta_one ** STEP)
    second_hat = second_new / (1.0 - beta_two ** STEP)
    master_new = master - rate * (first_hat / (jnp.sqrt(second_hat) + adam_eps) + decay * master)
    return (master_new, first_new, second_new)

def reference(inputs, cotangent, segments, w_in, w_out, conv_w, w_gate, w_up, w_down, gains, m_in, m_out, m_conv, m_gate, m_up, m_down, m_gains, v_in, v_out, v_conv, v_gate, v_up, v_down, v_gains):
    params = (w_in, w_out, conv_w, w_gate, w_up, w_down, gains)

    def one_sequence(totals, item):
        rows, cot_rows, doc_ids = item
        result, pull = jax.vjp(lambda weights, values: forward(weights, values, doc_ids), params, rows.astype(jnp.float32))
        grad_weights, grad_rows = pull(cot_rows.astype(jnp.float32))
        totals = jax.tree.map(lambda left, right: left + right, totals, grad_weights)
        return (totals, (result.astype(jnp.bfloat16), grad_rows))
    zeros = jax.tree.map(jnp.zeros_like, params)
    totals, (outputs, grad_inputs) = lax.scan(one_sequence, zeros, (inputs, cotangent, segments))
    firsts = (m_in, m_out, m_conv, m_gate, m_up, m_down, m_gains)
    seconds = (v_in, v_out, v_conv, v_gate, v_up, v_down, v_gains)
    rates = (learn_rate, learn_rate, small_rate, learn_rate, learn_rate, learn_rate, small_rate)
    decays = (weight_decay, weight_decay, 0.0, weight_decay, weight_decay, weight_decay, 0.0)
    updated = [adamw(params[index], firsts[index], seconds[index], totals[index], rates[index], decays[index]) for index in range(7)]
    new_w = [item[0] for item in updated]
    new_m = [item[1] for item in updated]
    new_v = [item[2] for item in updated]
    return (outputs, grad_inputs, new_w[0], new_w[1], new_w[2], new_w[3], new_w[4], new_w[5], new_w[6], new_m[0], new_m[1], new_m[2], new_m[3], new_m[4], new_m[5], new_m[6], new_v[0], new_v[1], new_v[2], new_v[3], new_v[4], new_v[5], new_v[6])
```

```python
import jax
import jax.numpy as jnp
from jax import lax
from jax.sharding import PartitionSpec as P

STEP = 10


norm_eps = 1e-05
learn_rate = 0.02
small_rate = 1.0
beta_one = 0.9
beta_two = 0.95
adam_eps = 1e-08
weight_decay = 0.1
LANES = 128
bf16 = jnp.bfloat16
f32 = jnp.float32


def from_behind(shard, axis, by):
    peers = lax.axis_size(axis)
    pairs = [(i, i + by) for i in range(peers) if 0 <= i + by < peers]
    return lax.ppermute(shard, axis, pairs)


def to_sibling(block):
    return lax.ppermute(block, "dp", [(i, i ^ 1) for i in range(lax.axis_size("dp"))])


def along_z(block, by):
    count = lax.axis_size("dp")
    return lax.ppermute(block, "dp", [(i, (i + 2 * by) % count) for i in range(count)])


def across_seq(block, by):
    return lax.ppermute(block, "seq", [(i, i ^ by) for i in range(lax.axis_size("seq"))])


def dot(first, second):
    return jnp.dot(first, second, preferred_element_type=f32)


def left_contract(first, second):
    return lax.dot_general(first, second, (((0,), (0,)), ((), ())), preferred_element_type=f32)


def right_contract(first, second):
    return lax.dot_general(first, second, (((1,), (1,)), ((), ())), preferred_element_type=f32)


def pick(stacked, index):
    return lax.dynamic_index_in_dim(stacked, index, 0, keepdims=False)


def normed(values, gain):
    scale = lax.rsqrt(jnp.mean(values * values, -1, keepdims=True) + norm_eps)
    unit = values * scale
    return (unit, scale, (unit * gain).astype(bf16))


def norm_back(grad_out, unit, scale, gain):
    grad_gain = jnp.sum(grad_out * unit, 0)
    grad_unit = grad_out * gain
    grad_in = scale * (grad_unit - unit * jnp.mean(grad_unit * unit, -1, keepdims=True))
    return (grad_in, grad_gain)


def adamw(master, first, second, grad, rate, decay):
    first_new = beta_one * first + (1.0 - beta_one) * grad
    second_new = beta_two * second + (1.0 - beta_two) * grad * grad
    first_hat = first_new / (1.0 - beta_one**STEP)
    second_hat = second_new / (1.0 - beta_two**STEP)
    master_new = master - rate * (first_hat / (jnp.sqrt(second_hat) + adam_eps) + decay * master)
    return (master_new, first_new, second_new)


def local(
    inputs,
    cotangent,
    segments,
    w_in,
    w_out,
    conv_w,
    w_gate,
    w_up,
    w_down,
    gains,
    m_in,
    m_out,
    m_conv,
    m_gate,
    m_up,
    m_down,
    m_gains,
    v_in,
    v_out,
    v_conv,
    v_gate,
    v_up,
    v_down,
    v_gains,
):
    seqs_here, stretch, width = inputs.shape
    rows = seqs_here * stretch
    n_dp = lax.axis_size("dp")
    n_seq = lax.axis_size("seq")
    n_z = n_dp // 2
    own = w_in.shape[0]
    own_ff = w_down.shape[0]
    ff_part = n_dp * own_ff
    dp = lax.axis_index("dp")
    sq = lax.axis_index("seq")
    z = dp // 2
    core = dp % 2
    first_core = core == 0

    def halves(full):
        split = full.reshape(rows, n_z, 2, n_seq * own)
        even, odd = split[:, :, 0], split[:, :, 1]
        mine = jnp.where(first_core, even, odd).reshape(rows, width // 2)
        other = jnp.where(first_core, odd, even).reshape(rows, width // 2)
        return mine, other

    def joined(mine, other):
        shape = (rows, n_z, 1, n_seq * own)
        mine, other = mine.reshape(shape), other.reshape(shape)
        return jnp.concatenate(
            [jnp.where(first_core, mine, other), jnp.where(first_core, other, mine)], 2
        ).reshape(rows, width)

    def seq_ordered(pieces):
        stacked = jnp.stack(pieces, 0)
        return jnp.stack([pick(stacked, sq ^ j) for j in range(n_seq)], 0)

    def by_part(weight):
        low = weight.astype(bf16).reshape(own, n_dp, n_seq, own_ff)
        return low.transpose(2, 0, 1, 3).reshape(n_seq, own, ff_part)

    smalls = jnp.pad(
        jnp.concatenate([conv_w, gains], 0).astype(bf16), ((0, own - 5), (0, LANES - own))
    )
    mix = jnp.concatenate([w_in.astype(bf16), w_out.astype(bf16), smalls], 1)
    z_blocks = jnp.stack([mix] + [along_z(mix, -k) for k in range(1, n_z)], 0)
    z_twice = jnp.concatenate([z_blocks, z_blocks], 0)
    z_order = lax.dynamic_slice_in_dim(z_twice, (n_z - z) % n_z, n_z, 0)
    mix_mine = lax.all_gather(z_order, "seq", axis=1).reshape(width // 2, -1)
    mix_other = to_sibling(mix_mine)

    gate_up = jnp.concatenate([by_part(w_gate), by_part(w_up)], 2)
    gate_up = seq_ordered(
        [pick(gate_up, sq)] + [across_seq(pick(gate_up, sq ^ k), k) for k in range(1, n_seq)]
    )
    mat_gate_up = lax.all_gather(gate_up, "dp", axis=0).reshape(width, 2 * ff_part)
    mat_down = lax.all_gather(w_down.astype(bf16), "dp", axis=0, tiled=True)

    grad_top = cotangent.reshape(rows, width)
    tops = [grad_top] + [across_seq(grad_top, k) for k in range(1, n_seq)]

    cut_in, cut_out = 3 * width, 4 * width
    in_mine, in_other = mix_mine[:, :cut_in], mix_other[:, :cut_in]
    out_mine, out_other = mix_mine[:, cut_in:cut_out], mix_other[:, cut_in:cut_out]
    small_mine = mix_mine[:, cut_out:].reshape(n_z, n_seq, own, LANES)[:, :, :5, :own]
    small_other = mix_other[:, cut_out:].reshape(n_z, n_seq, own, LANES)[:, :, :5, :own]
    small_all = jnp.stack(
        [
            jnp.where(first_core, small_mine, small_other),
            jnp.where(first_core, small_other, small_mine),
        ],
        1,
    )
    small_all = small_all.transpose(3, 0, 1, 2, 4).reshape(5, width).astype(f32)
    taps, gain_vals = small_all[:3], small_all[3:]

    residual = inputs.reshape(rows, width).astype(f32)
    unit_one, scale_one, norm_one = normed(residual, gain_vals[0])
    norm_mine, norm_other = halves(norm_one)
    projected = dot(norm_mine, in_mine) + dot(norm_other, in_other)
    b_gate = projected[:, :width]
    c_gate = projected[:, width : 2 * width]
    x_part = projected[:, 2 * width :]
    conv_in = (b_gate * x_part).astype(bf16).reshape(seqs_here, stretch, width)
    prev_rows, prev_ids = from_behind(
        (conv_in[:, -2:, :], segments[:, -2:].astype(bf16)), "seq", 1
    )
    extended = jnp.concatenate([prev_rows, conv_in], 1).astype(f32)
    ext_ids = jnp.concatenate([prev_ids.astype(jnp.int32), segments], 1)
    near_one = (ext_ids[:, 1:-1] == segments).astype(f32)[..., None]
    near_two = (ext_ids[:, :-2] == segments).astype(f32)[..., None]
    tap_now = extended[:, 2:]
    tap_one = extended[:, 1:-1] * near_one
    tap_two = extended[:, :-2] * near_two
    conv_out = (taps[2] * tap_now + taps[1] * tap_one + taps[0] * tap_two).reshape(rows, width)
    mixed_in = (c_gate * conv_out).astype(bf16)
    mixed_mine, mixed_other = halves(mixed_in)
    middle = residual + dot(mixed_mine, out_mine) + dot(mixed_other, out_other)
    unit_two, scale_two, norm_two = normed(middle, gain_vals[1])

    norms = [norm_two] + [across_seq(norm_two, k) for k in range(1, n_seq)]
    hiddens, act_grads, norm_parts, out_parts = [], [], [], []
    for block, top in zip(norms, tops):
        both = dot(block, mat_gate_up)
        gate, up_part = both[:, :ff_part], both[:, ff_part:]
        sigma = jax.nn.sigmoid(gate)
        silu_vals = gate * sigma
        grad_hidden = right_contract(top, mat_down)
        hiddens.append((silu_vals * up_part).astype(bf16))
        grad_gate_act = (grad_hidden * up_part * sigma * (1.0 + gate * (1.0 - sigma))).astype(bf16)
        grad_up_act = (grad_hidden * silu_vals).astype(bf16)
        act_grads.append(jnp.concatenate([grad_gate_act, grad_up_act], 1))
        norm_parts.append(right_contract(act_grads[-1], mat_gate_up))
        out_parts.append(dot(hiddens[-1], mat_down))
    grad_norm_two = norm_parts[0]
    for k in range(1, n_seq):
        grad_norm_two = grad_norm_two + across_seq(norm_parts[k].astype(bf16), k).astype(f32)
    output = middle + out_parts[0]
    for k in range(1, n_seq):
        output = output + across_seq(out_parts[k].astype(bf16), k).astype(f32)
    output = output.astype(bf16)
    hidden_all = jnp.concatenate(hiddens, 0)
    top_all = jnp.concatenate(tops, 0)
    norm_all = jnp.concatenate(norms, 0)
    act_all = jnp.concatenate(act_grads, 0)
    grad_down = left_contract(hidden_all, top_all)
    grad_gate_up = left_contract(norm_all, act_all)

    back_two, gain_two = norm_back(grad_norm_two, unit_two, scale_two, gain_vals[1])
    grad_middle = grad_top.astype(f32) + back_two
    grad_branch = grad_middle.astype(bf16)
    grad_out_mine = left_contract(mixed_mine, grad_branch)
    grad_out_other = left_contract(mixed_other, grad_branch)
    grad_mixed = joined(
        right_contract(grad_branch, out_mine), right_contract(grad_branch, out_other)
    )
    grad_c = grad_mixed * conv_out
    grad_conv = (grad_mixed * c_gate).reshape(seqs_here, stretch, width)
    grad_taps = [
        jnp.sum(tap_two * grad_conv, (0, 1)),
        jnp.sum(tap_one * grad_conv, (0, 1)),
        jnp.sum(tap_now * grad_conv, (0, 1)),
    ]
    term_now = taps[2] * grad_conv
    term_one = taps[1] * grad_conv * near_one
    term_two = taps[0] * grad_conv * near_two
    grad_ext = (
        jnp.pad(term_now, ((0, 0), (2, 0), (0, 0)))
        + jnp.pad(term_one, ((0, 0), (1, 1), (0, 0)))
        + jnp.pad(term_two, ((0, 0), (0, 2), (0, 0)))
    )
    next_terms = from_behind(grad_ext[:, :2, :], "seq", -1)
    grad_conv_in = (
        grad_ext[:, 2:, :] + jnp.pad(next_terms, ((0, 0), (stretch - 2, 0), (0, 0)))
    ).reshape(rows, width)
    grad_proj = jnp.concatenate([grad_conv_in * x_part, grad_c, grad_conv_in * b_gate], -1).astype(
        bf16
    )
    grad_in_mine = left_contract(norm_mine, grad_proj)
    grad_in_other = left_contract(norm_other, grad_proj)
    grad_norm_one = joined(right_contract(grad_proj, in_mine), right_contract(grad_proj, in_other))
    back_one, gain_one = norm_back(grad_norm_one, unit_one, scale_one, gain_vals[0])
    input_grad = (grad_middle + back_one).reshape(seqs_here, stretch, width)

    def sum_core(mine, other):
        return mine + to_sibling(other.astype(bf16)).astype(f32)

    def sum_z(blocks):
        low = blocks.astype(bf16)
        total = pick(blocks, z)
        for k in range(1, n_z):
            total = total + along_z(pick(low, (z + k) % n_z), k).astype(f32)
        return total

    def sum_seq_z(mine):
        blocks = mine.reshape(n_z, n_seq, own, -1)
        low = blocks.astype(bf16)
        total = lax.dynamic_index_in_dim(blocks, sq, 1, keepdims=False)
        for k in range(1, n_seq):
            part = lax.dynamic_index_in_dim(low, sq ^ k, 1, keepdims=False)
            total = total + across_seq(part, k).astype(f32)
        return sum_z(total)

    small_grads = jnp.stack(grad_taps + [gain_one, gain_two], 0)
    small_grads = small_grads.reshape(5, n_z, 2, n_seq, own).transpose(2, 1, 3, 0, 4)
    small_grads = jnp.pad(
        small_grads, ((0, 0), (0, 0), (0, 0), (0, own - 5), (0, LANES - own))
    ).reshape(2, width // 2, LANES)
    small_sum = sum_seq_z(sum_core(pick(small_grads, core), pick(small_grads, 1 - core)))
    sum_out = sum_seq_z(sum_core(grad_out_mine, grad_out_other))
    sum_in = sum_seq_z(sum_core(grad_in_mine, grad_in_other))

    gu_blocks = grad_gate_up.reshape(n_z, 2, n_seq * own, 2 * ff_part)
    gu_mine = jnp.where(first_core, gu_blocks[:, 0], gu_blocks[:, 1])
    gu_other = jnp.where(first_core, gu_blocks[:, 1], gu_blocks[:, 0])
    gu_sum = sum_z(sum_core(gu_mine, gu_other)).astype(bf16).reshape(n_seq, own, 2 * ff_part)
    gu_sum = seq_ordered(
        [pick(gu_sum, sq)] + [across_seq(pick(gu_sum, sq ^ k), k) for k in range(1, n_seq)]
    ).astype(f32)

    def by_row(part):
        return (
            part.reshape(n_seq, own, n_dp, own_ff)
            .transpose(1, 2, 0, 3)
            .reshape(own, n_seq * ff_part)
        )

    sum_gate = by_row(gu_sum[:, :, :ff_part])
    sum_up = by_row(gu_sum[:, :, ff_part:])
    sum_down = lax.psum_scatter(grad_down, "dp", scatter_dimension=0, tiled=True)

    reduced = (
        sum_in,
        sum_out,
        small_sum[:3, :own],
        sum_gate,
        sum_up,
        sum_down,
        small_sum[3:5, :own],
    )
    masters = (w_in, w_out, conv_w, w_gate, w_up, w_down, gains)
    firsts = (m_in, m_out, m_conv, m_gate, m_up, m_down, m_gains)
    seconds = (v_in, v_out, v_conv, v_gate, v_up, v_down, v_gains)
    rates = (learn_rate, learn_rate, small_rate, learn_rate, learn_rate, learn_rate, small_rate)
    decays = (weight_decay, weight_decay, 0.0, weight_decay, weight_decay, weight_decay, 0.0)
    updated = [
        adamw(
            masters[index],
            firsts[index],
            seconds[index],
            reduced[index],
            rates[index],
            decays[index],
        )
        for index in range(7)
    ]
    new_w = [item[0] for item in updated]
    new_m = [item[1] for item in updated]
    new_v = [item[2] for item in updated]
    return (
        output.reshape(seqs_here, stretch, width),
        input_grad,
        *new_w,
        *new_m,
        *new_v,
    )


def solution(mesh):
    tokens = P("dp", "seq", None)
    matrix = P(("dp", "seq"), None)
    vector = P(None, ("dp", "seq"))
    weights = (matrix, matrix, vector, matrix, matrix, matrix, vector)
    return jax.shard_map(
        local,
        mesh=mesh,
        in_specs=(tokens, tokens, P("dp", "seq")) + weights * 3,
        out_specs=(tokens, tokens) + weights * 3,
        check_vma=False,
    )
```

```python
import jax
import jax.numpy as jnp
from jax import lax
from jax.sharding import PartitionSpec as P

STEP = 10


norm_eps = 1e-05
learn_rate = 0.02
small_rate = 1.0
beta_one = 0.9
beta_two = 0.95
adam_eps = 1e-08
weight_decay = 0.1
LANES = 128
bf16 = jnp.bfloat16
f32 = jnp.float32


def from_behind(shard, axis, by):
    peers = lax.axis_size(axis)
    pairs = [(i, i + by) for i in range(peers) if 0 <= i + by < peers]
    return lax.ppermute(shard, axis, pairs)


def to_sibling(block):
    return lax.ppermute(block, "dp", [(i, i ^ 1) for i in range(lax.axis_size("dp"))])


def along_z(block, by):
    count = lax.axis_size("dp")
    return lax.ppermute(block, "dp", [(i, (i + 2 * by) % count) for i in range(count)])


def across_seq(block, by):
    return lax.ppermute(block, "seq", [(i, i ^ by) for i in range(lax.axis_size("seq"))])


def dot(first, second):
    return jnp.dot(first, second, preferred_element_type=f32)


def left_contract(first, second):
    return lax.dot_general(first, second, (((0,), (0,)), ((), ())), preferred_element_type=f32)


def right_contract(first, second):
    return lax.dot_general(first, second, (((1,), (1,)), ((), ())), preferred_element_type=f32)


def tie(values):
    return lax.optimization_barrier(values)


def pick(stacked, index):
    return lax.dynamic_index_in_dim(stacked, index, 0, keepdims=False)


def normed(values, gain):
    scale = lax.rsqrt(jnp.mean(values * values, -1, keepdims=True) + norm_eps)
    unit = values * scale
    return (unit, scale, (unit * gain).astype(bf16))


def norm_back(grad_out, unit, scale, gain):
    grad_gain = jnp.sum(grad_out * unit, 0)
    grad_unit = grad_out * gain
    grad_in = scale * (grad_unit - unit * jnp.mean(grad_unit * unit, -1, keepdims=True))
    return (grad_in, grad_gain)


def adamw(master, first, second, grad, rate, decay):
    first_new = beta_one * first + (1.0 - beta_one) * grad
    second_new = beta_two * second + (1.0 - beta_two) * grad * grad
    first_hat = first_new / (1.0 - beta_one**STEP)
    second_hat = second_new / (1.0 - beta_two**STEP)
    master_new = master - rate * (first_hat / (jnp.sqrt(second_hat) + adam_eps) + decay * master)
    return (master_new, first_new, second_new)


def local(
    inputs,
    cotangent,
    segments,
    w_in,
    w_out,
    conv_w,
    w_gate,
    w_up,
    w_down,
    gains,
    m_in,
    m_out,
    m_conv,
    m_gate,
    m_up,
    m_down,
    m_gains,
    v_in,
    v_out,
    v_conv,
    v_gate,
    v_up,
    v_down,
    v_gains,
):
    seqs_here, stretch, width = inputs.shape
    rows = seqs_here * stretch
    n_dp = lax.axis_size("dp")
    n_seq = lax.axis_size("seq")
    n_z = n_dp // 2
    own = w_in.shape[0]
    own_ff = w_down.shape[0]
    ff_part = n_dp * own_ff
    dp = lax.axis_index("dp")
    sq = lax.axis_index("seq")
    z = dp // 2
    core = dp % 2
    first_core = core == 0

    lane = n_seq * own

    def halves(full):
        blocks = [full[:, i * lane : (i + 1) * lane] for i in range(2 * n_z)]
        even = jnp.concatenate(blocks[0::2], 1)
        odd = jnp.concatenate(blocks[1::2], 1)
        return jnp.where(first_core, even, odd), jnp.where(first_core, odd, even)

    def joined(mine, other):
        even = jnp.where(first_core, mine, other)
        odd = jnp.where(first_core, other, mine)
        blocks = []
        for i in range(n_z):
            blocks += [even[:, i * lane : (i + 1) * lane], odd[:, i * lane : (i + 1) * lane]]
        return jnp.concatenate(blocks, 1)

    def seq_ordered(pieces):
        stacked = jnp.stack(pieces, 0)
        return jnp.stack([pick(stacked, sq ^ j) for j in range(n_seq)], 0)

    def by_part(weight):
        low = weight.astype(bf16).reshape(own, n_dp, n_seq, own_ff)
        return low.transpose(2, 0, 1, 3).reshape(n_seq, own, ff_part)

    smalls = jnp.pad(
        jnp.concatenate([conv_w, gains], 0).astype(bf16), ((0, own - 5), (0, LANES - own))
    )
    mix = jnp.concatenate([w_in.astype(bf16), w_out.astype(bf16), smalls], 1)
    gate_up = jnp.concatenate([by_part(w_gate), by_part(w_up)], 2)

    z_parts = [along_z(mix, -k) for k in range(1, n_z)]
    gu_parts = [across_seq(pick(gate_up, sq ^ k), k) for k in range(1, n_seq)]
    grad_top = cotangent.reshape(rows, width)
    gu_parts, top_out = tie((gu_parts, grad_top))
    last = n_seq - 1
    top_last = across_seq(top_out, last)
    z_parts, gu_parts, top_last = tie((z_parts, gu_parts, top_last))
    gate_up = seq_ordered([pick(gate_up, sq)] + gu_parts)
    mat_gate_up = lax.all_gather(gate_up, "dp", axis=0).reshape(width, 2 * ff_part)

    z_twice = jnp.stack(([mix] + z_parts) * 2, 0)
    z_order = lax.dynamic_slice_in_dim(z_twice, (n_z - z) % n_z, n_z, 0)
    mix_parts = {k: across_seq(z_order, k) for k in range(n_seq - 1, 0, -1)}
    mix_parts, top_out, low_down = tie((mix_parts, top_out, w_down.astype(bf16)))
    mix_parts[0] = z_order
    mix_mine = seq_ordered([mix_parts[k] for k in range(n_seq)])
    mix_mine = mix_mine.transpose(1, 0, 2, 3).reshape(width // 2, -1)

    mix_other = to_sibling(mix_mine)
    mat_down = lax.all_gather(low_down, "dp", axis=0, tiled=True)
    tops = {k: across_seq(top_out, k) for k in range(1, last)}
    tops[0], tops[last] = grad_top, top_last

    cut_in, cut_out = 3 * width, 4 * width
    in_mine, in_other = mix_mine[:, :cut_in], mix_other[:, :cut_in]
    out_mine, out_other = mix_mine[:, cut_in:cut_out], mix_other[:, cut_in:cut_out]
    small_mine = mix_mine[:, cut_out:].reshape(n_z, n_seq, own, LANES)[:, :, :5, :own]
    small_other = mix_other[:, cut_out:].reshape(n_z, n_seq, own, LANES)[:, :, :5, :own]
    small_all = jnp.stack(
        [
            jnp.where(first_core, small_mine, small_other),
            jnp.where(first_core, small_other, small_mine),
        ],
        1,
    )
    small_all = small_all.transpose(3, 0, 1, 2, 4).reshape(5, width).astype(f32)
    taps, gain_vals = small_all[:3], small_all[3:]

    residual = inputs.reshape(rows, width).astype(f32)
    unit_one, scale_one, norm_one = normed(residual, gain_vals[0])
    norm_mine, norm_other = halves(norm_one)
    projected = dot(norm_mine, in_mine) + dot(norm_other, in_other)
    b_gate = projected[:, :width]
    c_gate = projected[:, width : 2 * width]
    x_part = projected[:, 2 * width :]
    conv_in = (b_gate * x_part).astype(bf16).reshape(seqs_here, stretch, width)
    edge_ids = jnp.pad(segments[:, -2:, None].astype(bf16), ((0, 0), (0, 0), (0, LANES - 1)))
    edge = from_behind(jnp.concatenate([conv_in[:, -2:, :], edge_ids], 2), "seq", 1)
    prev_rows, prev_ids = edge[:, :, :width], edge[:, :, width]
    extended = jnp.concatenate([prev_rows, conv_in], 1).astype(f32)
    ext_ids = jnp.concatenate([prev_ids.astype(jnp.int32), segments], 1)
    near_one = (ext_ids[:, 1:-1] == segments).astype(f32)[..., None]
    near_two = (ext_ids[:, :-2] == segments).astype(f32)[..., None]
    tap_now = extended[:, 2:]
    tap_one = extended[:, 1:-1] * near_one
    tap_two = extended[:, :-2] * near_two
    conv_out = (taps[2] * tap_now + taps[1] * tap_one + taps[0] * tap_two).reshape(rows, width)
    mixed_in = (c_gate * conv_out).astype(bf16)
    mixed_mine, mixed_other = halves(mixed_in)
    middle = residual + dot(mixed_mine, out_mine) + dot(mixed_other, out_other)
    unit_two, scale_two, norm_two = normed(middle, gain_vals[1])

    norms = {k: across_seq(norm_two, k) for k in range(last, 0, -1)}
    norms[0] = norm_two
    order = [0] + list(range(last, 0, -1))
    hiddens, act_grads, norm_parts = {}, {}, {}
    for k in order:
        both = dot(norms[k], mat_gate_up)
        gate, up_part = both[:, :ff_part], both[:, ff_part:]
        sigma = jax.nn.sigmoid(gate)
        silu_vals = gate * sigma
        grad_hidden = right_contract(tops[k], mat_down)
        hiddens[k] = (silu_vals * up_part).astype(bf16)
        grad_gate_act = (grad_hidden * up_part * sigma * (1.0 + gate * (1.0 - sigma))).astype(bf16)
        grad_up_act = (grad_hidden * silu_vals).astype(bf16)
        act_grads[k] = jnp.concatenate([grad_gate_act, grad_up_act], 1)
        norm_parts[k] = right_contract(act_grads[k], mat_gate_up)
    norm_sums = {k: across_seq(norm_parts[k].astype(bf16), k) for k in order[1:]}

    def rows_of(blocks):
        return jnp.concatenate([blocks[k] for k in order], 0)

    grad_down = left_contract(rows_of(hiddens), rows_of(tops)).astype(bf16)
    grad_gate_up = left_contract(rows_of(norms), rows_of(act_grads)).astype(bf16)
    sum_down = lax.psum_scatter(grad_down, "dp", scatter_dimension=0, tiled=True).astype(f32)
    gu_sum = lax.psum_scatter(grad_gate_up, "dp", scatter_dimension=0, tiled=True)
    out_parts = {k: dot(hiddens[k], mat_down) for k in order}
    norm_sums, out_low = tie((norm_sums, {k: out_parts[k].astype(bf16) for k in order[1:]}))
    grad_norm_two = norm_parts[0]
    output = middle + out_parts[0]
    for k in order[1:]:
        grad_norm_two = grad_norm_two + norm_sums[k].astype(f32)
        output = output + across_seq(out_low[k], k).astype(f32)
    output = output.astype(bf16)

    back_two, gain_two = norm_back(grad_norm_two, unit_two, scale_two, gain_vals[1])
    grad_middle = grad_top.astype(f32) + back_two
    grad_branch = grad_middle.astype(bf16)
    grad_out_mine = left_contract(mixed_mine, grad_branch)
    grad_out_other = left_contract(mixed_other, grad_branch)
    grad_mixed = joined(
        right_contract(grad_branch, out_mine), right_contract(grad_branch, out_other)
    )
    grad_c = grad_mixed * conv_out
    grad_conv = (grad_mixed * c_gate).reshape(seqs_here, stretch, width)
    grad_taps = [
        jnp.sum(tap_two * grad_conv, (0, 1)),
        jnp.sum(tap_one * grad_conv, (0, 1)),
        jnp.sum(tap_now * grad_conv, (0, 1)),
    ]
    term_now = taps[2] * grad_conv
    term_one = taps[1] * grad_conv * near_one
    term_two = taps[0] * grad_conv * near_two
    grad_ext = (
        jnp.pad(term_now, ((0, 0), (2, 0), (0, 0)))
        + jnp.pad(term_one, ((0, 0), (1, 1), (0, 0)))
        + jnp.pad(term_two, ((0, 0), (0, 2), (0, 0)))
    )
    next_terms = from_behind(grad_ext[:, :2, :], "seq", -1)
    grad_conv_in = (
        grad_ext[:, 2:, :] + jnp.pad(next_terms, ((0, 0), (stretch - 2, 0), (0, 0)))
    ).reshape(rows, width)
    grad_proj = jnp.concatenate([grad_conv_in * x_part, grad_c, grad_conv_in * b_gate], -1).astype(
        bf16
    )
    grad_in_mine = left_contract(norm_mine, grad_proj)
    grad_in_other = left_contract(norm_other, grad_proj)
    grad_norm_one = joined(right_contract(grad_proj, in_mine), right_contract(grad_proj, in_other))
    back_one, gain_one = norm_back(grad_norm_one, unit_one, scale_one, gain_vals[0])
    input_grad = (grad_middle + back_one).reshape(seqs_here, stretch, width)

    def sum_core(mine, other):
        return mine + to_sibling(other.astype(bf16)).astype(f32)

    small_grads = jnp.stack(grad_taps + [gain_one, gain_two], 0)
    small_grads = small_grads.reshape(5, n_z, 2, n_seq, own).transpose(2, 1, 3, 0, 4)
    small_grads = jnp.pad(
        small_grads, ((0, 0), (0, 0), (0, 0), (0, own - 5), (0, LANES - own))
    ).reshape(2, width // 2, LANES)
    mixed = jnp.concatenate(
        [
            sum_core(grad_in_mine, grad_in_other),
            sum_core(grad_out_mine, grad_out_other),
            sum_core(pick(small_grads, core), pick(small_grads, 1 - core)),
        ],
        1,
    ).astype(bf16)
    mixed = mixed.reshape(n_z, n_seq, own, -1)

    def seq_block(index):
        return lax.dynamic_index_in_dim(mixed, index, 1, keepdims=False)

    seq_parts = [across_seq(seq_block(sq ^ k), k) for k in range(n_seq - 1, 0, -1)]
    total = seq_block(sq).astype(f32)
    for part in seq_parts:
        total = total + part.astype(f32)
    low = total.astype(bf16)
    z_sums = [along_z(pick(low, (z + k) % n_z), k) for k in range(1, n_z)]
    total = pick(total, z)
    for part in z_sums:
        total = total + part.astype(f32)
    sum_in, sum_out, small_sum = total[:, :cut_in], total[:, cut_in:cut_out], total[:, cut_out:]

    gu_sum = gu_sum.reshape(n_seq, own, 2 * ff_part)
    gu_sum = seq_ordered(
        [pick(gu_sum, sq)] + [across_seq(pick(gu_sum, sq ^ k), k) for k in range(1, n_seq)]
    ).astype(f32)

    def by_row(part):
        return (
            part.reshape(n_seq, own, n_dp, own_ff)
            .transpose(1, 2, 0, 3)
            .reshape(own, n_seq * ff_part)
        )

    sum_gate = by_row(gu_sum[:, :, :ff_part])
    sum_up = by_row(gu_sum[:, :, ff_part:])

    reduced = (
        sum_in,
        sum_out,
        small_sum[:3, :own],
        sum_gate,
        sum_up,
        sum_down,
        small_sum[3:5, :own],
    )
    masters = (w_in, w_out, conv_w, w_gate, w_up, w_down, gains)
    firsts = (m_in, m_out, m_conv, m_gate, m_up, m_down, m_gains)
    seconds = (v_in, v_out, v_conv, v_gate, v_up, v_down, v_gains)
    rates = (learn_rate, learn_rate, small_rate, learn_rate, learn_rate, learn_rate, small_rate)
    decays = (weight_decay, weight_decay, 0.0, weight_decay, weight_decay, weight_decay, 0.0)
    updated = [
        adamw(
            masters[index],
            firsts[index],
            seconds[index],
            reduced[index],
            rates[index],
            decays[index],
        )
        for index in range(7)
    ]
    new_w = [item[0] for item in updated]
    new_m = [item[1] for item in updated]
    new_v = [item[2] for item in updated]
    return (
        output.reshape(seqs_here, stretch, width),
        input_grad,
        *new_w,
        *new_m,
        *new_v,
    )


def solution(mesh):
    tokens = P("dp", "seq", None)
    matrix = P(("dp", "seq"), None)
    vector = P(None, ("dp", "seq"))
    weights = (matrix, matrix, vector, matrix, matrix, matrix, vector)
    return jax.shard_map(
        local,
        mesh=mesh,
        in_specs=(tokens, tokens, P("dp", "seq")) + weights * 3,
        out_specs=(tokens, tokens) + weights * 3,
        check_vma=False,
    )
```

```python
import jax
import jax.numpy as jnp
from jax import lax
from jax.experimental import pallas as pl
from jax.experimental.pallas import tpu as pltpu
from jax.sharding import PartitionSpec as P

STEP = 10


norm_eps = 1e-05
learn_rate = 0.02
small_rate = 1.0
beta_one = 0.9
beta_two = 0.95
adam_eps = 1e-08
weight_decay = 0.1
LANES = 128
bf16 = jnp.bfloat16
f32 = jnp.float32


def from_behind(shard, axis, by):
    peers = lax.axis_size(axis)
    pairs = [(i, i + by) for i in range(peers) if 0 <= i + by < peers]
    return lax.ppermute(shard, axis, pairs)


def to_sibling(block):
    return lax.ppermute(block, "dp", [(i, i ^ 1) for i in range(lax.axis_size("dp"))])


def along_z(block, by):
    count = lax.axis_size("dp")
    return lax.ppermute(block, "dp", [(i, (i + 2 * by) % count) for i in range(count)])


def across_seq(block, by):
    return lax.ppermute(block, "seq", [(i, i ^ by) for i in range(lax.axis_size("seq"))])


def dot(first, second):
    return jnp.dot(first, second, preferred_element_type=f32)


def left_contract(first, second):
    return lax.dot_general(first, second, (((0,), (0,)), ((), ())), preferred_element_type=f32)


def right_contract(first, second):
    return lax.dot_general(first, second, (((1,), (1,)), ((), ())), preferred_element_type=f32)


def tie(values):
    return lax.optimization_barrier(values)


def pick(stacked, index):
    return lax.dynamic_index_in_dim(stacked, index, 0, keepdims=False)


def place(blocks, slots, shape, axis):
    def kernel(slots_ref, *refs):
        sources, out, sems = refs[:-2], refs[-2], refs[-1]
        copies = []
        for k, source in enumerate(sources):
            target = out.at[slots_ref[k]] if axis == 0 else out.at[:, slots_ref[k]]
            copies.append(pltpu.make_async_copy(source, target, sems.at[k]))
        for copy in copies:
            copy.start()
        for copy in copies:
            copy.wait()

    anywhere = pl.BlockSpec(memory_space=pl.ANY)
    size = sum(block.size for block in blocks) * 4
    return pl.pallas_call(
        kernel,
        out_shape=jax.ShapeDtypeStruct(shape, blocks[0].dtype),
        in_specs=[pl.BlockSpec(memory_space=pltpu.SMEM)] + [anywhere] * len(blocks),
        out_specs=anywhere,
        scratch_shapes=[pltpu.SemaphoreType.DMA((len(blocks),))],
        cost_estimate=pl.CostEstimate(flops=0, bytes_accessed=size, transcendentals=0),
    )(slots.astype(jnp.int32), *blocks)


def normed(values, gain):
    scale = lax.rsqrt(jnp.mean(values * values, -1, keepdims=True) + norm_eps)
    unit = values * scale
    return (unit, scale, (unit * gain).astype(bf16))


def norm_back(grad_out, unit, scale, gain):
    grad_gain = jnp.sum(grad_out * unit, 0)
    grad_unit = grad_out * gain
    grad_in = scale * (grad_unit - unit * jnp.mean(grad_unit * unit, -1, keepdims=True))
    return (grad_in, grad_gain)


def adamw(master, first, second, grad, rate, decay):
    first_new = beta_one * first + (1.0 - beta_one) * grad
    second_new = beta_two * second + (1.0 - beta_two) * grad * grad
    first_hat = first_new / (1.0 - beta_one**STEP)
    second_hat = second_new / (1.0 - beta_two**STEP)
    master_new = master - rate * (first_hat / (jnp.sqrt(second_hat) + adam_eps) + decay * master)
    return (master_new, first_new, second_new)


def local(
    inputs,
    cotangent,
    segments,
    w_in,
    w_out,
    conv_w,
    w_gate,
    w_up,
    w_down,
    gains,
    m_in,
    m_out,
    m_conv,
    m_gate,
    m_up,
    m_down,
    m_gains,
    v_in,
    v_out,
    v_conv,
    v_gate,
    v_up,
    v_down,
    v_gains,
):
    seqs_here, stretch, width = inputs.shape
    rows = seqs_here * stretch
    n_dp = lax.axis_size("dp")
    n_seq = lax.axis_size("seq")
    n_z = n_dp // 2
    own = w_in.shape[0]
    own_ff = w_down.shape[0]
    ff_part = n_dp * own_ff
    dp = lax.axis_index("dp")
    sq = lax.axis_index("seq")
    z = dp // 2
    core = dp % 2
    first_core = core == 0

    lane = n_seq * own

    def halves(full):
        blocks = [full[:, i * lane : (i + 1) * lane] for i in range(2 * n_z)]
        even = jnp.concatenate(blocks[0::2], 1)
        odd = jnp.concatenate(blocks[1::2], 1)
        return jnp.where(first_core, even, odd), jnp.where(first_core, odd, even)

    def seq_ordered(pieces):
        stacked = jnp.stack(pieces, 0)
        return jnp.stack([pick(stacked, sq ^ j) for j in range(n_seq)], 0)

    def by_part(weight):
        low = weight.astype(bf16).reshape(own, n_dp, n_seq, own_ff)
        return low.transpose(2, 0, 1, 3).reshape(n_seq, own, ff_part)

    smalls = jnp.pad(
        jnp.concatenate([conv_w, gains], 0).astype(bf16), ((0, own - 5), (0, LANES - own))
    )
    mix = jnp.concatenate([w_in.astype(bf16), w_out.astype(bf16), smalls], 1)
    gate_up = jnp.concatenate([by_part(w_gate), by_part(w_up)], 2)

    residual_low = inputs.reshape(rows, width)
    edge_ids = jnp.pad(segments[:, -2:, None].astype(bf16), ((0, 0), (0, 0), (0, LANES - 1)))
    edge = from_behind(jnp.concatenate([inputs[:, -2:, :], edge_ids], 2), "seq", 1)
    z_parts = [along_z(mix, -k) for k in range(1, n_z)]
    gu_parts = [across_seq(pick(gate_up, sq ^ k), k) for k in range(1, n_seq)]
    low_down = w_down.astype(bf16)
    z_parts, gu_parts, edge, low_down = tie((z_parts, gu_parts, edge, low_down))
    gate_up = seq_ordered([pick(gate_up, sq)] + gu_parts)
    mat_gate_up = lax.all_gather(gate_up, "dp", axis=0).reshape(width, 2 * ff_part)
    mat_down = lax.all_gather(low_down, "dp", axis=0, tiled=True)

    columns = mix.shape[1]

    z_slots = (z + jnp.arange(n_z)) % n_z
    seq_slots = sq ^ jnp.arange(n_seq)
    core_slots = core ^ jnp.arange(2)
    last = n_seq - 1
    order = [0] + list(range(last, 0, -1))
    grad_top = cotangent.reshape(rows, width)
    z_order = place([mix] + z_parts, z_slots, (n_z, own, columns), 0)
    mix_parts = {k: across_seq(z_order, k) for k in order[1:]}
    mix_parts, top_out = tie((mix_parts, grad_top))
    mix_parts[0] = z_order
    mix_mine = place(
        [mix_parts[k] for k in range(n_seq)], seq_slots, (n_z, n_seq, own, columns), 1
    ).reshape(width // 2, columns)

    mix_other = to_sibling(mix_mine)
    tops = {k: across_seq(top_out, k) for k in order[1:]}

    cut_in, cut_out = 3 * width, 4 * width
    in_mine, in_other = mix_mine[:, :cut_in], mix_other[:, :cut_in]
    out_mine, out_other = mix_mine[:, cut_in:cut_out], mix_other[:, cut_in:cut_out]

    half = width // 2
    feature = lax.broadcasted_iota(jnp.int32, (1, width), 1)
    lane_of = lax.broadcasted_iota(jnp.int32, (LANES, width), 0)
    spread = (lane_of == feature % own).astype(bf16)

    def row_blocks(which):
        row = lax.broadcasted_iota(jnp.int32, (half, 1), 0) // own
        return ((row // n_seq) * 2 + which) * n_seq + row % n_seq

    def small_rows(packed, which):
        wide = jnp.where(row_blocks(which) == feature // own, dot(packed, spread), 0.0)
        chosen = lax.broadcasted_iota(jnp.int32, (8, half), 1) % own
        chosen = chosen == lax.broadcasted_iota(jnp.int32, (8, half), 0)
        return dot(chosen.astype(bf16), wide.astype(bf16))

    small_all = small_rows(mix_mine[:, cut_out:], core) + small_rows(
        mix_other[:, cut_out:], 1 - core
    )
    taps, gain_vals = small_all[:3], small_all[3:5]

    residual = residual_low.astype(f32)
    unit_one, scale_one, norm_one = normed(residual, gain_vals[0])
    edge_rows = jnp.pad(edge[:, :, :width].reshape(2 * seqs_here, width), ((0, 12), (0, 0)))
    edge_mine, edge_other = halves(normed(edge_rows.astype(f32), gain_vals[0])[2])

    def edge_dot(start):
        stop = start + width
        return dot(edge_mine, in_mine[:, start:stop]) + dot(edge_other, in_other[:, start:stop])

    prev_rows = (edge_dot(0) * edge_dot(2 * width)).astype(bf16)[: 2 * seqs_here]
    prev_rows = prev_rows.reshape(seqs_here, 2, width)
    first_block = sq == 0
    prev_ids = jnp.where(first_block, -1, edge[:, :, width].astype(jnp.int32))
    norm_mine, norm_other = halves(norm_one)
    projected = dot(norm_mine, in_mine) + dot(norm_other, in_other)
    b_gate = projected[:, :width]
    c_gate = projected[:, width : 2 * width]
    x_part = projected[:, 2 * width :]
    conv_in = (b_gate * x_part).astype(bf16).reshape(seqs_here, stretch, width)
    extended = jnp.concatenate([prev_rows, conv_in], 1).astype(f32)
    ext_ids = jnp.concatenate([prev_ids, segments], 1)
    near_one = (ext_ids[:, 1:-1] == segments).astype(f32)[..., None]
    near_two = (ext_ids[:, :-2] == segments).astype(f32)[..., None]
    tap_now = extended[:, 2:]
    tap_one = extended[:, 1:-1] * near_one
    tap_two = extended[:, :-2] * near_two
    conv_out = (taps[2] * tap_now + taps[1] * tap_one + taps[0] * tap_two).reshape(rows, width)
    mixed_in = (c_gate * conv_out).astype(bf16)
    mixed_mine, mixed_other = halves(mixed_in)
    middle = residual + dot(mixed_mine, out_mine) + dot(mixed_other, out_other)
    unit_two, scale_two, norm_two = normed(middle, gain_vals[1])

    shape = (n_z, 2, half // n_z)
    in_full = place(
        [in_mine.reshape(n_z, -1, cut_in), in_other.reshape(n_z, -1, cut_in)],
        core_slots,
        shape + (cut_in,),
        1,
    ).reshape(width, cut_in)
    out_full = place(
        [out_mine.reshape(n_z, -1, width), out_other.reshape(n_z, -1, width)],
        core_slots,
        shape + (width,),
        1,
    ).reshape(width, width)

    norm_two, tops = tie((norm_two, tops))
    tops[0] = grad_top
    norms = {k: across_seq(norm_two, k) for k in order[1:]}
    norms[0] = norm_two
    hiddens, act_grads, norm_parts, out_parts = {}, {}, {}, {}

    def hidden_block(k):
        both = dot(norms[k], mat_gate_up)
        gate, up_part = both[:, :ff_part], both[:, ff_part:]
        sigma = jax.nn.sigmoid(gate)
        silu_vals = gate * sigma
        grad_hidden = right_contract(tops[k], mat_down)
        hiddens[k] = (silu_vals * up_part).astype(bf16)
        grad_gate_act = (grad_hidden * up_part * sigma * (1.0 + gate * (1.0 - sigma))).astype(bf16)
        grad_up_act = (grad_hidden * silu_vals).astype(bf16)
        act_grads[k] = jnp.concatenate([grad_gate_act, grad_up_act], 1)

    hidden_block(0)
    norms[last], hiddens[0], act_grads[0], in_full, out_full = tie(
        (norms[last], hiddens[0], act_grads[0], in_full, out_full)
    )
    hidden_block(last)
    norm_parts[last] = right_contract(act_grads[last], mat_gate_up).astype(bf16)
    out_parts[0] = dot(hiddens[0], mat_down)
    norm_parts[0] = right_contract(act_grads[0], mat_gate_up)
    norm_sums = {last: across_seq(norm_parts[last], last)}
    for k in order[2:]:
        norms[k], norm_parts, out_parts, act_grads = tie(
            (norms[k], norm_parts, out_parts, act_grads)
        )
        hidden_block(k)
        if k == order[-1]:
            act_grads, norm_sums[last] = tie((act_grads, norm_sums[last]))
        norm_parts[k] = right_contract(act_grads[k], mat_gate_up).astype(bf16)
        norm_sums[k] = across_seq(norm_parts[k], k)
    norm_parts, hiddens, act_grads = tie((norm_parts, hiddens, act_grads))

    def rows_of(blocks):
        return jnp.concatenate([blocks[k] for k in order], 0)

    grad_down = left_contract(rows_of(hiddens), rows_of(tops)).astype(bf16)
    sum_down = lax.psum_scatter(grad_down, "dp", scatter_dimension=0, tiled=True).astype(f32)
    hiddens, grad_down = tie((hiddens, grad_down))
    grad_gate_up = left_contract(rows_of(norms), rows_of(act_grads)).astype(bf16)
    gu_sum = lax.psum_scatter(grad_gate_up, "dp", scatter_dimension=0, tiled=True)
    hiddens, grad_gate_up = tie((hiddens, grad_gate_up))
    out_low = {k: dot(hiddens[k], mat_down).astype(bf16) for k in order[1:]}
    norm_sums, out_low = tie((norm_sums, out_low))
    grad_norm_two = norm_parts[0]
    for k in order[1:]:
        grad_norm_two = grad_norm_two + norm_sums[k].astype(f32)

    back_two, gain_two = norm_back(grad_norm_two, unit_two, scale_two, gain_vals[1])
    grad_middle = grad_top.astype(f32) + back_two
    grad_branch = grad_middle.astype(bf16)
    grad_out_mine = left_contract(mixed_mine, grad_branch)
    grad_out_other = left_contract(mixed_other, grad_branch)
    grad_mixed = right_contract(grad_branch, out_full)
    grad_c = grad_mixed * conv_out
    grad_conv = (grad_mixed * c_gate).reshape(seqs_here, stretch, width)
    grad_taps = [
        jnp.sum(tap_two * grad_conv, (0, 1)),
        jnp.sum(tap_one * grad_conv, (0, 1)),
        jnp.sum(tap_now * grad_conv, (0, 1)),
    ]
    term_now = taps[2] * grad_conv
    term_one = taps[1] * grad_conv * near_one
    term_two = taps[0] * grad_conv * near_two
    grad_ext = (
        jnp.pad(term_now, ((0, 0), (2, 0), (0, 0)))
        + jnp.pad(term_one, ((0, 0), (1, 1), (0, 0)))
        + jnp.pad(term_two, ((0, 0), (0, 2), (0, 0)))
    )
    next_terms = from_behind(grad_ext[:, :2, :], "seq", -1)
    next_terms, out_low[last] = tie((next_terms, out_low[last]))
    out_sums = {last: across_seq(out_low[last], last)}
    grad_conv_in = (
        grad_ext[:, 2:, :] + jnp.pad(next_terms, ((0, 0), (stretch - 2, 0), (0, 0)))
    ).reshape(rows, width)
    grad_proj = jnp.concatenate([grad_conv_in * x_part, grad_c, grad_conv_in * b_gate], -1).astype(
        bf16
    )
    grad_in_mine = left_contract(norm_mine, grad_proj)
    grad_in_other = left_contract(norm_other, grad_proj)
    grad_norm_one = right_contract(grad_proj, in_full)
    back_one, gain_one = norm_back(grad_norm_one, unit_one, scale_one, gain_vals[0])
    input_grad = (grad_middle + back_one).reshape(seqs_here, stretch, width)

    def sum_core(mine, other):
        return mine + to_sibling(other.astype(bf16)).astype(f32)

    small_grads = jnp.stack(grad_taps + [gain_one, gain_two], 0)
    small_grads = (small_grads + to_sibling(small_grads)).astype(bf16)
    small_wide = jnp.tile(jnp.pad(small_grads, ((0, own - 5), (0, 0))), (half // own, 1))
    small_wide = jnp.where(row_blocks(core) == feature // own, small_wide, 0.0).astype(bf16)
    mixed = jnp.concatenate(
        [
            sum_core(grad_in_mine, grad_in_other),
            sum_core(grad_out_mine, grad_out_other),
            right_contract(small_wide, spread),
        ],
        1,
    ).astype(bf16)
    mixed, out_sums, sum_down = tie((mixed, out_sums, sum_down))
    mixed = mixed.reshape(n_z, n_seq, own, -1)

    def seq_block(index):
        return lax.dynamic_index_in_dim(mixed, index, 1, keepdims=False)

    seq_parts = [across_seq(seq_block(sq ^ k), k) for k in order[1:]]
    seq_parts, gu_sum, out_low = tie((seq_parts, gu_sum, out_low))
    total = seq_block(sq).astype(f32)
    for part in seq_parts:
        total = total + part.astype(f32)
    low = total.astype(bf16)
    z_sums = [along_z(pick(low, (z + k) % n_z), k) for k in range(1, n_z)]
    gu_sum = gu_sum.reshape(n_seq, own, 2 * ff_part)
    gu_parts = [across_seq(pick(gu_sum, sq ^ k), k) for k in range(1, n_seq)]
    for k in order[2:]:
        out_sums[k] = across_seq(out_low[k], k)
    z_sums, gu_parts = tie((z_sums, gu_parts))
    total = pick(total, z)
    for part in z_sums:
        total = total + part.astype(f32)
    sum_in, sum_out, small_sum = total[:, :cut_in], total[:, cut_in:cut_out], total[:, cut_out:]

    gu_sum = seq_ordered([pick(gu_sum, sq)] + gu_parts).astype(f32)
    output = middle + out_parts[0]
    for k in order[1:]:
        output = output + out_sums[k].astype(f32)
    output = output.astype(bf16)

    def by_row(part):
        return (
            part.reshape(n_seq, own, n_dp, own_ff)
            .transpose(1, 2, 0, 3)
            .reshape(own, n_seq * ff_part)
        )

    sum_gate = by_row(gu_sum[:, :, :ff_part])
    sum_up = by_row(gu_sum[:, :, ff_part:])

    reduced = (
        sum_in,
        sum_out,
        small_sum[:3, :own],
        sum_gate,
        sum_up,
        sum_down,
        small_sum[3:5, :own],
    )
    masters = (w_in, w_out, conv_w, w_gate, w_up, w_down, gains)
    firsts = (m_in, m_out, m_conv, m_gate, m_up, m_down, m_gains)
    seconds = (v_in, v_out, v_conv, v_gate, v_up, v_down, v_gains)
    rates = (learn_rate, learn_rate, small_rate, learn_rate, learn_rate, learn_rate, small_rate)
    decays = (weight_decay, weight_decay, 0.0, weight_decay, weight_decay, weight_decay, 0.0)
    updated = [
        adamw(
            masters[index],
            firsts[index],
            seconds[index],
            reduced[index],
            rates[index],
            decays[index],
        )
        for index in range(7)
    ]
    new_w = [item[0] for item in updated]
    new_m = [item[1] for item in updated]
    new_v = [item[2] for item in updated]
    return (
        output.reshape(seqs_here, stretch, width),
        input_grad,
        *new_w,
        *new_m,
        *new_v,
    )


def solution(mesh):
    tokens = P("dp", "seq", None)
    matrix = P(("dp", "seq"), None)
    vector = P(None, ("dp", "seq"))
    weights = (matrix, matrix, vector, matrix, matrix, matrix, vector)
    return jax.shard_map(
        local,
        mesh=mesh,
        in_specs=(tokens, tokens, P("dp", "seq")) + weights * 3,
        out_specs=(tokens, tokens) + weights * 3,
        check_vma=False,
    )
```

```python
import jax
import jax.numpy as jnp
from jax import lax
from jax.experimental import pallas as pl
from jax.experimental.pallas import tpu as pltpu
from jax.sharding import PartitionSpec as P

STEP = 10


norm_eps = 1e-05
learn_rate = 0.02
small_rate = 1.0
beta_one = 0.9
beta_two = 0.95
adam_eps = 1e-08
weight_decay = 0.1
LANES = 128
bf16 = jnp.bfloat16
f32 = jnp.float32


def from_behind(shard, axis, by):
    peers = lax.axis_size(axis)
    pairs = [(i, i + by) for i in range(peers) if 0 <= i + by < peers]
    return lax.ppermute(shard, axis, pairs)


def to_sibling(block):
    return lax.ppermute(block, "dp", [(i, i ^ 1) for i in range(lax.axis_size("dp"))])


def along_z(block, by):
    count = lax.axis_size("dp")
    return lax.ppermute(block, "dp", [(i, (i + 2 * by) % count) for i in range(count)])


def across_seq(block, by):
    return lax.ppermute(block, "seq", [(i, i ^ by) for i in range(lax.axis_size("seq"))])


def dot(first, second):
    return jnp.dot(first, second, preferred_element_type=f32)


def left_contract(first, second):
    return lax.dot_general(first, second, (((0,), (0,)), ((), ())), preferred_element_type=f32)


def right_contract(first, second):
    return lax.dot_general(first, second, (((1,), (1,)), ((), ())), preferred_element_type=f32)


def tie(values):
    return lax.optimization_barrier(values)


def pick(stacked, index):
    return lax.dynamic_index_in_dim(stacked, index, 0, keepdims=False)


def place(blocks, slots, chunk, first=0, columns=None):
    outer, depth, width = blocks[0].shape
    columns = width if columns is None else columns
    count = len(blocks)

    def kernel(slots_ref, *refs):
        for k in range(count):
            refs[-1][:, slots_ref[k]] = refs[k][...]

    size = 4 * count * outer * depth * columns
    return pl.pallas_call(
        kernel,
        grid=(columns // chunk,),
        out_shape=jax.ShapeDtypeStruct((outer, count, depth, columns), blocks[0].dtype),
        in_specs=[pl.BlockSpec(memory_space=pltpu.SMEM)]
        + [pl.BlockSpec((outer, depth, chunk), lambda j: (0, 0, j + first // chunk))] * count,
        out_specs=pl.BlockSpec((outer, count, depth, chunk), lambda j: (0, 0, 0, j)),
        compiler_params=pltpu.CompilerParams(vmem_limit_bytes=32 * 2**20),
        cost_estimate=pl.CostEstimate(flops=0, bytes_accessed=size, transcendentals=0),
    )(slots.astype(jnp.int32), *blocks)


def normed(values, gain):
    scale = lax.rsqrt(jnp.mean(values * values, -1, keepdims=True) + norm_eps)
    unit = values * scale
    return (unit, scale, (unit * gain).astype(bf16))


def norm_back(grad_out, unit, scale, gain):
    grad_gain = jnp.sum(grad_out * unit, 0)
    grad_unit = grad_out * gain
    grad_in = scale * (grad_unit - unit * jnp.mean(grad_unit * unit, -1, keepdims=True))
    return (grad_in, grad_gain)


def adamw(master, first, second, grad, rate, decay):
    first_new = beta_one * first + (1.0 - beta_one) * grad
    second_new = beta_two * second + (1.0 - beta_two) * grad * grad
    first_hat = first_new / (1.0 - beta_one**STEP)
    second_hat = second_new / (1.0 - beta_two**STEP)
    master_new = master - rate * (first_hat / (jnp.sqrt(second_hat) + adam_eps) + decay * master)
    return (master_new, first_new, second_new)


def local(
    inputs,
    cotangent,
    segments,
    w_in,
    w_out,
    conv_w,
    w_gate,
    w_up,
    w_down,
    gains,
    m_in,
    m_out,
    m_conv,
    m_gate,
    m_up,
    m_down,
    m_gains,
    v_in,
    v_out,
    v_conv,
    v_gate,
    v_up,
    v_down,
    v_gains,
):
    seqs_here, stretch, width = inputs.shape
    rows = seqs_here * stretch
    n_dp = lax.axis_size("dp")
    n_seq = lax.axis_size("seq")
    n_z = n_dp // 2
    own = w_in.shape[0]
    own_ff = w_down.shape[0]
    ff_part = n_dp * own_ff
    dp = lax.axis_index("dp")
    sq = lax.axis_index("seq")
    z = dp // 2
    core = dp % 2
    first_core = core == 0

    lane = n_seq * own

    def halves(full):
        blocks = [full[:, i * lane : (i + 1) * lane] for i in range(2 * n_z)]
        even = jnp.concatenate(blocks[0::2], 1)
        odd = jnp.concatenate(blocks[1::2], 1)
        return jnp.where(first_core, even, odd), jnp.where(first_core, odd, even)

    def seq_ordered(pieces):
        stacked = jnp.stack(pieces, 0)
        return jnp.stack([pick(stacked, sq ^ j) for j in range(n_seq)], 0)

    def by_part(weight):
        low = weight.astype(bf16).reshape(own, n_dp, n_seq, own_ff)
        return low.transpose(2, 0, 1, 3).reshape(n_seq, own, ff_part)

    smalls = jnp.pad(
        jnp.concatenate([conv_w, gains], 0).astype(bf16), ((0, own - 5), (0, LANES - own))
    )
    mix = jnp.concatenate([w_in.astype(bf16), w_out.astype(bf16), smalls], 1)
    gate_up = jnp.concatenate([by_part(w_gate), by_part(w_up)], 2)

    residual_low = inputs.reshape(rows, width)
    edge_ids = jnp.pad(segments[:, -2:, None].astype(bf16), ((0, 0), (0, 0), (0, LANES - 1)))
    edge = from_behind(jnp.concatenate([inputs[:, -2:, :], edge_ids], 2), "seq", 1)
    z_parts = [along_z(mix, -k) for k in range(1, n_z)]
    gu_parts = [across_seq(pick(gate_up, sq ^ k), k) for k in range(1, n_seq)]
    low_down = w_down.astype(bf16)
    z_parts, gu_parts, edge, low_down = tie((z_parts, gu_parts, edge, low_down))
    gate_up = seq_ordered([pick(gate_up, sq)] + gu_parts)
    mat_gate_up = lax.all_gather(gate_up, "dp", axis=0).reshape(width, 2 * ff_part)
    mat_down = lax.all_gather(low_down, "dp", axis=0, tiled=True)

    columns = mix.shape[1]

    z_slots = (z + jnp.arange(n_z)) % n_z
    seq_slots = sq ^ jnp.arange(n_seq)
    core_slots = core ^ jnp.arange(2)
    last = n_seq - 1
    order = [0] + list(range(last, 0, -1))
    grad_top = cotangent.reshape(rows, width)
    z_order = place([part[None] for part in [mix] + z_parts], z_slots, columns // 3)[0]
    mix_parts = {k: across_seq(z_order, k) for k in order[1:]}
    mix_parts, top_out = tie((mix_parts, grad_top))
    mix_parts[0] = z_order
    mix_mine = place([mix_parts[k] for k in range(n_seq)], seq_slots, columns // 3)
    mix_mine = mix_mine.reshape(width // 2, columns)

    mix_other = to_sibling(mix_mine)
    tops = {k: across_seq(top_out, k) for k in order[1:]}

    cut_in, cut_out = 3 * width, 4 * width
    in_mine, in_other = mix_mine[:, :cut_in], mix_other[:, :cut_in]
    out_mine, out_other = mix_mine[:, cut_in:cut_out], mix_other[:, cut_in:cut_out]

    half = width // 2
    feature = lax.broadcasted_iota(jnp.int32, (1, width), 1)
    lane_of = lax.broadcasted_iota(jnp.int32, (LANES, width), 0)
    spread = (lane_of == feature % own).astype(bf16)

    def row_blocks(which):
        row = lax.broadcasted_iota(jnp.int32, (half, 1), 0) // own
        return ((row // n_seq) * 2 + which) * n_seq + row % n_seq

    def small_rows(packed, which):
        wide = jnp.where(row_blocks(which) == feature // own, dot(packed, spread), 0.0)
        chosen = lax.broadcasted_iota(jnp.int32, (8, half), 1) % own
        chosen = chosen == lax.broadcasted_iota(jnp.int32, (8, half), 0)
        return dot(chosen.astype(bf16), wide.astype(bf16))

    small_all = small_rows(mix_mine[:, cut_out:], core) + small_rows(
        mix_other[:, cut_out:], 1 - core
    )
    taps, gain_vals = small_all[:3], small_all[3:5]

    residual = residual_low.astype(f32)
    unit_one, scale_one, norm_one = normed(residual, gain_vals[0])
    edge_rows = jnp.pad(edge[:, :, :width].reshape(2 * seqs_here, width), ((0, 12), (0, 0)))
    edge_mine, edge_other = halves(normed(edge_rows.astype(f32), gain_vals[0])[2])

    def edge_dot(start):
        stop = start + width
        return dot(edge_mine, in_mine[:, start:stop]) + dot(edge_other, in_other[:, start:stop])

    prev_rows = (edge_dot(0) * edge_dot(2 * width)).astype(bf16)[: 2 * seqs_here]
    prev_rows = prev_rows.reshape(seqs_here, 2, width)
    first_block = sq == 0
    prev_ids = jnp.where(first_block, -1, edge[:, :, width].astype(jnp.int32))
    norm_mine, norm_other = halves(norm_one)
    projected = dot(norm_mine, in_mine) + dot(norm_other, in_other)
    b_gate = projected[:, :width]
    c_gate = projected[:, width : 2 * width]
    x_part = projected[:, 2 * width :]
    conv_in = (b_gate * x_part).astype(bf16).reshape(seqs_here, stretch, width)
    extended = jnp.concatenate([prev_rows, conv_in], 1).astype(f32)
    ext_ids = jnp.concatenate([prev_ids, segments], 1)
    near_one = (ext_ids[:, 1:-1] == segments).astype(f32)[..., None]
    near_two = (ext_ids[:, :-2] == segments).astype(f32)[..., None]
    tap_now = extended[:, 2:]
    tap_one = extended[:, 1:-1] * near_one
    tap_two = extended[:, :-2] * near_two
    conv_out = (taps[2] * tap_now + taps[1] * tap_one + taps[0] * tap_two).reshape(rows, width)
    mixed_in = (c_gate * conv_out).astype(bf16)
    mixed_mine, mixed_other = halves(mixed_in)
    middle = residual + dot(mixed_mine, out_mine) + dot(mixed_other, out_other)
    unit_two, scale_two, norm_two = normed(middle, gain_vals[1])

    both_halves = [mix_mine.reshape(n_z, -1, columns), mix_other.reshape(n_z, -1, columns)]
    in_full = place(both_halves, core_slots, width, 0, cut_in).reshape(width, cut_in)
    out_full = place(both_halves, core_slots, width, cut_in, width).reshape(width, width)

    norm_two, tops = tie((norm_two, tops))
    tops[0] = grad_top
    norms = {k: across_seq(norm_two, k) for k in order[1:]}
    norms[0] = norm_two
    hiddens, act_grads, norm_parts, out_parts = {}, {}, {}, {}

    def hidden_block(k):
        both = dot(norms[k], mat_gate_up)
        gate, up_part = both[:, :ff_part], both[:, ff_part:]
        sigma = jax.nn.sigmoid(gate)
        silu_vals = gate * sigma
        grad_hidden = right_contract(tops[k], mat_down)
        hiddens[k] = (silu_vals * up_part).astype(bf16)
        grad_gate_act = (grad_hidden * up_part * sigma * (1.0 + gate * (1.0 - sigma))).astype(bf16)
        grad_up_act = (grad_hidden * silu_vals).astype(bf16)
        act_grads[k] = jnp.concatenate([grad_gate_act, grad_up_act], 1)

    hidden_block(0)
    norms[last], hiddens[0], act_grads[0], in_full, out_full = tie(
        (norms[last], hiddens[0], act_grads[0], in_full, out_full)
    )
    hidden_block(last)
    norm_parts[last] = right_contract(act_grads[last], mat_gate_up).astype(bf16)
    out_parts[0] = dot(hiddens[0], mat_down)
    norm_parts[0] = right_contract(act_grads[0], mat_gate_up)
    norm_sums = {last: across_seq(norm_parts[last], last)}
    for k in order[2:]:
        norms[k], norm_parts, out_parts, act_grads = tie(
            (norms[k], norm_parts, out_parts, act_grads)
        )
        hidden_block(k)
        if k == order[-1]:
            act_grads, norm_sums[last] = tie((act_grads, norm_sums[last]))
        norm_parts[k] = right_contract(act_grads[k], mat_gate_up).astype(bf16)
        norm_sums[k] = across_seq(norm_parts[k], k)
    norm_parts, hiddens, act_grads = tie((norm_parts, hiddens, act_grads))

    def rows_of(blocks):
        return jnp.concatenate([blocks[k] for k in order], 0)

    grad_down = left_contract(rows_of(hiddens), rows_of(tops)).astype(bf16)
    sum_down = lax.psum_scatter(grad_down, "dp", scatter_dimension=0, tiled=True).astype(f32)
    hiddens, grad_down = tie((hiddens, grad_down))
    grad_gate_up = left_contract(rows_of(norms), rows_of(act_grads)).astype(bf16)
    gu_sum = lax.psum_scatter(grad_gate_up, "dp", scatter_dimension=0, tiled=True)
    hiddens, grad_gate_up = tie((hiddens, grad_gate_up))
    out_low = {k: dot(hiddens[k], mat_down).astype(bf16) for k in order[1:]}
    norm_sums, out_low = tie((norm_sums, out_low))
    grad_norm_two = norm_parts[0]
    for k in order[1:]:
        grad_norm_two = grad_norm_two + norm_sums[k].astype(f32)

    back_two, gain_two = norm_back(grad_norm_two, unit_two, scale_two, gain_vals[1])
    grad_middle = grad_top.astype(f32) + back_two
    grad_branch = grad_middle.astype(bf16)
    grad_out_mine = left_contract(mixed_mine, grad_branch)
    grad_out_other = left_contract(mixed_other, grad_branch)
    grad_mixed = right_contract(grad_branch, out_full)
    grad_c = grad_mixed * conv_out
    grad_conv = (grad_mixed * c_gate).reshape(seqs_here, stretch, width)
    grad_taps = [
        jnp.sum(tap_two * grad_conv, (0, 1)),
        jnp.sum(tap_one * grad_conv, (0, 1)),
        jnp.sum(tap_now * grad_conv, (0, 1)),
    ]
    term_now = taps[2] * grad_conv
    term_one = taps[1] * grad_conv * near_one
    term_two = taps[0] * grad_conv * near_two
    grad_ext = (
        jnp.pad(term_now, ((0, 0), (2, 0), (0, 0)))
        + jnp.pad(term_one, ((0, 0), (1, 1), (0, 0)))
        + jnp.pad(term_two, ((0, 0), (0, 2), (0, 0)))
    )
    next_terms = from_behind(grad_ext[:, :2, :], "seq", -1)
    next_terms, out_low[last] = tie((next_terms, out_low[last]))
    out_sums = {last: across_seq(out_low[last], last)}
    grad_conv_in = (
        grad_ext[:, 2:, :] + jnp.pad(next_terms, ((0, 0), (stretch - 2, 0), (0, 0)))
    ).reshape(rows, width)
    grad_proj = jnp.concatenate([grad_conv_in * x_part, grad_c, grad_conv_in * b_gate], -1).astype(
        bf16
    )
    grad_in_mine = left_contract(norm_mine, grad_proj)
    grad_in_other = left_contract(norm_other, grad_proj)
    grad_norm_one = right_contract(grad_proj, in_full)
    back_one, gain_one = norm_back(grad_norm_one, unit_one, scale_one, gain_vals[0])
    input_grad = (grad_middle + back_one).reshape(seqs_here, stretch, width)

    def sum_core(mine, other):
        return mine + to_sibling(other.astype(bf16)).astype(f32)

    small_grads = jnp.stack(grad_taps + [gain_one, gain_two], 0)
    small_grads = (small_grads + to_sibling(small_grads)).astype(bf16)
    small_wide = jnp.tile(jnp.pad(small_grads, ((0, own - 5), (0, 0))), (half // own, 1))
    small_wide = jnp.where(row_blocks(core) == feature // own, small_wide, 0.0).astype(bf16)
    in_received = to_sibling(grad_in_other.astype(bf16))
    in_received, out_sums[last] = tie((in_received, out_sums[last]))
    mixed = jnp.concatenate(
        [
            grad_in_mine + in_received.astype(f32),
            sum_core(grad_out_mine, grad_out_other),
            right_contract(small_wide, spread),
        ],
        1,
    ).astype(bf16)
    mixed = mixed.reshape(n_z, n_seq, own, -1)

    def seq_block(index):
        return lax.dynamic_index_in_dim(mixed, index, 1, keepdims=False)

    seq_parts = [across_seq(seq_block(sq ^ k), k) for k in order[1:]]
    gu_sum = gu_sum.reshape(n_seq, own, 2 * ff_part)
    gu_parts = [across_seq(pick(gu_sum, sq ^ k), k) for k in range(1, n_seq)]
    seq_parts, gu_parts, out_low, sum_down = tie((seq_parts, gu_parts, out_low, sum_down))
    total = seq_block(sq).astype(f32)
    for part in seq_parts:
        total = total + part.astype(f32)
    low = total.astype(bf16)
    z_sums = [along_z(pick(low, (z + k) % n_z), k) for k in range(1, n_z)]
    for k in order[2:]:
        out_sums[k] = across_seq(out_low[k], k)
    gu_sum = seq_ordered([pick(gu_sum, sq)] + gu_parts).astype(f32)

    def by_row(part):
        return (
            part.reshape(n_seq, own, n_dp, own_ff)
            .transpose(1, 2, 0, 3)
            .reshape(own, n_seq * ff_part)
        )

    def matrix_step(master, first, second, grad):
        return adamw(master, first, second, grad, learn_rate, weight_decay)

    step_gate = matrix_step(w_gate, m_gate, v_gate, by_row(gu_sum[:, :, :ff_part]))
    step_up = matrix_step(w_up, m_up, v_up, by_row(gu_sum[:, :, ff_part:]))
    step_down = matrix_step(w_down, m_down, v_down, sum_down)
    z_sums, step_gate, step_up, step_down = tie((z_sums, step_gate, step_up, step_down))
    total = pick(total, z)
    for part in z_sums:
        total = total + part.astype(f32)
    sum_in, sum_out, small_sum = total[:, :cut_in], total[:, cut_in:cut_out], total[:, cut_out:]

    output = middle + out_parts[0]
    for k in order[1:]:
        output = output + out_sums[k].astype(f32)
    output = output.astype(bf16)

    step_in = matrix_step(w_in, m_in, v_in, sum_in)
    step_out = matrix_step(w_out, m_out, v_out, sum_out)
    step_conv = adamw(conv_w, m_conv, v_conv, small_sum[:3, :own], small_rate, 0.0)
    step_gains = adamw(gains, m_gains, v_gains, small_sum[3:5, :own], small_rate, 0.0)
    updated = [step_in, step_out, step_conv, step_gate, step_up, step_down, step_gains]
    new_w = [item[0] for item in updated]
    new_m = [item[1] for item in updated]
    new_v = [item[2] for item in updated]
    return (
        output.reshape(seqs_here, stretch, width),
        input_grad,
        *new_w,
        *new_m,
        *new_v,
    )


def solution(mesh):
    tokens = P("dp", "seq", None)
    matrix = P(("dp", "seq"), None)
    vector = P(None, ("dp", "seq"))
    weights = (matrix, matrix, vector, matrix, matrix, matrix, vector)
    return jax.shard_map(
        local,
        mesh=mesh,
        in_specs=(tokens, tokens, P("dp", "seq")) + weights * 3,
        out_specs=(tokens, tokens) + weights * 3,
        check_vma=False,
    )
```

```python
import jax
import jax.numpy as jnp
from jax import lax
from jax.experimental import pallas as pl
from jax.experimental.pallas import tpu as pltpu
from jax.sharding import PartitionSpec as P

STEP = 10


norm_eps = 1e-05
learn_rate = 0.02
small_rate = 1.0
beta_one = 0.9
beta_two = 0.95
adam_eps = 1e-08
weight_decay = 0.1
LANES = 128
bf16 = jnp.bfloat16
f32 = jnp.float32


def from_behind(shard, axis, by):
    peers = lax.axis_size(axis)
    pairs = [(i, i + by) for i in range(peers) if 0 <= i + by < peers]
    return lax.ppermute(shard, axis, pairs)


def to_sibling(block):
    return lax.ppermute(block, "dp", [(i, i ^ 1) for i in range(lax.axis_size("dp"))])


def along_z(block, by):
    count = lax.axis_size("dp")
    return lax.ppermute(block, "dp", [(i, (i + 2 * by) % count) for i in range(count)])


def across_seq(block, by):
    return lax.ppermute(block, "seq", [(i, i ^ by) for i in range(lax.axis_size("seq"))])


def swap_near(block):
    count = lax.axis_size("seq")
    near = (1, 2) if count == 4 else range(1, count)
    return {k: across_seq(block, k) for k in near}


def swap_far(near):
    if lax.axis_size("seq") != 4:
        return {}
    half = near[1].shape[0] // 2
    first, second = across_seq(near[1][:half], 2), across_seq(near[2][half:], 1)
    return {3: jnp.concatenate([first, second], 0)}


def sum_far(block):
    half = block.shape[0] // 2
    return across_seq(block[:half], 1), across_seq(block[half:], 2)


def add_far(terms, received):
    if not received:
        return terms
    first, second = received
    half = first.shape[0]
    terms = dict(terms)
    terms[2] = jnp.concatenate([terms[2][:half] + first.astype(f32), terms[2][half:]], 0)
    terms[1] = jnp.concatenate([terms[1][:half], terms[1][half:] + second.astype(f32)], 0)
    return terms


def dot(first, second):
    return jnp.dot(first, second, preferred_element_type=f32)


def left_contract(first, second):
    return lax.dot_general(first, second, (((0,), (0,)), ((), ())), preferred_element_type=f32)


def right_contract(first, second):
    return lax.dot_general(first, second, (((1,), (1,)), ((), ())), preferred_element_type=f32)


def tie(values):
    return lax.optimization_barrier(values)


def pick(stacked, index):
    return lax.dynamic_index_in_dim(stacked, index, 0, keepdims=False)


def place(blocks, slots, chunk, first=0, columns=None):
    outer, depth, width = blocks[0].shape
    columns = width if columns is None else columns
    count = len(blocks)

    def kernel(slots_ref, *refs):
        for k in range(count):
            refs[-1][:, slots_ref[k]] = refs[k][...]

    size = 4 * count * outer * depth * columns
    return pl.pallas_call(
        kernel,
        grid=(columns // chunk,),
        out_shape=jax.ShapeDtypeStruct((outer, count, depth, columns), blocks[0].dtype),
        in_specs=[pl.BlockSpec(memory_space=pltpu.SMEM)]
        + [pl.BlockSpec((outer, depth, chunk), lambda j: (0, 0, j + first // chunk))] * count,
        out_specs=pl.BlockSpec((outer, count, depth, chunk), lambda j: (0, 0, 0, j)),
        compiler_params=pltpu.CompilerParams(vmem_limit_bytes=32 * 2**20),
        cost_estimate=pl.CostEstimate(flops=0, bytes_accessed=size, transcendentals=0),
    )(slots.astype(jnp.int32), *blocks)


def normed(values, gain):
    scale = lax.rsqrt(jnp.mean(values * values, -1, keepdims=True) + norm_eps)
    unit = values * scale
    return (unit, scale, (unit * gain).astype(bf16))


def norm_back(grad_out, unit, scale, gain):
    grad_gain = jnp.sum(grad_out * unit, 0)
    grad_unit = grad_out * gain
    grad_in = scale * (grad_unit - unit * jnp.mean(grad_unit * unit, -1, keepdims=True))
    return (grad_in, grad_gain)


def adamw(master, first, second, grad, rate, decay):
    first_new = beta_one * first + (1.0 - beta_one) * grad
    second_new = beta_two * second + (1.0 - beta_two) * grad * grad
    first_hat = first_new / (1.0 - beta_one**STEP)
    second_hat = second_new / (1.0 - beta_two**STEP)
    master_new = master - rate * (first_hat / (jnp.sqrt(second_hat) + adam_eps) + decay * master)
    return (master_new, first_new, second_new)


def local(
    inputs,
    cotangent,
    segments,
    w_in,
    w_out,
    conv_w,
    w_gate,
    w_up,
    w_down,
    gains,
    m_in,
    m_out,
    m_conv,
    m_gate,
    m_up,
    m_down,
    m_gains,
    v_in,
    v_out,
    v_conv,
    v_gate,
    v_up,
    v_down,
    v_gains,
):
    seqs_here, stretch, width = inputs.shape
    rows = seqs_here * stretch
    n_dp = lax.axis_size("dp")
    n_seq = lax.axis_size("seq")
    n_z = n_dp // 2
    own = w_in.shape[0]
    own_ff = w_down.shape[0]
    ff_part = n_dp * own_ff
    dp = lax.axis_index("dp")
    sq = lax.axis_index("seq")
    z = dp // 2
    core = dp % 2
    first_core = core == 0

    lane = n_seq * own

    def halves(full):
        blocks = [full[:, i * lane : (i + 1) * lane] for i in range(2 * n_z)]
        even = jnp.concatenate(blocks[0::2], 1)
        odd = jnp.concatenate(blocks[1::2], 1)
        return jnp.where(first_core, even, odd), jnp.where(first_core, odd, even)

    def seq_ordered(pieces):
        stacked = jnp.stack(pieces, 0)
        return jnp.stack([pick(stacked, sq ^ j) for j in range(n_seq)], 0)

    def by_part(weight):
        low = weight.astype(bf16).reshape(own, n_dp, n_seq, own_ff)
        return low.transpose(2, 0, 1, 3).reshape(n_seq, own, ff_part)

    smalls = jnp.pad(
        jnp.concatenate([conv_w, gains], 0).astype(bf16), ((0, own - 5), (0, LANES - own))
    )
    mix = jnp.concatenate([w_in.astype(bf16), w_out.astype(bf16), smalls], 1)
    gate_up = jnp.concatenate([by_part(w_gate), by_part(w_up)], 2)

    residual_low = inputs.reshape(rows, width)
    edge_ids = jnp.pad(segments[:, -2:, None].astype(bf16), ((0, 0), (0, 0), (0, LANES - 1)))
    edge = from_behind(jnp.concatenate([inputs[:, -2:, :], edge_ids], 2), "seq", 1)
    z_parts = [along_z(mix, -k) for k in range(1, n_z)]
    gu_parts = [across_seq(pick(gate_up, sq ^ k), k) for k in range(1, n_seq)]
    low_down = w_down.astype(bf16)
    z_parts, gu_parts, edge, low_down = tie((z_parts, gu_parts, edge, low_down))
    gate_up = seq_ordered([pick(gate_up, sq)] + gu_parts)
    mat_gate_up = lax.all_gather(gate_up, "dp", axis=0).reshape(width, 2 * ff_part)
    mat_down = lax.all_gather(low_down, "dp", axis=0, tiled=True)

    columns = mix.shape[1]

    z_slots = (z + jnp.arange(n_z)) % n_z
    seq_slots = sq ^ jnp.arange(n_seq)
    core_slots = core ^ jnp.arange(2)
    order = list(range(n_seq))
    near = order[1:3] if n_seq == 4 else order[1:]
    last = order[-1]
    grad_top = cotangent.reshape(rows, width)
    z_order = place([part[None] for part in [mix] + z_parts], z_slots, columns // 3)[0]
    mix_parts = swap_near(z_order)
    mix_parts = tie(mix_parts)
    mix_parts.update(swap_far(mix_parts))
    mix_parts, top_out = tie((mix_parts, grad_top))
    mix_parts[0] = z_order
    mix_mine = place([mix_parts[k] for k in range(n_seq)], seq_slots, columns // 3)
    mix_mine = mix_mine.reshape(width // 2, columns)

    mix_other = to_sibling(mix_mine)
    tops = swap_near(top_out)
    tops.update(swap_far(tops))

    cut_in, cut_out = 3 * width, 4 * width
    in_mine, in_other = mix_mine[:, :cut_in], mix_other[:, :cut_in]
    out_mine, out_other = mix_mine[:, cut_in:cut_out], mix_other[:, cut_in:cut_out]

    half = width // 2
    feature = lax.broadcasted_iota(jnp.int32, (1, width), 1)
    lane_of = lax.broadcasted_iota(jnp.int32, (LANES, width), 0)
    spread = (lane_of == feature % own).astype(bf16)

    def row_blocks(which):
        row = lax.broadcasted_iota(jnp.int32, (half, 1), 0) // own
        return ((row // n_seq) * 2 + which) * n_seq + row % n_seq

    def small_rows(packed, which):
        wide = jnp.where(row_blocks(which) == feature // own, dot(packed, spread), 0.0)
        chosen = lax.broadcasted_iota(jnp.int32, (8, half), 1) % own
        chosen = chosen == lax.broadcasted_iota(jnp.int32, (8, half), 0)
        return dot(chosen.astype(bf16), wide.astype(bf16))

    small_all = small_rows(mix_mine[:, cut_out:], core) + small_rows(
        mix_other[:, cut_out:], 1 - core
    )
    taps, gain_vals = small_all[:3], small_all[3:5]

    residual = residual_low.astype(f32)
    unit_one, scale_one, norm_one = normed(residual, gain_vals[0])
    edge_rows = jnp.pad(edge[:, :, :width].reshape(2 * seqs_here, width), ((0, 12), (0, 0)))
    edge_norm = normed(edge_rows.astype(f32), gain_vals[0])[2]
    norm_mine, norm_other = halves(norm_one)
    edge_mine, edge_other = halves(edge_norm)
    projected = dot(jnp.concatenate([norm_mine, edge_mine], 0), in_mine) + dot(
        jnp.concatenate([norm_other, edge_other], 0), in_other
    )
    edge_rows = projected[rows : rows + 2 * seqs_here]
    prev_rows = (edge_rows[:, :width] * edge_rows[:, 2 * width :]).astype(bf16)
    prev_rows = prev_rows.reshape(seqs_here, 2, width)
    projected = projected[:rows]
    first_block = sq == 0
    prev_ids = jnp.where(first_block, -1, edge[:, :, width].astype(jnp.int32))
    b_gate = projected[:, :width]
    c_gate = projected[:, width : 2 * width]
    x_part = projected[:, 2 * width :]
    conv_in = (b_gate * x_part).astype(bf16).reshape(seqs_here, stretch, width)
    extended = jnp.concatenate([prev_rows, conv_in], 1).astype(f32)
    ext_ids = jnp.concatenate([prev_ids, segments], 1)
    near_one = (ext_ids[:, 1:-1] == segments).astype(f32)[..., None]
    near_two = (ext_ids[:, :-2] == segments).astype(f32)[..., None]
    tap_now = extended[:, 2:]
    tap_one = extended[:, 1:-1] * near_one
    tap_two = extended[:, :-2] * near_two
    conv_out = (taps[2] * tap_now + taps[1] * tap_one + taps[0] * tap_two).reshape(rows, width)
    mixed_in = (c_gate * conv_out).astype(bf16)
    mixed_mine, mixed_other = halves(mixed_in)
    middle = residual + dot(mixed_mine, out_mine) + dot(mixed_other, out_other)
    unit_two, scale_two, norm_two = normed(middle, gain_vals[1])

    both_halves = [mix_mine.reshape(n_z, -1, columns), mix_other.reshape(n_z, -1, columns)]
    in_full = place(both_halves, core_slots, width, 0, cut_in).reshape(width, cut_in)
    out_full = place(both_halves, core_slots, width, cut_in, width).reshape(width, width)

    norm_two, tops = tie((norm_two, tops))
    tops[0] = grad_top
    norms = swap_near(norm_two)
    hiddens, act_grads, norm_parts, out_parts = {}, {}, {}, {}

    def hidden_block(k):
        both = dot(norms[k], mat_gate_up)
        gate, up_part = both[:, :ff_part], both[:, ff_part:]
        sigma = jax.nn.sigmoid(gate)
        silu_vals = gate * sigma
        grad_hidden = right_contract(tops[k], mat_down)
        hiddens[k] = (silu_vals * up_part).astype(bf16)
        grad_gate_act = (grad_hidden * up_part * sigma * (1.0 + gate * (1.0 - sigma))).astype(bf16)
        grad_up_act = (grad_hidden * silu_vals).astype(bf16)
        act_grads[k] = jnp.concatenate([grad_gate_act, grad_up_act], 1)

    norms[0] = norm_two
    hidden_block(0)
    norm_parts[0] = right_contract(act_grads[0], mat_gate_up)
    out_parts[0] = dot(hiddens[0], mat_down)
    norms, hiddens, act_grads, norm_parts, out_parts, in_full, out_full = tie(
        (norms, hiddens, act_grads, norm_parts, out_parts, in_full, out_full)
    )
    norms.update(swap_far(norms))
    norm_sums = {}
    for k in order[1:]:
        hidden_block(k)
        norm_parts[k] = right_contract(act_grads[k], mat_gate_up).astype(bf16)
        norm_sums[k] = across_seq(norm_parts[k], k)
        if k != last:
            norms[k + 1], act_grads, norm_parts = tie((norms[k + 1], act_grads, norm_parts))
    early = {k: norm_sums[k] for k in order[1:-2]}
    norm_parts, hiddens, act_grads, early = tie((norm_parts, hiddens, act_grads, early))
    norm_sums.update(early)

    def rows_of(blocks):
        return jnp.concatenate([blocks[k] for k in order], 0)

    grad_down = left_contract(rows_of(hiddens), rows_of(tops)).astype(bf16)
    sum_down = lax.psum_scatter(grad_down, "dp", scatter_dimension=0, tiled=True).astype(f32)
    hiddens, act_grads, grad_down, norm_sums[order[-2]] = tie(
        (hiddens, act_grads, grad_down, norm_sums[order[-2]])
    )
    grad_gate_up = left_contract(rows_of(norms), rows_of(act_grads)).astype(bf16)
    gu_sum = lax.psum_scatter(grad_gate_up, "dp", scatter_dimension=0, tiled=True)
    out_far = dot(hiddens[last], mat_down).astype(bf16)
    norm_sums[last], grad_gate_up, out_far, hiddens = tie(
        (norm_sums[last], grad_gate_up, out_far, hiddens)
    )
    grad_norm_two = norm_parts[0]
    for k in order[1:]:
        grad_norm_two = grad_norm_two + norm_sums[k].astype(f32)

    back_two, gain_two = norm_back(grad_norm_two, unit_two, scale_two, gain_vals[1])
    grad_middle = grad_top.astype(f32) + back_two
    grad_branch = grad_middle.astype(bf16)
    grad_out_mine = left_contract(mixed_mine, grad_branch)
    grad_out_other = left_contract(mixed_other, grad_branch)
    grad_mixed = right_contract(grad_branch, out_full)
    grad_c = grad_mixed * conv_out
    grad_conv = (grad_mixed * c_gate).reshape(seqs_here, stretch, width)
    grad_taps = [
        jnp.sum(tap_two * grad_conv, (0, 1)),
        jnp.sum(tap_one * grad_conv, (0, 1)),
        jnp.sum(tap_now * grad_conv, (0, 1)),
    ]
    term_now = taps[2] * grad_conv
    term_one = taps[1] * grad_conv * near_one
    term_two = taps[0] * grad_conv * near_two
    grad_ext = (
        jnp.pad(term_now, ((0, 0), (2, 0), (0, 0)))
        + jnp.pad(term_one, ((0, 0), (1, 1), (0, 0)))
        + jnp.pad(term_two, ((0, 0), (0, 2), (0, 0)))
    )
    next_terms = from_behind(grad_ext[:, :2, :], "seq", -1)
    next_terms, out_far = tie((next_terms, out_far))
    out_relay = sum_far(out_far) if n_seq == 4 else ()
    grad_conv_in = (
        grad_ext[:, 2:, :] + jnp.pad(next_terms, ((0, 0), (stretch - 2, 0), (0, 0)))
    ).reshape(rows, width)
    grad_proj = jnp.concatenate([grad_conv_in * x_part, grad_c, grad_conv_in * b_gate], -1).astype(
        bf16
    )
    grad_in_mine = left_contract(norm_mine, grad_proj)
    grad_in_other = left_contract(norm_other, grad_proj)
    grad_norm_one = right_contract(grad_proj, in_full)
    back_one, gain_one = norm_back(grad_norm_one, unit_one, scale_one, gain_vals[0])
    input_grad = (grad_middle + back_one).reshape(seqs_here, stretch, width)

    def sum_core(mine, other):
        return mine + to_sibling(other.astype(bf16)).astype(f32)

    small_grads = jnp.stack(grad_taps + [gain_one, gain_two], 0)
    small_grads = (small_grads + to_sibling(small_grads)).astype(bf16)
    small_wide = jnp.tile(jnp.pad(small_grads, ((0, own - 5), (0, 0))), (half // own, 1))
    small_wide = jnp.where(row_blocks(core) == feature // own, small_wide, 0.0).astype(bf16)
    in_received = to_sibling(grad_in_other.astype(bf16))
    mixed = jnp.concatenate(
        [
            grad_in_mine + in_received.astype(f32),
            sum_core(grad_out_mine, grad_out_other),
            right_contract(small_wide, spread),
        ],
        1,
    ).astype(bf16)
    mixed, out_relay, hiddens = tie((mixed, out_relay, hiddens))
    mixed = mixed.reshape(n_z, n_seq, own, -1)

    def seq_block(index):
        return lax.dynamic_index_in_dim(mixed, index, 1, keepdims=False)

    gu_sum = gu_sum.reshape(n_seq, own, 2 * ff_part)
    gu_parts = [across_seq(pick(gu_sum, sq ^ k), k) for k in range(1, n_seq)]
    seq_terms = {k: seq_block(sq ^ k) for k in near}
    if n_seq == 4:
        seq_relay = tie(sum_far(seq_block(sq ^ last)))
        seq_terms = {k: term.astype(f32) for k, term in seq_terms.items()}
        seq_terms = {k: term.astype(bf16) for k, term in add_far(seq_terms, seq_relay).items()}
    seq_parts = [across_seq(seq_terms[k], k) for k in near]
    out_low = add_far({k: dot(hiddens[k], mat_down) for k in near}, out_relay)
    out_low = {k: term.astype(bf16) for k, term in out_low.items()}
    seq_parts, gu_parts, out_low, sum_down = tie((seq_parts, gu_parts, out_low, sum_down))
    total = seq_block(sq).astype(f32)
    for part in seq_parts:
        total = total + part.astype(f32)
    low = total.astype(bf16)
    low, gu_parts = tie((low, gu_parts))
    z_sums = [along_z(pick(low, (z + k) % n_z), k) for k in range(1, n_z)]
    out_sums = {k: across_seq(out_low[k], k) for k in near}
    gu_sum = seq_ordered([pick(gu_sum, sq)] + gu_parts).astype(f32)

    def by_row(part):
        return (
            part.reshape(n_seq, own, n_dp, own_ff)
            .transpose(1, 2, 0, 3)
            .reshape(own, n_seq * ff_part)
        )

    def matrix_step(master, first, second, grad):
        return adamw(master, first, second, grad, learn_rate, weight_decay)

    step_gate = matrix_step(w_gate, m_gate, v_gate, by_row(gu_sum[:, :, :ff_part]))
    step_up = matrix_step(w_up, m_up, v_up, by_row(gu_sum[:, :, ff_part:]))
    step_down = matrix_step(w_down, m_down, v_down, sum_down)
    z_sums, step_gate, step_up, step_down = tie((z_sums, step_gate, step_up, step_down))
    total = pick(total, z)
    for part in z_sums:
        total = total + part.astype(f32)
    sum_in, sum_out, small_sum = total[:, :cut_in], total[:, cut_in:cut_out], total[:, cut_out:]

    output = middle + out_parts[0]
    for k in near:
        output = output + out_sums[k].astype(f32)
    output = output.astype(bf16)

    step_in = matrix_step(w_in, m_in, v_in, sum_in)
    step_out = matrix_step(w_out, m_out, v_out, sum_out)
    step_conv = adamw(conv_w, m_conv, v_conv, small_sum[:3, :own], small_rate, 0.0)
    step_gains = adamw(gains, m_gains, v_gains, small_sum[3:5, :own], small_rate, 0.0)
    updated = [step_in, step_out, step_conv, step_gate, step_up, step_down, step_gains]
    new_w = [item[0] for item in updated]
    new_m = [item[1] for item in updated]
    new_v = [item[2] for item in updated]
    return (
        output.reshape(seqs_here, stretch, width),
        input_grad,
        *new_w,
        *new_m,
        *new_v,
    )


def solution(mesh):
    tokens = P("dp", "seq", None)
    matrix = P(("dp", "seq"), None)
    vector = P(None, ("dp", "seq"))
    weights = (matrix, matrix, vector, matrix, matrix, matrix, vector)
    return jax.shard_map(
        local,
        mesh=mesh,
        in_specs=(tokens, tokens, P("dp", "seq")) + weights * 3,
        out_specs=(tokens, tokens) + weights * 3,
        check_vma=False,
    )
```

```python
import jax
import jax.numpy as jnp
from jax import lax
from jax.experimental import pallas as pl
from jax.experimental.pallas import tpu as pltpu
from jax.sharding import PartitionSpec as P

STEP = 10


norm_eps = 1e-05
learn_rate = 0.02
small_rate = 1.0
beta_one = 0.9
beta_two = 0.95
adam_eps = 1e-08
weight_decay = 0.1
LANES = 128
bf16 = jnp.bfloat16
f32 = jnp.float32


def from_behind(shard, axis, by):
    peers = lax.axis_size(axis)
    pairs = [(i, i + by) for i in range(peers) if 0 <= i + by < peers]
    return lax.ppermute(shard, axis, pairs)


def to_sibling(block):
    return lax.ppermute(block, "dp", [(i, i ^ 1) for i in range(lax.axis_size("dp"))])


def along_z(block, by):
    count = lax.axis_size("dp")
    return lax.ppermute(block, "dp", [(i, (i + 2 * by) % count) for i in range(count)])


def across_seq(block, by):
    return lax.ppermute(block, "seq", [(i, i ^ by) for i in range(lax.axis_size("seq"))])


def swap_near(block):
    count = lax.axis_size("seq")
    near = (1, 2) if count == 4 else range(1, count)
    return {k: across_seq(block, k) for k in near}


def swap_far(near):
    if lax.axis_size("seq") != 4:
        return {}
    half = near[1].shape[0] // 2
    first, second = across_seq(near[1][:half], 2), across_seq(near[2][half:], 1)
    return {3: jnp.concatenate([first, second], 0)}


def sum_far(block):
    half = block.shape[0] // 2
    return across_seq(block[:half], 1), across_seq(block[half:], 2)


def add_far(terms, received):
    if not received:
        return terms
    first, second = received
    half = first.shape[0]
    terms = dict(terms)
    terms[2] = jnp.concatenate([terms[2][:half] + first.astype(f32), terms[2][half:]], 0)
    terms[1] = jnp.concatenate([terms[1][:half], terms[1][half:] + second.astype(f32)], 0)
    return terms


def dot(first, second):
    return jnp.dot(first, second, preferred_element_type=f32)


def left_contract(first, second):
    return lax.dot_general(first, second, (((0,), (0,)), ((), ())), preferred_element_type=f32)


def right_contract(first, second):
    return lax.dot_general(first, second, (((1,), (1,)), ((), ())), preferred_element_type=f32)


def tie(values):
    return lax.optimization_barrier(values)


def pick(stacked, index):
    return lax.dynamic_index_in_dim(stacked, index, 0, keepdims=False)


def place(blocks, slots, chunk, first=0, columns=None):
    outer, depth, width = blocks[0].shape
    columns = width if columns is None else columns
    count = len(blocks)

    def kernel(slots_ref, *refs):
        for k in range(count):
            refs[-1][:, slots_ref[k]] = refs[k][...]

    size = 4 * count * outer * depth * columns
    return pl.pallas_call(
        kernel,
        grid=(columns // chunk,),
        out_shape=jax.ShapeDtypeStruct((outer, count, depth, columns), blocks[0].dtype),
        in_specs=[pl.BlockSpec(memory_space=pltpu.SMEM)]
        + [pl.BlockSpec((outer, depth, chunk), lambda j: (0, 0, j + first // chunk))] * count,
        out_specs=pl.BlockSpec((outer, count, depth, chunk), lambda j: (0, 0, 0, j)),
        compiler_params=pltpu.CompilerParams(vmem_limit_bytes=32 * 2**20),
        cost_estimate=pl.CostEstimate(flops=0, bytes_accessed=size, transcendentals=0),
    )(slots.astype(jnp.int32), *blocks)


def normed(values, gain):
    scale = lax.rsqrt(jnp.mean(values * values, -1, keepdims=True) + norm_eps)
    unit = values * scale
    return (unit, scale, (unit * gain).astype(bf16))


def norm_back(grad_out, unit, scale, gain):
    grad_gain = jnp.sum(grad_out * unit, 0)
    grad_unit = grad_out * gain
    grad_in = scale * (grad_unit - unit * jnp.mean(grad_unit * unit, -1, keepdims=True))
    return (grad_in, grad_gain)


def adamw(master, first, second, grad, rate, decay):
    first_new = beta_one * first + (1.0 - beta_one) * grad
    second_new = beta_two * second + (1.0 - beta_two) * grad * grad
    first_hat = first_new / (1.0 - beta_one**STEP)
    second_hat = second_new / (1.0 - beta_two**STEP)
    master_new = master - rate * (first_hat / (jnp.sqrt(second_hat) + adam_eps) + decay * master)
    return (master_new, first_new, second_new)


def local(
    inputs,
    cotangent,
    segments,
    w_in,
    w_out,
    conv_w,
    w_gate,
    w_up,
    w_down,
    gains,
    m_in,
    m_out,
    m_conv,
    m_gate,
    m_up,
    m_down,
    m_gains,
    v_in,
    v_out,
    v_conv,
    v_gate,
    v_up,
    v_down,
    v_gains,
):
    seqs_here, stretch, width = inputs.shape
    rows = seqs_here * stretch
    n_dp = lax.axis_size("dp")
    n_seq = lax.axis_size("seq")
    n_z = n_dp // 2
    own = w_in.shape[0]
    own_ff = w_down.shape[0]
    ff_part = n_dp * own_ff
    dp = lax.axis_index("dp")
    sq = lax.axis_index("seq")
    z = dp // 2
    core = dp % 2
    first_core = core == 0

    lane = n_seq * own

    def halves(full):
        blocks = [full[:, i * lane : (i + 1) * lane] for i in range(2 * n_z)]
        even = jnp.concatenate(blocks[0::2], 1)
        odd = jnp.concatenate(blocks[1::2], 1)
        return jnp.where(first_core, even, odd), jnp.where(first_core, odd, even)

    def seq_ordered(pieces):
        stacked = jnp.stack(pieces, 0)
        return jnp.stack([pick(stacked, sq ^ j) for j in range(n_seq)], 0)

    def by_part(weight):
        low = weight.astype(bf16).reshape(own, n_dp, n_seq, own_ff)
        return low.transpose(2, 0, 1, 3).reshape(n_seq, own, ff_part)

    smalls = jnp.pad(
        jnp.concatenate([conv_w, gains], 0).astype(bf16), ((0, own - 5), (0, LANES - own))
    )
    mix = jnp.concatenate([w_in.astype(bf16), w_out.astype(bf16), smalls], 1)
    gate_up = jnp.concatenate([by_part(w_gate), by_part(w_up)], 2)

    residual_low = inputs.reshape(rows, width)
    edge_ids = jnp.pad(segments[:, -2:, None].astype(bf16), ((0, 0), (0, 0), (0, LANES - 1)))
    edge = from_behind(jnp.concatenate([inputs[:, -2:, :], edge_ids], 2), "seq", 1)
    z_parts = [along_z(mix, -k) for k in range(1, n_z)]
    gu_parts = [across_seq(pick(gate_up, sq ^ k), k) for k in range(1, n_seq)]
    low_down = w_down.astype(bf16)
    z_parts, gu_parts, edge, low_down = tie((z_parts, gu_parts, edge, low_down))
    gate_up = seq_ordered([pick(gate_up, sq)] + gu_parts)
    mat_gate_up = lax.all_gather(gate_up, "dp", axis=0).reshape(width, 2 * ff_part)
    mat_down = lax.all_gather(low_down, "dp", axis=0, tiled=True)

    columns = mix.shape[1]

    z_slots = (z + jnp.arange(n_z)) % n_z
    seq_slots = sq ^ jnp.arange(n_seq)
    core_slots = core ^ jnp.arange(2)
    order = list(range(n_seq))
    near = order[1:3] if n_seq == 4 else order[1:]
    last = order[-1]
    grad_top = cotangent.reshape(rows, width)
    z_order = place([part[None] for part in [mix] + z_parts], z_slots, columns // 3)[0]
    mix_parts = swap_near(z_order)
    mix_parts = tie(mix_parts)
    mix_parts.update(swap_far(mix_parts))
    mix_parts, top_out = tie((mix_parts, grad_top))
    mix_parts[0] = z_order
    mix_mine = place([mix_parts[k] for k in range(n_seq)], seq_slots, columns // 3)
    mix_mine = mix_mine.reshape(width // 2, columns)

    mix_other = to_sibling(mix_mine)
    tops = swap_near(top_out)

    cut_in, cut_out = 3 * width, 4 * width
    in_mine, in_other = mix_mine[:, :cut_in], mix_other[:, :cut_in]
    out_mine, out_other = mix_mine[:, cut_in:cut_out], mix_other[:, cut_in:cut_out]

    half = width // 2
    feature = lax.broadcasted_iota(jnp.int32, (1, width), 1)
    lane_of = lax.broadcasted_iota(jnp.int32, (LANES, width), 0)
    spread = (lane_of == feature % own).astype(bf16)

    def row_blocks(which):
        row = lax.broadcasted_iota(jnp.int32, (half, 1), 0) // own
        return ((row // n_seq) * 2 + which) * n_seq + row % n_seq

    def small_rows(packed, which):
        wide = jnp.where(row_blocks(which) == feature // own, dot(packed, spread), 0.0)
        chosen = lax.broadcasted_iota(jnp.int32, (8, half), 1) % own
        chosen = chosen == lax.broadcasted_iota(jnp.int32, (8, half), 0)
        return dot(chosen.astype(bf16), wide.astype(bf16))

    small_all = small_rows(mix_mine[:, cut_out:], core) + small_rows(
        mix_other[:, cut_out:], 1 - core
    )
    taps, gain_vals = small_all[:3], small_all[3:5]

    residual = residual_low.astype(f32)
    unit_one, scale_one, norm_one = normed(residual, gain_vals[0])
    edge_rows = jnp.pad(edge[:, :, :width].reshape(2 * seqs_here, width), ((0, 12), (0, 0)))
    edge_norm = normed(edge_rows.astype(f32), gain_vals[0])[2]
    norm_mine, norm_other = halves(norm_one)
    edge_mine, edge_other = halves(edge_norm)
    projected = dot(jnp.concatenate([norm_mine, edge_mine], 0), in_mine) + dot(
        jnp.concatenate([norm_other, edge_other], 0), in_other
    )
    edge_rows = projected[rows : rows + 2 * seqs_here]
    prev_rows = (edge_rows[:, :width] * edge_rows[:, 2 * width :]).astype(bf16)
    prev_rows = prev_rows.reshape(seqs_here, 2, width)
    projected = projected[:rows]
    first_block = sq == 0
    prev_ids = jnp.where(first_block, -1, edge[:, :, width].astype(jnp.int32))
    b_gate = projected[:, :width]
    c_gate = projected[:, width : 2 * width]
    x_part = projected[:, 2 * width :]
    conv_in = (b_gate * x_part).astype(bf16).reshape(seqs_here, stretch, width)
    extended = jnp.concatenate([prev_rows, conv_in], 1).astype(f32)
    ext_ids = jnp.concatenate([prev_ids, segments], 1)
    near_one = (ext_ids[:, 1:-1] == segments).astype(f32)[..., None]
    near_two = (ext_ids[:, :-2] == segments).astype(f32)[..., None]
    tap_now = extended[:, 2:]
    tap_one = extended[:, 1:-1] * near_one
    tap_two = extended[:, :-2] * near_two
    conv_out = (taps[2] * tap_now + taps[1] * tap_one + taps[0] * tap_two).reshape(rows, width)
    mixed_in = (c_gate * conv_out).astype(bf16)
    mixed_in, tops = tie((mixed_in, tops))
    tops.update(swap_far(tops))
    mixed_mine, mixed_other = halves(mixed_in)
    middle = residual + dot(mixed_mine, out_mine) + dot(mixed_other, out_other)
    unit_two, scale_two, norm_two = normed(middle, gain_vals[1])

    both_halves = [mix_mine.reshape(n_z, -1, columns), mix_other.reshape(n_z, -1, columns)]
    in_full = place(both_halves, core_slots, width, 0, cut_in).reshape(width, cut_in)
    out_full = place(both_halves, core_slots, width, cut_in, width).reshape(width, width)

    norm_two, tops = tie((norm_two, tops))
    tops[0] = grad_top
    norms = swap_near(norm_two)
    hiddens, act_grads, norm_parts, out_parts = {}, {}, {}, {}

    def hidden_block(k):
        both = dot(norms[k], mat_gate_up)
        gate, up_part = both[:, :ff_part], both[:, ff_part:]
        sigma = jax.nn.sigmoid(gate)
        silu_vals = gate * sigma
        grad_hidden = right_contract(tops[k], mat_down)
        hiddens[k] = (silu_vals * up_part).astype(bf16)
        grad_gate_act = (grad_hidden * up_part * sigma * (1.0 + gate * (1.0 - sigma))).astype(bf16)
        grad_up_act = (grad_hidden * silu_vals).astype(bf16)
        act_grads[k] = jnp.concatenate([grad_gate_act, grad_up_act], 1)

    norms[0] = norm_two
    hidden_block(0)
    norm_parts[0] = right_contract(act_grads[0], mat_gate_up)
    out_parts[0] = dot(hiddens[0], mat_down)
    norms, hiddens, act_grads, norm_parts, out_parts, in_full, out_full = tie(
        (norms, hiddens, act_grads, norm_parts, out_parts, in_full, out_full)
    )
    norms.update(swap_far(norms))
    norm_sums = {}
    for k in order[1:-1]:
        hidden_block(k)
        norm_parts[k] = right_contract(act_grads[k], mat_gate_up).astype(bf16)
        norm_sums[k] = across_seq(norm_parts[k], k)
        norms, act_grads, norm_parts = tie((norms, act_grads, norm_parts))
    hidden_block(last)
    last_parts = [
        right_contract(act_grads[last][start : start + rows // 2], mat_gate_up).astype(bf16)
        for start in (0, rows // 2)
    ]
    last_sums = [across_seq(part, last) for part in last_parts]
    early = {k: norm_sums[k] for k in order[1:-2]}
    out_far = dot(hiddens[last], mat_down).astype(bf16)
    last_parts, hiddens, act_grads, early, out_far = tie(
        (last_parts, hiddens, act_grads, early, out_far)
    )
    norm_sums.update(early)

    def rows_of(blocks):
        return jnp.concatenate([blocks[k] for k in order], 0)

    grad_down = left_contract(rows_of(hiddens), rows_of(tops)).astype(bf16)
    hiddens, act_grads, grad_down, norm_sums[order[-2]], last_sums[0] = tie(
        (hiddens, act_grads, grad_down, norm_sums[order[-2]], last_sums[0])
    )
    grad_gate_up = left_contract(rows_of(norms), rows_of(act_grads)).astype(bf16)
    gu_sum = lax.psum_scatter(grad_gate_up, "dp", scatter_dimension=0, tiled=True)
    grad_down, grad_gate_up = tie((grad_down, grad_gate_up))
    sum_down = lax.psum_scatter(grad_down, "dp", scatter_dimension=0, tiled=True)
    last_sums, grad_gate_up, hiddens = tie((last_sums, grad_gate_up, hiddens))
    norm_sums[last] = jnp.concatenate(last_sums, 0)
    grad_norm_two = norm_parts[0]
    for k in order[1:]:
        grad_norm_two = grad_norm_two + norm_sums[k].astype(f32)

    back_two, gain_two = norm_back(grad_norm_two, unit_two, scale_two, gain_vals[1])
    grad_middle = grad_top.astype(f32) + back_two
    grad_branch = grad_middle.astype(bf16)
    grad_out_mine = left_contract(mixed_mine, grad_branch)
    grad_out_other = left_contract(mixed_other, grad_branch)
    grad_mixed = right_contract(grad_branch, out_full)
    grad_c = grad_mixed * conv_out
    grad_conv = (grad_mixed * c_gate).reshape(seqs_here, stretch, width)
    grad_taps = [
        jnp.sum(tap_two * grad_conv, (0, 1)),
        jnp.sum(tap_one * grad_conv, (0, 1)),
        jnp.sum(tap_now * grad_conv, (0, 1)),
    ]
    term_now = taps[2] * grad_conv
    term_one = taps[1] * grad_conv * near_one
    term_two = taps[0] * grad_conv * near_two
    grad_ext = (
        jnp.pad(term_now, ((0, 0), (2, 0), (0, 0)))
        + jnp.pad(term_one, ((0, 0), (1, 1), (0, 0)))
        + jnp.pad(term_two, ((0, 0), (0, 2), (0, 0)))
    )
    next_terms = from_behind(grad_ext[:, :2, :], "seq", -1)
    next_terms, out_far = tie((next_terms, out_far))
    out_relay = sum_far(out_far) if n_seq == 4 else ()
    grad_conv_in = (
        grad_ext[:, 2:, :] + jnp.pad(next_terms, ((0, 0), (stretch - 2, 0), (0, 0)))
    ).reshape(rows, width)
    grad_proj = jnp.concatenate([grad_conv_in * x_part, grad_c, grad_conv_in * b_gate], -1).astype(
        bf16
    )
    grad_in_mine = left_contract(norm_mine, grad_proj)
    grad_in_other = left_contract(norm_other, grad_proj)
    grad_norm_one = right_contract(grad_proj, in_full)
    back_one, gain_one = norm_back(grad_norm_one, unit_one, scale_one, gain_vals[0])
    input_grad = (grad_middle + back_one).reshape(seqs_here, stretch, width)

    def sum_core(mine, other):
        return mine + to_sibling(other.astype(bf16)).astype(f32)

    small_grads = jnp.stack(grad_taps + [gain_one, gain_two], 0)
    small_grads = (small_grads + to_sibling(small_grads)).astype(bf16)
    small_wide = jnp.tile(jnp.pad(small_grads, ((0, own - 5), (0, 0))), (half // own, 1))
    small_wide = jnp.where(row_blocks(core) == feature // own, small_wide, 0.0).astype(bf16)
    in_received = to_sibling(grad_in_other.astype(bf16))
    mixed = jnp.concatenate(
        [
            grad_in_mine + in_received.astype(f32),
            sum_core(grad_out_mine, grad_out_other),
            right_contract(small_wide, spread),
        ],
        1,
    ).astype(bf16)
    gu_sum = gu_sum.reshape(n_seq, own, 2 * ff_part)
    gu_parts = [across_seq(pick(gu_sum, sq ^ k), k) for k in range(1, n_seq)]
    mixed, out_relay = tie((mixed, out_relay))
    mixed = mixed.reshape(n_z, n_seq, own, -1)

    def seq_block(index):
        return lax.dynamic_index_in_dim(mixed, index, 1, keepdims=False)

    seq_terms = {k: seq_block(sq ^ k) for k in near}
    if n_seq == 4:
        seq_relay = sum_far(seq_block(sq ^ last))
        seq_relay, gu_parts, hiddens = tie((seq_relay, gu_parts, hiddens))
        seq_terms = {k: term.astype(f32) for k, term in seq_terms.items()}
        seq_terms = {k: term.astype(bf16) for k, term in add_far(seq_terms, seq_relay).items()}
    seq_parts = [across_seq(seq_terms[k], k) for k in near]
    out_low = add_far({k: dot(hiddens[k], mat_down) for k in near}, out_relay)
    out_low = {k: term.astype(bf16) for k, term in out_low.items()}
    gu_sum = seq_ordered([pick(gu_sum, sq)] + gu_parts).astype(f32)

    def by_row(part):
        return (
            part.reshape(n_seq, own, n_dp, own_ff)
            .transpose(1, 2, 0, 3)
            .reshape(own, n_seq * ff_part)
        )

    def matrix_step(master, first, second, grad):
        return adamw(master, first, second, grad, learn_rate, weight_decay)

    step_gate = matrix_step(w_gate, m_gate, v_gate, by_row(gu_sum[:, :, :ff_part]))
    step_up = matrix_step(w_up, m_up, v_up, by_row(gu_sum[:, :, ff_part:]))
    seq_parts, out_low, step_gate, step_up = tie((seq_parts, out_low, step_gate, step_up))
    total = seq_block(sq).astype(f32)
    for part in seq_parts:
        total = total + part.astype(f32)
    low = total.astype(bf16)
    low, sum_down = tie((low, sum_down))
    z_sums = [along_z(pick(low, (z + k) % n_z), k) for k in range(1, n_z)]
    out_sums = {k: across_seq(out_low[k], k) for k in near}
    total = pick(total, z)
    for part in z_sums:
        total = total + part.astype(f32)
    sum_in, sum_out, small_sum = total[:, :cut_in], total[:, cut_in:cut_out], total[:, cut_out:]

    output = middle + out_parts[0]
    for k in near:
        output = output + out_sums[k].astype(f32)
    output = output.astype(bf16)

    step_down = matrix_step(w_down, m_down, v_down, sum_down.astype(f32))
    step_in = matrix_step(w_in, m_in, v_in, sum_in)
    step_out = matrix_step(w_out, m_out, v_out, sum_out)
    step_conv = adamw(conv_w, m_conv, v_conv, small_sum[:3, :own], small_rate, 0.0)
    step_gains = adamw(gains, m_gains, v_gains, small_sum[3:5, :own], small_rate, 0.0)
    updated = [step_in, step_out, step_conv, step_gate, step_up, step_down, step_gains]
    new_w = [item[0] for item in updated]
    new_m = [item[1] for item in updated]
    new_v = [item[2] for item in updated]
    return (
        output.reshape(seqs_here, stretch, width),
        input_grad,
        *new_w,
        *new_m,
        *new_v,
    )


def solution(mesh):
    tokens = P("dp", "seq", None)
    matrix = P(("dp", "seq"), None)
    vector = P(None, ("dp", "seq"))
    weights = (matrix, matrix, vector, matrix, matrix, matrix, vector)
    return jax.shard_map(
        local,
        mesh=mesh,
        in_specs=(tokens, tokens, P("dp", "seq")) + weights * 3,
        out_specs=(tokens, tokens) + weights * 3,
        check_vma=False,
    )
```

```python
import jax
import jax.numpy as jnp
from jax import lax
from jax.experimental import pallas as pl
from jax.experimental.pallas import tpu as pltpu
from jax.sharding import PartitionSpec as P

STEP = 10


norm_eps = 1e-05
learn_rate = 0.02
small_rate = 1.0
beta_one = 0.9
beta_two = 0.95
adam_eps = 1e-08
weight_decay = 0.1
LANES = 128
bf16 = jnp.bfloat16
f32 = jnp.float32


def from_behind(shard, axis, by):
    peers = lax.axis_size(axis)
    pairs = [(i, i + by) for i in range(peers) if 0 <= i + by < peers]
    return lax.ppermute(shard, axis, pairs)


def to_sibling(block):
    return lax.ppermute(block, "dp", [(i, i ^ 1) for i in range(lax.axis_size("dp"))])


def along_z(block, by):
    count = lax.axis_size("dp")
    return lax.ppermute(block, "dp", [(i, (i + 2 * by) % count) for i in range(count)])


def across_seq(block, by):
    return lax.ppermute(block, "seq", [(i, i ^ by) for i in range(lax.axis_size("seq"))])


def swap_near(block):
    count = lax.axis_size("seq")
    near = (1, 2) if count == 4 else range(1, count)
    return {k: across_seq(block, k) for k in near}


def swap_far(near):
    if lax.axis_size("seq") != 4:
        return {}
    half = near[1].shape[0] // 2
    first, second = across_seq(near[1][:half], 2), across_seq(near[2][half:], 1)
    return {3: jnp.concatenate([first, second], 0)}


def sum_far(block):
    half = block.shape[0] // 2
    return across_seq(block[:half], 1), across_seq(block[half:], 2)


def add_far(terms, received):
    if not received:
        return terms
    first, second = received
    half = first.shape[0]
    terms = dict(terms)
    terms[2] = jnp.concatenate([terms[2][:half] + first.astype(f32), terms[2][half:]], 0)
    terms[1] = jnp.concatenate([terms[1][:half], terms[1][half:] + second.astype(f32)], 0)
    return terms


def dot(first, second):
    return jnp.dot(first, second, preferred_element_type=f32)


def left_contract(first, second):
    return lax.dot_general(first, second, (((0,), (0,)), ((), ())), preferred_element_type=f32)


def right_contract(first, second):
    return lax.dot_general(first, second, (((1,), (1,)), ((), ())), preferred_element_type=f32)


def tie(values):
    return lax.optimization_barrier(values)


def pick(stacked, index):
    return lax.dynamic_index_in_dim(stacked, index, 0, keepdims=False)


def place(blocks, slots, chunk, first=0, columns=None):
    outer, depth, width = blocks[0].shape
    columns = width if columns is None else columns
    count = len(blocks)

    def kernel(slots_ref, *refs):
        for k in range(count):
            refs[-1][:, slots_ref[k]] = refs[k][...]

    size = 4 * count * outer * depth * columns
    return pl.pallas_call(
        kernel,
        grid=(columns // chunk,),
        out_shape=jax.ShapeDtypeStruct((outer, count, depth, columns), blocks[0].dtype),
        in_specs=[pl.BlockSpec(memory_space=pltpu.SMEM)]
        + [pl.BlockSpec((outer, depth, chunk), lambda j: (0, 0, j + first // chunk))] * count,
        out_specs=pl.BlockSpec((outer, count, depth, chunk), lambda j: (0, 0, 0, j)),
        compiler_params=pltpu.CompilerParams(vmem_limit_bytes=32 * 2**20),
        cost_estimate=pl.CostEstimate(flops=0, bytes_accessed=size, transcendentals=0),
    )(slots.astype(jnp.int32), *blocks)


def normed(values, gain):
    scale = lax.rsqrt(jnp.mean(values * values, -1, keepdims=True) + norm_eps)
    unit = values * scale
    return (unit, scale, (unit * gain).astype(bf16))


def norm_back(grad_out, unit, scale, gain):
    grad_gain = jnp.sum(grad_out * unit, 0)
    grad_unit = grad_out * gain
    grad_in = scale * (grad_unit - unit * jnp.mean(grad_unit * unit, -1, keepdims=True))
    return (grad_in, grad_gain)


def adamw(master, first, second, grad, rate, decay):
    first_new = beta_one * first + (1.0 - beta_one) * grad
    second_new = beta_two * second + (1.0 - beta_two) * grad * grad
    first_hat = first_new / (1.0 - beta_one**STEP)
    second_hat = second_new / (1.0 - beta_two**STEP)
    master_new = master - rate * (first_hat / (jnp.sqrt(second_hat) + adam_eps) + decay * master)
    return (master_new, first_new, second_new)


def local(
    inputs,
    cotangent,
    segments,
    w_in,
    w_out,
    conv_w,
    w_gate,
    w_up,
    w_down,
    gains,
    m_in,
    m_out,
    m_conv,
    m_gate,
    m_up,
    m_down,
    m_gains,
    v_in,
    v_out,
    v_conv,
    v_gate,
    v_up,
    v_down,
    v_gains,
):
    seqs_here, stretch, width = inputs.shape
    rows = seqs_here * stretch
    n_dp = lax.axis_size("dp")
    n_seq = lax.axis_size("seq")
    n_z = n_dp // 2
    own = w_in.shape[0]
    own_ff = w_down.shape[0]
    ff_part = n_dp * own_ff
    dp = lax.axis_index("dp")
    sq = lax.axis_index("seq")
    z = dp // 2
    core = dp % 2
    first_core = core == 0

    lane = n_seq * own

    def halves(full):
        blocks = [full[:, i * lane : (i + 1) * lane] for i in range(2 * n_z)]
        even = jnp.concatenate(blocks[0::2], 1)
        odd = jnp.concatenate(blocks[1::2], 1)
        return jnp.where(first_core, even, odd), jnp.where(first_core, odd, even)

    def seq_ordered(pieces):
        stacked = jnp.stack(pieces, 0)
        return jnp.stack([pick(stacked, sq ^ j) for j in range(n_seq)], 0)

    def by_part(weight):
        low = weight.astype(bf16).reshape(own, n_dp, n_seq, own_ff)
        return low.transpose(2, 0, 1, 3).reshape(n_seq, own, ff_part)

    smalls = jnp.pad(
        jnp.concatenate([conv_w, gains], 0).astype(bf16), ((0, own - 5), (0, LANES - own))
    )
    mix = jnp.concatenate([w_in.astype(bf16), w_out.astype(bf16), smalls], 1)
    gate_up = jnp.concatenate([by_part(w_gate), by_part(w_up)], 2)

    residual_low = inputs.reshape(rows, width)
    edge_ids = jnp.pad(segments[:, -2:, None].astype(bf16), ((0, 0), (0, 0), (0, LANES - 1)))
    edge = from_behind(jnp.concatenate([inputs[:, -2:, :], edge_ids], 2), "seq", 1)
    z_parts = [along_z(mix, -k) for k in range(1, n_z)]
    gu_parts = [across_seq(pick(gate_up, sq ^ k), k) for k in range(1, n_seq)]
    low_down = w_down.astype(bf16)
    z_parts, gu_parts, edge, low_down = tie((z_parts, gu_parts, edge, low_down))
    gate_up = seq_ordered([pick(gate_up, sq)] + gu_parts)
    mat_gate_up = lax.all_gather(gate_up, "dp", axis=0).reshape(width, 2 * ff_part)
    mat_down = lax.all_gather(low_down, "dp", axis=0, tiled=True)

    columns = mix.shape[1]

    z_slots = (z + jnp.arange(n_z)) % n_z
    seq_slots = sq ^ jnp.arange(n_seq)
    core_slots = core ^ jnp.arange(2)
    order = list(range(n_seq))
    near = order[1:3] if n_seq == 4 else order[1:]
    last = order[-1]
    grad_top = cotangent.reshape(rows, width)
    z_order = place([part[None] for part in [mix] + z_parts], z_slots, columns // 3)[0]
    mix_parts = swap_near(z_order)
    mix_parts = tie(mix_parts)
    mix_parts.update(swap_far(mix_parts))
    mix_parts, top_out = tie((mix_parts, grad_top))
    mix_parts[0] = z_order
    mix_mine = place([mix_parts[k] for k in range(n_seq)], seq_slots, columns // 3)
    mix_mine = mix_mine.reshape(width // 2, columns)

    mix_other = to_sibling(mix_mine)
    tops = swap_near(top_out)

    cut_in, cut_out = 3 * width, 4 * width
    in_mine, in_other = mix_mine[:, :cut_in], mix_other[:, :cut_in]
    out_mine, out_other = mix_mine[:, cut_in:cut_out], mix_other[:, cut_in:cut_out]

    half = width // 2
    feature = lax.broadcasted_iota(jnp.int32, (1, width), 1)
    lane_of = lax.broadcasted_iota(jnp.int32, (LANES, width), 0)
    spread = (lane_of == feature % own).astype(bf16)

    def row_blocks(which):
        row = lax.broadcasted_iota(jnp.int32, (half, 1), 0) // own
        return ((row // n_seq) * 2 + which) * n_seq + row % n_seq

    def small_rows(packed, which):
        wide = jnp.where(row_blocks(which) == feature // own, dot(packed, spread), 0.0)
        chosen = lax.broadcasted_iota(jnp.int32, (8, half), 1) % own
        chosen = chosen == lax.broadcasted_iota(jnp.int32, (8, half), 0)
        return dot(chosen.astype(bf16), wide.astype(bf16))

    small_all = small_rows(mix_mine[:, cut_out:], core) + small_rows(
        mix_other[:, cut_out:], 1 - core
    )
    taps, gain_vals = small_all[:3], small_all[3:5]

    residual = residual_low.astype(f32)
    unit_one, scale_one, norm_one = normed(residual, gain_vals[0])
    edge_rows = jnp.pad(edge[:, :, :width].reshape(2 * seqs_here, width), ((0, 12), (0, 0)))
    edge_norm = normed(edge_rows.astype(f32), gain_vals[0])[2]
    norm_mine, norm_other = halves(norm_one)
    edge_mine, edge_other = halves(edge_norm)
    projected = dot(jnp.concatenate([norm_mine, edge_mine], 0), in_mine) + dot(
        jnp.concatenate([norm_other, edge_other], 0), in_other
    )
    edge_rows = projected[rows : rows + 2 * seqs_here]
    prev_rows = (edge_rows[:, :width] * edge_rows[:, 2 * width :]).astype(bf16)
    prev_rows = prev_rows.reshape(seqs_here, 2, width)
    projected = projected[:rows]
    first_block = sq == 0
    prev_ids = jnp.where(first_block, -1, edge[:, :, width].astype(jnp.int32))
    b_gate = projected[:, :width]
    c_gate = projected[:, width : 2 * width]
    x_part = projected[:, 2 * width :]
    conv_in = (b_gate * x_part).astype(bf16).reshape(seqs_here, stretch, width)
    extended = jnp.concatenate([prev_rows, conv_in], 1).astype(f32)
    ext_ids = jnp.concatenate([prev_ids, segments], 1)
    near_one = (ext_ids[:, 1:-1] == segments).astype(f32)[..., None]
    near_two = (ext_ids[:, :-2] == segments).astype(f32)[..., None]
    tap_now = extended[:, 2:]
    tap_one = extended[:, 1:-1] * near_one
    tap_two = extended[:, :-2] * near_two
    conv_out = (taps[2] * tap_now + taps[1] * tap_one + taps[0] * tap_two).reshape(rows, width)
    mixed_in = (c_gate * conv_out).astype(bf16)
    mixed_in, tops = tie((mixed_in, tops))
    tops.update(swap_far(tops))
    mixed_mine, mixed_other = halves(mixed_in)
    middle = residual + dot(mixed_mine, out_mine) + dot(mixed_other, out_other)
    unit_two, scale_two, norm_two = normed(middle, gain_vals[1])

    norm_two, tops = tie((norm_two, tops))
    tops[0] = grad_top
    norms = swap_near(norm_two)
    hiddens, act_grads, norm_parts, out_parts = {}, {}, {}, {}

    def hidden_block(k):
        both = dot(norms[k], mat_gate_up)
        gate, up_part = both[:, :ff_part], both[:, ff_part:]
        sigma = jax.nn.sigmoid(gate)
        silu_vals = gate * sigma
        grad_hidden = right_contract(tops[k], mat_down)
        hiddens[k] = (silu_vals * up_part).astype(bf16)
        grad_gate_act = (grad_hidden * up_part * sigma * (1.0 + gate * (1.0 - sigma))).astype(bf16)
        grad_up_act = (grad_hidden * silu_vals).astype(bf16)
        act_grads[k] = jnp.concatenate([grad_gate_act, grad_up_act], 1)

    norms[0] = norm_two
    hidden_block(0)
    norm_parts[0] = right_contract(act_grads[0], mat_gate_up)
    out_parts[0] = dot(hiddens[0], mat_down)
    norms, hiddens, act_grads, norm_parts, out_parts = tie(
        (norms, hiddens, act_grads, norm_parts, out_parts)
    )
    norms.update(swap_far(norms))
    norm_sums = {}
    for k in order[1:-1]:
        hidden_block(k)
        norm_parts[k] = right_contract(act_grads[k], mat_gate_up).astype(bf16)
        if k == 1:
            norm_parts, mix_mine, mix_other = tie((norm_parts, mix_mine, mix_other))
            both_halves = [
                mix_mine.reshape(n_z, -1, columns),
                mix_other.reshape(n_z, -1, columns),
            ]
            in_full = place(both_halves, core_slots, width, 0, cut_in).reshape(width, cut_in)
            out_full = place(both_halves, core_slots, width, cut_in, width).reshape(width, width)
            out_parts[1] = dot(hiddens[1], mat_down)
        norms, act_grads, norm_parts, out_parts, in_full, out_full = tie(
            (norms, act_grads, norm_parts, out_parts, in_full, out_full)
        )
        norm_sums[k] = across_seq(norm_parts[k], k)
    hidden_block(last)
    last_parts = [
        right_contract(act_grads[last][start : start + rows // 2], mat_gate_up).astype(bf16)
        for start in (0, rows // 2)
    ]
    last_sums = [across_seq(part, last) for part in last_parts]
    early = {k: norm_sums[k] for k in order[1:-2]}
    out_far = dot(hiddens[last], mat_down).astype(bf16)
    last_parts, hiddens, act_grads, early, out_far = tie(
        (last_parts, hiddens, act_grads, early, out_far)
    )
    norm_sums.update(early)

    def rows_of(blocks):
        return jnp.concatenate([blocks[k] for k in order], 0)

    grad_down = left_contract(rows_of(hiddens), rows_of(tops)).astype(bf16)
    out_parts.update({k: dot(hiddens[k], mat_down) for k in near[1:]})
    out_parts, act_grads, grad_down, norm_sums[order[-2]], last_sums[0] = tie(
        (out_parts, act_grads, grad_down, norm_sums[order[-2]], last_sums[0])
    )
    grad_gate_up = left_contract(rows_of(norms), rows_of(act_grads)).astype(bf16)
    last_sums, grad_gate_up, grad_down = tie((last_sums, grad_gate_up, grad_down))
    gu_sum = lax.psum_scatter(grad_gate_up, "dp", scatter_dimension=0, tiled=True)
    sum_down = lax.psum_scatter(grad_down, "dp", scatter_dimension=0, tiled=True)
    norm_sums[last] = jnp.concatenate(last_sums, 0)
    grad_norm_two = norm_parts[0]
    for k in order[1:]:
        grad_norm_two = grad_norm_two + norm_sums[k].astype(f32)

    back_two, gain_two = norm_back(grad_norm_two, unit_two, scale_two, gain_vals[1])
    grad_middle = grad_top.astype(f32) + back_two
    grad_branch = grad_middle.astype(bf16)
    grad_out_mine = left_contract(mixed_mine, grad_branch)
    grad_out_other = left_contract(mixed_other, grad_branch)
    grad_mixed = right_contract(grad_branch, out_full)
    grad_c = grad_mixed * conv_out
    grad_conv = (grad_mixed * c_gate).reshape(seqs_here, stretch, width)
    grad_taps = [
        jnp.sum(tap_two * grad_conv, (0, 1)),
        jnp.sum(tap_one * grad_conv, (0, 1)),
        jnp.sum(tap_now * grad_conv, (0, 1)),
    ]
    term_now = taps[2] * grad_conv
    term_one = taps[1] * grad_conv * near_one
    term_two = taps[0] * grad_conv * near_two
    grad_ext = (
        jnp.pad(term_now, ((0, 0), (2, 0), (0, 0)))
        + jnp.pad(term_one, ((0, 0), (1, 1), (0, 0)))
        + jnp.pad(term_two, ((0, 0), (0, 2), (0, 0)))
    )
    next_terms = from_behind(grad_ext[:, :2, :], "seq", -1)
    next_terms, out_far = tie((next_terms, out_far))
    out_relay = sum_far(out_far) if n_seq == 4 else ()
    grad_conv_in = (
        grad_ext[:, 2:, :] + jnp.pad(next_terms, ((0, 0), (stretch - 2, 0), (0, 0)))
    ).reshape(rows, width)
    grad_proj = jnp.concatenate([grad_conv_in * x_part, grad_c, grad_conv_in * b_gate], -1).astype(
        bf16
    )
    grad_in_mine = left_contract(norm_mine, grad_proj)
    grad_in_other = left_contract(norm_other, grad_proj)
    grad_norm_one = right_contract(grad_proj, in_full)
    back_one, gain_one = norm_back(grad_norm_one, unit_one, scale_one, gain_vals[0])
    input_grad = (grad_middle + back_one).reshape(seqs_here, stretch, width)

    def sum_core(mine, other):
        return mine + to_sibling(other.astype(bf16)).astype(f32)

    small_grads = jnp.stack(grad_taps + [gain_one, gain_two], 0)
    small_received, out_relay = tie((to_sibling(small_grads), out_relay))
    small_grads = (small_grads + small_received).astype(bf16)
    small_wide = jnp.tile(jnp.pad(small_grads, ((0, own - 5), (0, 0))), (half // own, 1))
    small_wide = jnp.where(row_blocks(core) == feature // own, small_wide, 0.0).astype(bf16)
    in_received = to_sibling(grad_in_other.astype(bf16))
    mixed = jnp.concatenate(
        [
            grad_in_mine + in_received.astype(f32),
            sum_core(grad_out_mine, grad_out_other),
            right_contract(small_wide, spread),
        ],
        1,
    ).astype(bf16)
    gu_sum = gu_sum.reshape(n_seq, own, 2 * ff_part)
    gu_parts = [across_seq(pick(gu_sum, sq ^ k), k) for k in range(1, n_seq)]
    mixed = mixed.reshape(n_z, n_seq, own, -1)

    def seq_block(index):
        return lax.dynamic_index_in_dim(mixed, index, 1, keepdims=False)

    seq_terms = {k: seq_block(sq ^ k) for k in near}
    if n_seq == 4:
        seq_relay = sum_far(seq_block(sq ^ last))
        seq_relay, gu_parts = tie((seq_relay, gu_parts))
        seq_terms = {k: term.astype(f32) for k, term in seq_terms.items()}
        seq_terms = {k: term.astype(bf16) for k, term in add_far(seq_terms, seq_relay).items()}
    seq_parts = [across_seq(seq_terms[k], k) for k in near]
    out_low = add_far({k: out_parts[k] for k in near}, out_relay)
    out_low = {k: term.astype(bf16) for k, term in out_low.items()}
    gu_sum = seq_ordered([pick(gu_sum, sq)] + gu_parts)

    def by_row(part):
        return (
            part.reshape(n_seq, own, n_dp, own_ff)
            .transpose(1, 2, 0, 3)
            .reshape(own, n_seq * ff_part)
        )

    def matrix_step(master, first, second, grad):
        return adamw(master, first, second, grad, learn_rate, weight_decay)

    gate_rows, up_rows = by_row(gu_sum[:, :, :ff_part]), by_row(gu_sum[:, :, ff_part:])
    seq_parts, out_low, gate_rows, up_rows = tie((seq_parts, out_low, gate_rows, up_rows))
    total = seq_block(sq).astype(f32)
    for part in seq_parts:
        total = total + part.astype(f32)
    low = total.astype(bf16)
    low, sum_down = tie((low, sum_down))
    z_sums = [along_z(pick(low, (z + k) % n_z), k) for k in range(1, n_z)]
    out_sums = {k: across_seq(out_low[k], k) for k in near}
    step_gate = matrix_step(w_gate, m_gate, v_gate, gate_rows.astype(f32))
    step_up = matrix_step(w_up, m_up, v_up, up_rows.astype(f32))
    z_sums, step_gate, step_up = tie((z_sums, step_gate, step_up))
    total = pick(total, z)
    for part in z_sums:
        total = total + part.astype(f32)
    sum_in, sum_out, small_sum = total[:, :cut_in], total[:, cut_in:cut_out], total[:, cut_out:]

    output = middle + out_parts[0]
    for k in near:
        output = output + out_sums[k].astype(f32)
    output = output.astype(bf16)

    step_down = matrix_step(w_down, m_down, v_down, sum_down.astype(f32))
    step_in = matrix_step(w_in, m_in, v_in, sum_in)
    step_out = matrix_step(w_out, m_out, v_out, sum_out)
    step_conv = adamw(conv_w, m_conv, v_conv, small_sum[:3, :own], small_rate, 0.0)
    step_gains = adamw(gains, m_gains, v_gains, small_sum[3:5, :own], small_rate, 0.0)
    updated = [step_in, step_out, step_conv, step_gate, step_up, step_down, step_gains]
    new_w = [item[0] for item in updated]
    new_m = [item[1] for item in updated]
    new_v = [item[2] for item in updated]
    return (
        output.reshape(seqs_here, stretch, width),
        input_grad,
        *new_w,
        *new_m,
        *new_v,
    )


def solution(mesh):
    tokens = P("dp", "seq", None)
    matrix = P(("dp", "seq"), None)
    vector = P(None, ("dp", "seq"))
    weights = (matrix, matrix, vector, matrix, matrix, matrix, vector)
    return jax.shard_map(
        local,
        mesh=mesh,
        in_specs=(tokens, tokens, P("dp", "seq")) + weights * 3,
        out_specs=(tokens, tokens) + weights * 3,
        check_vma=False,
    )
```

```python
import jax
import jax.numpy as jnp
from jax import lax
from jax.experimental import pallas as pl
from jax.experimental.pallas import tpu as pltpu
from jax.sharding import PartitionSpec as P

STEP = 10


norm_eps = 1e-05
learn_rate = 0.02
small_rate = 1.0
beta_one = 0.9
beta_two = 0.95
adam_eps = 1e-08
weight_decay = 0.1
LANES = 128
bf16 = jnp.bfloat16
f32 = jnp.float32


def from_behind(shard, axis, by):
    peers = lax.axis_size(axis)
    pairs = [(i, i + by) for i in range(peers) if 0 <= i + by < peers]
    return lax.ppermute(shard, axis, pairs)


def to_sibling(block):
    return lax.ppermute(block, "dp", [(i, i ^ 1) for i in range(lax.axis_size("dp"))])


def along_z(block, by):
    count = lax.axis_size("dp")
    return lax.ppermute(block, "dp", [(i, (i + 2 * by) % count) for i in range(count)])


def across_seq(block, by):
    return lax.ppermute(block, "seq", [(i, i ^ by) for i in range(lax.axis_size("seq"))])


def swap_near(block):
    count = lax.axis_size("seq")
    near = (1, 2) if count == 4 else range(1, count)
    return {k: across_seq(block, k) for k in near}


def swap_far(near):
    if lax.axis_size("seq") != 4:
        return {}
    half = near[1].shape[0] // 2
    first, second = across_seq(near[1][:half], 2), across_seq(near[2][half:], 1)
    return {3: jnp.concatenate([first, second], 0)}


def sum_far(block):
    half = block.shape[0] // 2
    return across_seq(block[:half], 1), across_seq(block[half:], 2)


def add_far(terms, received):
    if not received:
        return terms
    first, second = received
    half = first.shape[0]
    terms = dict(terms)
    terms[2] = jnp.concatenate([terms[2][:half] + first.astype(f32), terms[2][half:]], 0)
    terms[1] = jnp.concatenate([terms[1][:half], terms[1][half:] + second.astype(f32)], 0)
    return terms


def dot(first, second):
    return jnp.dot(first, second, preferred_element_type=f32)


def left_contract(first, second):
    return lax.dot_general(first, second, (((0,), (0,)), ((), ())), preferred_element_type=f32)


def right_contract(first, second):
    return lax.dot_general(first, second, (((1,), (1,)), ((), ())), preferred_element_type=f32)


def tie(values):
    return lax.optimization_barrier(values)


def pick(stacked, index):
    return lax.dynamic_index_in_dim(stacked, index, 0, keepdims=False)


def place(blocks, slots, chunk, first=0, columns=None):
    outer, depth, width = blocks[0].shape
    columns = width if columns is None else columns
    count = len(blocks)

    def kernel(slots_ref, *refs):
        for k in range(count):
            refs[-1][:, slots_ref[k]] = refs[k][...]

    size = 4 * count * outer * depth * columns
    return pl.pallas_call(
        kernel,
        grid=(columns // chunk,),
        out_shape=jax.ShapeDtypeStruct((outer, count, depth, columns), blocks[0].dtype),
        in_specs=[pl.BlockSpec(memory_space=pltpu.SMEM)]
        + [pl.BlockSpec((outer, depth, chunk), lambda j: (0, 0, j + first // chunk))] * count,
        out_specs=pl.BlockSpec((outer, count, depth, chunk), lambda j: (0, 0, 0, j)),
        compiler_params=pltpu.CompilerParams(vmem_limit_bytes=32 * 2**20),
        cost_estimate=pl.CostEstimate(flops=0, bytes_accessed=size, transcendentals=0),
    )(slots.astype(jnp.int32), *blocks)


def normed(values, gain):
    scale = lax.rsqrt(jnp.mean(values * values, -1, keepdims=True) + norm_eps)
    unit = values * scale
    return (unit, scale, (unit * gain).astype(bf16))


def norm_back(grad_out, unit, scale, gain):
    grad_gain = jnp.sum(grad_out * unit, 0)
    grad_unit = grad_out * gain
    grad_in = scale * (grad_unit - unit * jnp.mean(grad_unit * unit, -1, keepdims=True))
    return (grad_in, grad_gain)


def adamw(master, first, second, grad, rate, decay):
    first_new = beta_one * first + (1.0 - beta_one) * grad
    second_new = beta_two * second + (1.0 - beta_two) * grad * grad
    first_hat = first_new / (1.0 - beta_one**STEP)
    second_hat = second_new / (1.0 - beta_two**STEP)
    master_new = master - rate * (first_hat / (jnp.sqrt(second_hat) + adam_eps) + decay * master)
    return (master_new, first_new, second_new)


def local(
    inputs,
    cotangent,
    segments,
    w_in,
    w_out,
    conv_w,
    w_gate,
    w_up,
    w_down,
    gains,
    m_in,
    m_out,
    m_conv,
    m_gate,
    m_up,
    m_down,
    m_gains,
    v_in,
    v_out,
    v_conv,
    v_gate,
    v_up,
    v_down,
    v_gains,
):
    seqs_here, stretch, width = inputs.shape
    rows = seqs_here * stretch
    n_dp = lax.axis_size("dp")
    n_seq = lax.axis_size("seq")
    n_z = n_dp // 2
    own = w_in.shape[0]
    own_ff = w_down.shape[0]
    ff_part = n_dp * own_ff
    dp = lax.axis_index("dp")
    sq = lax.axis_index("seq")
    z = dp // 2
    core = dp % 2
    first_core = core == 0

    lane = n_seq * own

    def halves(full):
        blocks = [full[:, i * lane : (i + 1) * lane] for i in range(2 * n_z)]
        even = jnp.concatenate(blocks[0::2], 1)
        odd = jnp.concatenate(blocks[1::2], 1)
        return jnp.where(first_core, even, odd), jnp.where(first_core, odd, even)

    def seq_ordered(pieces):
        stacked = jnp.stack(pieces, 0)
        return jnp.stack([pick(stacked, sq ^ j) for j in range(n_seq)], 0)

    def by_part(weight):
        low = weight.astype(bf16).reshape(own, n_dp, n_seq, own_ff)
        return low.transpose(2, 0, 1, 3).reshape(n_seq, own, ff_part)

    smalls = jnp.pad(
        jnp.concatenate([conv_w, gains], 0).astype(bf16), ((0, own - 5), (0, LANES - own))
    )
    mix = jnp.concatenate([w_in.astype(bf16), w_out.astype(bf16), smalls], 1)
    gate_up = jnp.concatenate([by_part(w_gate), by_part(w_up)], 2)

    residual_low = inputs.reshape(rows, width)
    edge_ids = jnp.pad(segments[:, -2:, None].astype(bf16), ((0, 0), (0, 0), (0, LANES - 1)))
    edge = from_behind(jnp.concatenate([inputs[:, -2:, :], edge_ids], 2), "seq", 1)
    z_parts = [along_z(mix, -k) for k in range(1, n_z)]
    gu_parts = [across_seq(pick(gate_up, sq ^ k), k) for k in range(1, n_seq)]
    low_down = w_down.astype(bf16)
    z_parts, gu_parts, edge, low_down = tie((z_parts, gu_parts, edge, low_down))
    gate_up = seq_ordered([pick(gate_up, sq)] + gu_parts)
    mat_gate_up = lax.all_gather(gate_up, "dp", axis=0).reshape(width, 2 * ff_part)
    mat_down = lax.all_gather(low_down, "dp", axis=0, tiled=True)

    columns = mix.shape[1]

    z_slots = (z + jnp.arange(n_z)) % n_z
    seq_slots = sq ^ jnp.arange(n_seq)
    core_slots = core ^ jnp.arange(2)
    order = list(range(n_seq))
    near = order[1:3] if n_seq == 4 else order[1:]
    last = order[-1]
    grad_top = cotangent.reshape(rows, width)
    z_order = place([part[None] for part in [mix] + z_parts], z_slots, columns // 3)[0]
    mix_parts = swap_near(z_order)
    mix_parts = tie(mix_parts)
    mix_parts.update(swap_far(mix_parts))
    mix_parts, top_out = tie((mix_parts, grad_top))
    mix_parts[0] = z_order
    mix_mine = place([mix_parts[k] for k in range(n_seq)], seq_slots, columns // 3)
    mix_mine = mix_mine.reshape(width // 2, columns)

    mix_other = to_sibling(mix_mine)
    tops = swap_near(top_out)

    cut_in, cut_out = 3 * width, 4 * width
    in_mine, in_other = mix_mine[:, :cut_in], mix_other[:, :cut_in]
    out_mine, out_other = mix_mine[:, cut_in:cut_out], mix_other[:, cut_in:cut_out]

    half = width // 2
    feature = lax.broadcasted_iota(jnp.int32, (1, width), 1)
    lane_of = lax.broadcasted_iota(jnp.int32, (LANES, width), 0)
    spread = (lane_of == feature % own).astype(bf16)

    def row_blocks(which):
        row = lax.broadcasted_iota(jnp.int32, (half, 1), 0) // own
        return ((row // n_seq) * 2 + which) * n_seq + row % n_seq

    def small_rows(packed, which):
        wide = jnp.where(row_blocks(which) == feature // own, dot(packed, spread), 0.0)
        chosen = lax.broadcasted_iota(jnp.int32, (8, half), 1) % own
        chosen = chosen == lax.broadcasted_iota(jnp.int32, (8, half), 0)
        return dot(chosen.astype(bf16), wide.astype(bf16))

    small_all = small_rows(mix_mine[:, cut_out:], core) + small_rows(
        mix_other[:, cut_out:], 1 - core
    )
    taps, gain_vals = small_all[:3], small_all[3:5]

    residual = residual_low.astype(f32)
    unit_one, scale_one, norm_one = normed(residual, gain_vals[0])
    edge_rows = jnp.pad(edge[:, :, :width].reshape(2 * seqs_here, width), ((0, 12), (0, 0)))
    edge_norm = normed(edge_rows.astype(f32), gain_vals[0])[2]
    norm_mine, norm_other = halves(norm_one)
    edge_mine, edge_other = halves(edge_norm)
    projected = dot(jnp.concatenate([norm_mine, edge_mine], 0), in_mine) + dot(
        jnp.concatenate([norm_other, edge_other], 0), in_other
    )
    edge_rows = projected[rows : rows + 2 * seqs_here]
    prev_rows = (edge_rows[:, :width] * edge_rows[:, 2 * width :]).astype(bf16)
    prev_rows = prev_rows.reshape(seqs_here, 2, width)
    projected = projected[:rows]
    first_block = sq == 0
    prev_ids = jnp.where(first_block, -1, edge[:, :, width].astype(jnp.int32))
    b_gate = projected[:, :width]
    c_gate = projected[:, width : 2 * width]
    x_part = projected[:, 2 * width :]
    conv_in = (b_gate * x_part).astype(bf16).reshape(seqs_here, stretch, width)
    extended = jnp.concatenate([prev_rows, conv_in], 1).astype(f32)
    ext_ids = jnp.concatenate([prev_ids, segments], 1)
    near_one = (ext_ids[:, 1:-1] == segments).astype(f32)[..., None]
    near_two = (ext_ids[:, :-2] == segments).astype(f32)[..., None]
    tap_now = extended[:, 2:]
    tap_one = extended[:, 1:-1] * near_one
    tap_two = extended[:, :-2] * near_two
    conv_out = (taps[2] * tap_now + taps[1] * tap_one + taps[0] * tap_two).reshape(rows, width)
    mixed_in = (c_gate * conv_out).astype(bf16)
    mixed_in, tops = tie((mixed_in, tops))
    tops.update(swap_far(tops))
    mixed_mine, mixed_other = halves(mixed_in)
    middle = residual + dot(mixed_mine, out_mine) + dot(mixed_other, out_other)
    unit_two, scale_two, norm_two = normed(middle, gain_vals[1])

    norm_two, tops = tie((norm_two, tops))
    tops[0] = grad_top
    norms = swap_near(norm_two)
    hiddens, act_grads, norm_parts, out_parts = {}, {}, {}, {}

    def hidden_block(k):
        both = dot(norms[k], mat_gate_up)
        gate, up_part = both[:, :ff_part], both[:, ff_part:]
        sigma = jax.nn.sigmoid(gate)
        silu_vals = gate * sigma
        grad_hidden = right_contract(tops[k], mat_down)
        hiddens[k] = (silu_vals * up_part).astype(bf16)
        grad_gate_act = (grad_hidden * up_part * sigma * (1.0 + gate * (1.0 - sigma))).astype(bf16)
        grad_up_act = (grad_hidden * silu_vals).astype(bf16)
        act_grads[k] = jnp.concatenate([grad_gate_act, grad_up_act], 1)

    norms[0] = norm_two
    hidden_block(0)
    norm_parts[0] = right_contract(act_grads[0], mat_gate_up)
    out_parts[0] = dot(hiddens[0], mat_down)
    norms, hiddens, act_grads, norm_parts, out_parts = tie(
        (norms, hiddens, act_grads, norm_parts, out_parts)
    )
    norms.update(swap_far(norms))
    norm_sums = {}
    for k in order[1:-1]:
        hidden_block(k)
        norm_parts[k] = right_contract(act_grads[k], mat_gate_up).astype(bf16)
        norm_sums[k] = across_seq(norm_parts[k], k)
        norms, act_grads, norm_parts = tie((norms, act_grads, norm_parts))
    hidden_block(last)
    last_parts = [
        right_contract(act_grads[last][start : start + rows // 2], mat_gate_up).astype(bf16)
        for start in (0, rows // 2)
    ]
    last_sums = [across_seq(part, last) for part in last_parts]
    early = {k: norm_sums[k] for k in order[1:-2]}
    out_far = dot(hiddens[last], mat_down).astype(bf16)
    last_parts, hiddens, act_grads, early, out_far, mix_mine, mix_other = tie(
        (last_parts, hiddens, act_grads, early, out_far, mix_mine, mix_other)
    )
    norm_sums.update(early)

    def rows_of(blocks):
        return jnp.concatenate([blocks[k] for k in order], 0)

    grad_down = left_contract(rows_of(hiddens), rows_of(tops)).astype(bf16)
    out_parts.update({k: dot(hiddens[k], mat_down) for k in near})
    halves_of = [part.reshape(n_z, -1, columns) for part in (mix_mine, mix_other)]
    in_full = place(halves_of, core_slots, width, 0, cut_in).reshape(width, cut_in)
    out_full = place(halves_of, core_slots, width, cut_in, width).reshape(width, width)
    out_parts, act_grads, grad_down, norm_sums[order[-2]], last_sums[0], in_full, out_full = tie(
        (
            out_parts,
            act_grads,
            grad_down,
            norm_sums[order[-2]],
            last_sums[0],
            in_full,
            out_full,
        )
    )
    grad_gate_up = left_contract(rows_of(norms), rows_of(act_grads)).astype(bf16)
    last_sums, grad_gate_up, grad_down = tie((last_sums, grad_gate_up, grad_down))
    gu_sum = lax.psum_scatter(grad_gate_up, "dp", scatter_dimension=0, tiled=True)
    sum_down = lax.psum_scatter(grad_down, "dp", scatter_dimension=0, tiled=True)
    norm_sums[last] = jnp.concatenate(last_sums, 0)
    grad_norm_two = norm_parts[0]
    for k in order[1:]:
        grad_norm_two = grad_norm_two + norm_sums[k].astype(f32)

    back_two, gain_two = norm_back(grad_norm_two, unit_two, scale_two, gain_vals[1])
    grad_middle = grad_top.astype(f32) + back_two
    grad_branch = grad_middle.astype(bf16)
    grad_out_mine = left_contract(mixed_mine, grad_branch)
    grad_out_other = left_contract(mixed_other, grad_branch)
    grad_mixed = right_contract(grad_branch, out_full)
    grad_c = grad_mixed * conv_out
    grad_conv = (grad_mixed * c_gate).reshape(seqs_here, stretch, width)
    grad_taps = [
        jnp.sum(tap_two * grad_conv, (0, 1)),
        jnp.sum(tap_one * grad_conv, (0, 1)),
        jnp.sum(tap_now * grad_conv, (0, 1)),
    ]
    term_now = taps[2] * grad_conv
    term_one = taps[1] * grad_conv * near_one
    term_two = taps[0] * grad_conv * near_two
    grad_ext = (
        jnp.pad(term_now, ((0, 0), (2, 0), (0, 0)))
        + jnp.pad(term_one, ((0, 0), (1, 1), (0, 0)))
        + jnp.pad(term_two, ((0, 0), (0, 2), (0, 0)))
    )
    next_terms = from_behind(grad_ext[:, :2, :], "seq", -1)
    next_terms, out_far = tie((next_terms, out_far))
    out_relay = sum_far(out_far) if n_seq == 4 else ()
    grad_conv_in = (
        grad_ext[:, 2:, :] + jnp.pad(next_terms, ((0, 0), (stretch - 2, 0), (0, 0)))
    ).reshape(rows, width)
    grad_proj = jnp.concatenate([grad_conv_in * x_part, grad_c, grad_conv_in * b_gate], -1).astype(
        bf16
    )
    grad_in_mine = left_contract(norm_mine, grad_proj)
    grad_in_other = left_contract(norm_other, grad_proj)
    grad_norm_one = right_contract(grad_proj, in_full)
    back_one, gain_one = norm_back(grad_norm_one, unit_one, scale_one, gain_vals[0])
    input_grad = (grad_middle + back_one).reshape(seqs_here, stretch, width)

    def sum_core(mine, other):
        return mine + to_sibling(other.astype(bf16)).astype(f32)

    small_grads = jnp.stack(grad_taps + [gain_one, gain_two], 0)
    small_grads = (small_grads + to_sibling(small_grads)).astype(bf16)
    small_wide = jnp.tile(jnp.pad(small_grads, ((0, own - 5), (0, 0))), (half // own, 1))
    small_wide = jnp.where(row_blocks(core) == feature // own, small_wide, 0.0).astype(bf16)
    in_received = to_sibling(grad_in_other.astype(bf16))
    mixed = jnp.concatenate(
        [
            grad_in_mine + in_received.astype(f32),
            sum_core(grad_out_mine, grad_out_other),
            right_contract(small_wide, spread),
        ],
        1,
    ).astype(bf16)
    gu_sum = gu_sum.reshape(n_seq, own, 2 * ff_part)
    gu_parts = [across_seq(pick(gu_sum, sq ^ k), k) for k in range(1, n_seq)]
    mixed, out_relay = tie((mixed, out_relay))
    mixed = mixed.reshape(n_z, n_seq, own, -1)

    def seq_block(index):
        return lax.dynamic_index_in_dim(mixed, index, 1, keepdims=False)

    seq_terms = {k: seq_block(sq ^ k) for k in near}
    if n_seq == 4:
        seq_relay = sum_far(seq_block(sq ^ last))
        seq_relay, gu_parts = tie((seq_relay, gu_parts))
        seq_terms = {k: term.astype(f32) for k, term in seq_terms.items()}
        seq_terms = {k: term.astype(bf16) for k, term in add_far(seq_terms, seq_relay).items()}
    seq_parts = [across_seq(seq_terms[k], k) for k in near]
    out_low = add_far({k: out_parts[k] for k in near}, out_relay)
    out_low = {k: term.astype(bf16) for k, term in out_low.items()}
    gu_sum = seq_ordered([pick(gu_sum, sq)] + gu_parts)

    def by_row(part):
        return (
            part.reshape(n_seq, own, n_dp, own_ff)
            .transpose(1, 2, 0, 3)
            .reshape(own, n_seq * ff_part)
        )

    def matrix_step(master, first, second, grad):
        return adamw(master, first, second, grad, learn_rate, weight_decay)

    gate_rows, up_rows = by_row(gu_sum[:, :, :ff_part]), by_row(gu_sum[:, :, ff_part:])
    seq_parts, out_low, gate_rows, up_rows = tie((seq_parts, out_low, gate_rows, up_rows))
    total = seq_block(sq).astype(f32)
    for part in seq_parts:
        total = total + part.astype(f32)
    low = total.astype(bf16)
    low, sum_down = tie((low, sum_down))
    z_sums = [along_z(pick(low, (z + k) % n_z), k) for k in range(1, n_z)]
    out_sums = {k: across_seq(out_low[k], k) for k in near}
    step_gate = matrix_step(w_gate, m_gate, v_gate, gate_rows.astype(f32))
    step_up = matrix_step(w_up, m_up, v_up, up_rows.astype(f32))
    z_sums, step_gate, step_up = tie((z_sums, step_gate, step_up))
    total = pick(total, z)
    for part in z_sums:
        total = total + part.astype(f32)
    sum_in, sum_out, small_sum = total[:, :cut_in], total[:, cut_in:cut_out], total[:, cut_out:]

    output = middle + out_parts[0]
    for k in near:
        output = output + out_sums[k].astype(f32)
    output = output.astype(bf16)

    step_down = matrix_step(w_down, m_down, v_down, sum_down.astype(f32))
    step_in = matrix_step(w_in, m_in, v_in, sum_in)
    step_out = matrix_step(w_out, m_out, v_out, sum_out)
    step_conv = adamw(conv_w, m_conv, v_conv, small_sum[:3, :own], small_rate, 0.0)
    step_gains = adamw(gains, m_gains, v_gains, small_sum[3:5, :own], small_rate, 0.0)
    updated = [step_in, step_out, step_conv, step_gate, step_up, step_down, step_gains]
    new_w = [item[0] for item in updated]
    new_m = [item[1] for item in updated]
    new_v = [item[2] for item in updated]
    return (
        output.reshape(seqs_here, stretch, width),
        input_grad,
        *new_w,
        *new_m,
        *new_v,
    )


def solution(mesh):
    tokens = P("dp", "seq", None)
    matrix = P(("dp", "seq"), None)
    vector = P(None, ("dp", "seq"))
    weights = (matrix, matrix, vector, matrix, matrix, matrix, vector)
    return jax.shard_map(
        local,
        mesh=mesh,
        in_specs=(tokens, tokens, P("dp", "seq")) + weights * 3,
        out_specs=(tokens, tokens) + weights * 3,
        check_vma=False,
    )
```

```python
import jax
import jax.numpy as jnp
from jax import lax
from jax.experimental import pallas as pl
from jax.experimental.pallas import tpu as pltpu
from jax.sharding import PartitionSpec as P

STEP = 10


norm_eps = 1e-05
learn_rate = 0.02
small_rate = 1.0
beta_one = 0.9
beta_two = 0.95
adam_eps = 1e-08
weight_decay = 0.1
LANES = 128
bf16 = jnp.bfloat16
f32 = jnp.float32


def from_behind(shard, axis, by):
    peers = lax.axis_size(axis)
    pairs = [(i, i + by) for i in range(peers) if 0 <= i + by < peers]
    return lax.ppermute(shard, axis, pairs)


def to_sibling(block):
    return lax.ppermute(block, "dp", [(i, i ^ 1) for i in range(lax.axis_size("dp"))])


def along_z(block, by):
    count = lax.axis_size("dp")
    return lax.ppermute(block, "dp", [(i, (i + 2 * by) % count) for i in range(count)])


def across_seq(block, by):
    return lax.ppermute(block, "seq", [(i, i ^ by) for i in range(lax.axis_size("seq"))])


def swap_near(block):
    count = lax.axis_size("seq")
    near = (1, 2) if count == 4 else range(1, count)
    return {k: across_seq(block, k) for k in near}


def swap_far(near):
    if lax.axis_size("seq") != 4:
        return {}
    half = near[1].shape[0] // 2
    first, second = across_seq(near[1][:half], 2), across_seq(near[2][half:], 1)
    return {3: jnp.concatenate([first, second], 0)}


def sum_far(halves):
    return across_seq(halves[0], 1), across_seq(halves[1], 2)


def add_far(terms, received):
    if not received:
        return terms
    first, second = received
    half = first.shape[0]
    terms = dict(terms)
    terms[2] = jnp.concatenate([terms[2][:half] + first.astype(f32), terms[2][half:]], 0)
    terms[1] = jnp.concatenate([terms[1][:half], terms[1][half:] + second.astype(f32)], 0)
    return terms


def dot(first, second):
    return jnp.dot(first, second, preferred_element_type=f32)


def left_contract(first, second):
    return lax.dot_general(first, second, (((0,), (0,)), ((), ())), preferred_element_type=f32)


def right_contract(first, second):
    return lax.dot_general(first, second, (((1,), (1,)), ((), ())), preferred_element_type=f32)


def tie(values):
    return lax.optimization_barrier(values)


def pick(stacked, index):
    return lax.dynamic_index_in_dim(stacked, index, 0, keepdims=False)


def place(blocks, slots, chunk, first=0, columns=None):
    outer, depth, width = blocks[0].shape
    columns = width if columns is None else columns
    count = len(blocks)

    def kernel(slots_ref, *refs):
        for k in range(count):
            refs[-1][:, slots_ref[k]] = refs[k][...]

    size = 4 * count * outer * depth * columns
    return pl.pallas_call(
        kernel,
        grid=(columns // chunk,),
        out_shape=jax.ShapeDtypeStruct((outer, count, depth, columns), blocks[0].dtype),
        in_specs=[pl.BlockSpec(memory_space=pltpu.SMEM)]
        + [pl.BlockSpec((outer, depth, chunk), lambda j: (0, 0, j + first // chunk))] * count,
        out_specs=pl.BlockSpec((outer, count, depth, chunk), lambda j: (0, 0, 0, j)),
        compiler_params=pltpu.CompilerParams(vmem_limit_bytes=32 * 2**20),
        cost_estimate=pl.CostEstimate(flops=0, bytes_accessed=size, transcendentals=0),
    )(slots.astype(jnp.int32), *blocks)


def normed(values, gain):
    scale = lax.rsqrt(jnp.mean(values * values, -1, keepdims=True) + norm_eps)
    unit = values * scale
    return (unit, scale, (unit * gain).astype(bf16))


def norm_back(grad_out, unit, scale, gain):
    grad_gain = jnp.sum(grad_out * unit, 0)
    grad_unit = grad_out * gain
    grad_in = scale * (grad_unit - unit * jnp.mean(grad_unit * unit, -1, keepdims=True))
    return (grad_in, grad_gain)


def adamw(master, first, second, grad, rate, decay):
    first_new = beta_one * first + (1.0 - beta_one) * grad
    second_new = beta_two * second + (1.0 - beta_two) * grad * grad
    first_hat = first_new / (1.0 - beta_one**STEP)
    second_hat = second_new / (1.0 - beta_two**STEP)
    master_new = master - rate * (first_hat / (jnp.sqrt(second_hat) + adam_eps) + decay * master)
    return (master_new, first_new, second_new)


def local(
    inputs,
    cotangent,
    segments,
    w_in,
    w_out,
    conv_w,
    w_gate,
    w_up,
    w_down,
    gains,
    m_in,
    m_out,
    m_conv,
    m_gate,
    m_up,
    m_down,
    m_gains,
    v_in,
    v_out,
    v_conv,
    v_gate,
    v_up,
    v_down,
    v_gains,
):
    seqs_here, stretch, width = inputs.shape
    rows = seqs_here * stretch
    n_dp = lax.axis_size("dp")
    n_seq = lax.axis_size("seq")
    n_z = n_dp // 2
    own = w_in.shape[0]
    own_ff = w_down.shape[0]
    ff_part = n_dp * own_ff
    dp = lax.axis_index("dp")
    sq = lax.axis_index("seq")
    z = dp // 2
    core = dp % 2
    first_core = core == 0

    lane = n_seq * own

    def halves(full):
        blocks = [full[:, i * lane : (i + 1) * lane] for i in range(2 * n_z)]
        even = jnp.concatenate(blocks[0::2], 1)
        odd = jnp.concatenate(blocks[1::2], 1)
        return jnp.where(first_core, even, odd), jnp.where(first_core, odd, even)

    def seq_ordered(pieces):
        stacked = jnp.stack(pieces, 0)
        return jnp.stack([pick(stacked, sq ^ j) for j in range(n_seq)], 0)

    def by_part(weight):
        low = weight.astype(bf16).reshape(own, n_dp, n_seq, own_ff)
        return low.transpose(2, 0, 1, 3).reshape(n_seq, own, ff_part)

    smalls = jnp.pad(
        jnp.concatenate([conv_w, gains], 0).astype(bf16), ((0, own - 5), (0, LANES - own))
    )
    mix = jnp.concatenate([w_in.astype(bf16), w_out.astype(bf16), smalls], 1)
    gate_up = jnp.concatenate([by_part(w_gate), by_part(w_up)], 2)

    residual_low = inputs.reshape(rows, width)
    edge_ids = jnp.pad(segments[:, -2:, None].astype(bf16), ((0, 0), (0, 0), (0, LANES - 1)))
    edge = from_behind(jnp.concatenate([inputs[:, -2:, :], edge_ids], 2), "seq", 1)
    z_parts = [along_z(mix, -k) for k in range(1, n_z)]
    gu_parts = [across_seq(pick(gate_up, sq ^ k), k) for k in range(1, n_seq)]
    low_down = w_down.astype(bf16)
    z_parts, gu_parts, edge, low_down = tie((z_parts, gu_parts, edge, low_down))
    gate_up = seq_ordered([pick(gate_up, sq)] + gu_parts)
    mat_gate_up = lax.all_gather(gate_up, "dp", axis=0).reshape(width, 2 * ff_part)
    mat_down = lax.all_gather(low_down, "dp", axis=0, tiled=True)

    columns = mix.shape[1]

    z_slots = (z + jnp.arange(n_z)) % n_z
    seq_slots = sq ^ jnp.arange(n_seq)
    core_slots = core ^ jnp.arange(2)
    order = list(range(n_seq))
    near = order[1:3] if n_seq == 4 else order[1:]
    last = order[-1]
    grad_top = cotangent.reshape(rows, width)
    z_order = place([part[None] for part in [mix] + z_parts], z_slots, columns // 3)[0]
    mix_parts = swap_near(z_order)
    mix_parts = tie(mix_parts)
    mix_parts.update(swap_far(mix_parts))
    mix_parts, top_out = tie((mix_parts, grad_top))
    mix_parts[0] = z_order
    mix_mine = place([mix_parts[k] for k in range(n_seq)], seq_slots, columns // 3)
    mix_mine = mix_mine.reshape(width // 2, columns)

    mix_other = to_sibling(mix_mine)
    tops = swap_near(top_out)

    cut_in, cut_out = 3 * width, 4 * width
    in_mine, in_other = mix_mine[:, :cut_in], mix_other[:, :cut_in]
    out_mine, out_other = mix_mine[:, cut_in:cut_out], mix_other[:, cut_in:cut_out]

    half = width // 2
    feature = lax.broadcasted_iota(jnp.int32, (1, width), 1)
    lane_of = lax.broadcasted_iota(jnp.int32, (LANES, width), 0)
    spread = (lane_of == feature % own).astype(bf16)

    def row_blocks(which):
        row = lax.broadcasted_iota(jnp.int32, (half, 1), 0) // own
        return ((row // n_seq) * 2 + which) * n_seq + row % n_seq

    def small_rows(packed, which):
        wide = jnp.where(row_blocks(which) == feature // own, dot(packed, spread), 0.0)
        chosen = lax.broadcasted_iota(jnp.int32, (8, half), 1) % own
        chosen = chosen == lax.broadcasted_iota(jnp.int32, (8, half), 0)
        return dot(chosen.astype(bf16), wide.astype(bf16))

    small_all = small_rows(mix_mine[:, cut_out:], core) + small_rows(
        mix_other[:, cut_out:], 1 - core
    )
    taps, gain_vals = small_all[:3], small_all[3:5]

    residual = residual_low.astype(f32)
    unit_one, scale_one, norm_one = normed(residual, gain_vals[0])
    edge_rows = jnp.pad(edge[:, :, :width].reshape(2 * seqs_here, width), ((0, 12), (0, 0)))
    edge_norm = normed(edge_rows.astype(f32), gain_vals[0])[2]
    norm_mine, norm_other = halves(norm_one)
    edge_mine, edge_other = halves(edge_norm)
    projected = dot(jnp.concatenate([norm_mine, edge_mine], 0), in_mine) + dot(
        jnp.concatenate([norm_other, edge_other], 0), in_other
    )
    edge_rows = projected[rows : rows + 2 * seqs_here]
    prev_rows = (edge_rows[:, :width] * edge_rows[:, 2 * width :]).astype(bf16)
    prev_rows = prev_rows.reshape(seqs_here, 2, width)
    projected = projected[:rows]
    first_block = sq == 0
    prev_ids = jnp.where(first_block, -1, edge[:, :, width].astype(jnp.int32))
    b_gate = projected[:, :width]
    c_gate = projected[:, width : 2 * width]
    x_part = projected[:, 2 * width :]
    conv_in = (b_gate * x_part).astype(bf16).reshape(seqs_here, stretch, width)
    extended = jnp.concatenate([prev_rows, conv_in], 1).astype(f32)
    ext_ids = jnp.concatenate([prev_ids, segments], 1)
    near_one = (ext_ids[:, 1:-1] == segments).astype(f32)[..., None]
    near_two = (ext_ids[:, :-2] == segments).astype(f32)[..., None]
    tap_now = extended[:, 2:]
    tap_one = extended[:, 1:-1] * near_one
    tap_two = extended[:, :-2] * near_two
    conv_out = (taps[2] * tap_now + taps[1] * tap_one + taps[0] * tap_two).reshape(rows, width)
    mixed_in = (c_gate * conv_out).astype(bf16)
    mixed_in, tops = tie((mixed_in, tops))
    tops.update(swap_far(tops))
    mixed_mine, mixed_other = halves(mixed_in)
    middle = residual + dot(mixed_mine, out_mine) + dot(mixed_other, out_other)
    unit_two, scale_two, norm_two = normed(middle, gain_vals[1])

    norm_two, tops = tie((norm_two, tops))
    tops[0] = grad_top
    norms = swap_near(norm_two)
    hiddens, act_grads, norm_parts, out_parts = {}, {}, {}, {}

    def hidden_block(k):
        both = dot(norms[k], mat_gate_up)
        gate, up_part = both[:, :ff_part], both[:, ff_part:]
        sigma = jax.nn.sigmoid(gate)
        silu_vals = gate * sigma
        grad_hidden = right_contract(tops[k], mat_down)
        hiddens[k] = (silu_vals * up_part).astype(bf16)
        grad_gate_act = (grad_hidden * up_part * sigma * (1.0 + gate * (1.0 - sigma))).astype(bf16)
        grad_up_act = (grad_hidden * silu_vals).astype(bf16)
        act_grads[k] = jnp.concatenate([grad_gate_act, grad_up_act], 1)

    norms[0] = norm_two
    hidden_block(0)
    norm_parts[0] = right_contract(act_grads[0], mat_gate_up)
    out_parts[0] = dot(hiddens[0], mat_down)
    norms, hiddens, act_grads, norm_parts, out_parts = tie(
        (norms, hiddens, act_grads, norm_parts, out_parts)
    )
    norms.update(swap_far(norms))
    norm_sums = {}
    for k in order[1:-1]:
        hidden_block(k)
        norm_parts[k] = right_contract(act_grads[k], mat_gate_up).astype(bf16)
        norm_sums[k] = across_seq(norm_parts[k], k)
        norms, act_grads, norm_parts = tie((norms, act_grads, norm_parts))
    hidden_block(last)
    last_parts = [
        right_contract(act_grads[last][start : start + rows // 2], mat_gate_up).astype(bf16)
        for start in (0, rows // 2)
    ]
    last_sums = [across_seq(part, last) for part in last_parts]
    early = {k: norm_sums[k] for k in order[1:-2]}
    out_far = [
        dot(hiddens[last][start : start + rows // 2], mat_down).astype(bf16)
        for start in (0, rows // 2)
    ]
    last_parts, hiddens, act_grads, early, out_far, mix_mine, mix_other = tie(
        (last_parts, hiddens, act_grads, early, out_far, mix_mine, mix_other)
    )
    norm_sums.update(early)

    def rows_of(blocks):
        return jnp.concatenate([blocks[k] for k in order], 0)

    grad_down = left_contract(rows_of(hiddens), rows_of(tops)).astype(bf16)
    out_parts.update({k: dot(hiddens[k], mat_down) for k in near})
    halves_of = [part.reshape(n_z, -1, columns) for part in (mix_mine, mix_other)]
    in_full = place(halves_of, core_slots, width, 0, cut_in).reshape(width, cut_in)
    out_full = place(halves_of, core_slots, width, cut_in, width).reshape(width, width)
    out_parts, act_grads, grad_down, last_sums[0], in_full, out_full = tie(
        (out_parts, act_grads, grad_down, last_sums[0], in_full, out_full)
    )
    grad_gate_up = left_contract(rows_of(norms), rows_of(act_grads)).astype(bf16)
    last_sums, norm_sums, grad_gate_up, grad_down = tie(
        (last_sums, norm_sums, grad_gate_up, grad_down)
    )
    gu_sum = lax.psum_scatter(grad_gate_up, "dp", scatter_dimension=0, tiled=True)
    sum_down = lax.psum_scatter(grad_down, "dp", scatter_dimension=0, tiled=True)
    norm_sums[last] = jnp.concatenate(last_sums, 0)
    grad_norm_two = norm_parts[0]
    for k in order[1:]:
        grad_norm_two = grad_norm_two + norm_sums[k].astype(f32)

    back_two, gain_two = norm_back(grad_norm_two, unit_two, scale_two, gain_vals[1])
    grad_middle = grad_top.astype(f32) + back_two
    grad_branch = grad_middle.astype(bf16)
    grad_out_mine = left_contract(mixed_mine, grad_branch)
    grad_out_other = left_contract(mixed_other, grad_branch)
    grad_mixed = right_contract(grad_branch, out_full)
    grad_c = grad_mixed * conv_out
    grad_conv = (grad_mixed * c_gate).reshape(seqs_here, stretch, width)
    grad_taps = [
        jnp.sum(tap_two * grad_conv, (0, 1)),
        jnp.sum(tap_one * grad_conv, (0, 1)),
        jnp.sum(tap_now * grad_conv, (0, 1)),
    ]
    term_now = taps[2] * grad_conv
    term_one = taps[1] * grad_conv * near_one
    term_two = taps[0] * grad_conv * near_two
    grad_ext = (
        jnp.pad(term_now, ((0, 0), (2, 0), (0, 0)))
        + jnp.pad(term_one, ((0, 0), (1, 1), (0, 0)))
        + jnp.pad(term_two, ((0, 0), (0, 2), (0, 0)))
    )
    next_terms = from_behind(grad_ext[:, :2, :], "seq", -1)
    next_terms, out_far = tie((next_terms, out_far))
    out_relay = sum_far(out_far) if n_seq == 4 else ()
    grad_conv_in = (
        grad_ext[:, 2:, :] + jnp.pad(next_terms, ((0, 0), (stretch - 2, 0), (0, 0)))
    ).reshape(rows, width)
    grad_proj = jnp.concatenate([grad_conv_in * x_part, grad_c, grad_conv_in * b_gate], -1).astype(
        bf16
    )
    grad_in_mine = left_contract(norm_mine, grad_proj)
    grad_in_other = left_contract(norm_other, grad_proj)
    grad_norm_one = right_contract(grad_proj, in_full)
    back_one, gain_one = norm_back(grad_norm_one, unit_one, scale_one, gain_vals[0])
    input_grad = (grad_middle + back_one).reshape(seqs_here, stretch, width)

    def sum_core(mine, other):
        return mine + to_sibling(other.astype(bf16)).astype(f32)

    small_grads = jnp.stack(grad_taps + [gain_one, gain_two], 0)
    small_grads = (small_grads + to_sibling(small_grads)).astype(bf16)
    small_wide = jnp.tile(jnp.pad(small_grads, ((0, own - 5), (0, 0))), (half // own, 1))
    small_wide = jnp.where(row_blocks(core) == feature // own, small_wide, 0.0).astype(bf16)
    in_received = to_sibling(grad_in_other.astype(bf16))
    mixed = jnp.concatenate(
        [
            grad_in_mine + in_received.astype(f32),
            sum_core(grad_out_mine, grad_out_other),
            right_contract(small_wide, spread),
        ],
        1,
    ).astype(bf16)
    gu_sum = gu_sum.reshape(n_seq, own, 2 * ff_part)
    gu_parts = [across_seq(pick(gu_sum, sq ^ k), k) for k in range(1, n_seq)]
    mixed, out_relay = tie((mixed, out_relay))
    mixed = mixed.reshape(n_z, n_seq, own, -1)

    def seq_block(index):
        return lax.dynamic_index_in_dim(mixed, index, 1, keepdims=False)

    seq_terms = {k: seq_block(sq ^ k) for k in near}
    if n_seq == 4:
        far_block = seq_block(sq ^ last)
        seq_relay = sum_far((far_block[: n_z // 2], far_block[n_z // 2 :]))
        seq_relay, gu_parts = tie((seq_relay, gu_parts))
        seq_terms = {k: term.astype(f32) for k, term in seq_terms.items()}
        seq_terms = {k: term.astype(bf16) for k, term in add_far(seq_terms, seq_relay).items()}
    seq_parts = [across_seq(seq_terms[k], k) for k in near]
    out_low = add_far({k: out_parts[k] for k in near}, out_relay)
    out_low = {k: term.astype(bf16) for k, term in out_low.items()}
    gu_sum = seq_ordered([pick(gu_sum, sq)] + gu_parts)

    def by_row(part):
        return (
            part.reshape(n_seq, own, n_dp, own_ff)
            .transpose(1, 2, 0, 3)
            .reshape(own, n_seq * ff_part)
        )

    def matrix_step(master, first, second, grad):
        return adamw(master, first, second, grad, learn_rate, weight_decay)

    gate_rows, up_rows = by_row(gu_sum[:, :, :ff_part]), by_row(gu_sum[:, :, ff_part:])
    seq_parts, out_low, gate_rows, up_rows = tie((seq_parts, out_low, gate_rows, up_rows))
    total = seq_block(sq).astype(f32)
    for part in seq_parts:
        total = total + part.astype(f32)
    low = total.astype(bf16)
    low, sum_down = tie((low, sum_down))
    z_sums = [along_z(pick(low, (z + k) % n_z), k) for k in range(1, n_z)]
    out_sums = {k: across_seq(out_low[k], k) for k in near}
    step_gate = matrix_step(w_gate, m_gate, v_gate, gate_rows.astype(f32))
    step_up = matrix_step(w_up, m_up, v_up, up_rows.astype(f32))
    z_sums, step_gate, step_up = tie((z_sums, step_gate, step_up))
    total = pick(total, z)
    for part in z_sums:
        total = total + part.astype(f32)
    sum_in, sum_out, small_sum = total[:, :cut_in], total[:, cut_in:cut_out], total[:, cut_out:]

    output = middle + out_parts[0]
    for k in near:
        output = output + out_sums[k].astype(f32)
    output = output.astype(bf16)

    step_down = matrix_step(w_down, m_down, v_down, sum_down.astype(f32))
    step_in = matrix_step(w_in, m_in, v_in, sum_in)
    step_out = matrix_step(w_out, m_out, v_out, sum_out)
    step_conv = adamw(conv_w, m_conv, v_conv, small_sum[:3, :own], small_rate, 0.0)
    step_gains = adamw(gains, m_gains, v_gains, small_sum[3:5, :own], small_rate, 0.0)
    updated = [step_in, step_out, step_conv, step_gate, step_up, step_down, step_gains]
    new_w = [item[0] for item in updated]
    new_m = [item[1] for item in updated]
    new_v = [item[2] for item in updated]
    return (
        output.reshape(seqs_here, stretch, width),
        input_grad,
        *new_w,
        *new_m,
        *new_v,
    )


def solution(mesh):
    tokens = P("dp", "seq", None)
    matrix = P(("dp", "seq"), None)
    vector = P(None, ("dp", "seq"))
    weights = (matrix, matrix, vector, matrix, matrix, matrix, vector)
    return jax.shard_map(
        local,
        mesh=mesh,
        in_specs=(tokens, tokens, P("dp", "seq")) + weights * 3,
        out_specs=(tokens, tokens) + weights * 3,
        check_vma=False,
    )
```

```python
import jax
import jax.numpy as jnp
from jax import lax
from jax.experimental import pallas as pl
from jax.experimental.pallas import tpu as pltpu
from jax.sharding import PartitionSpec as P

STEP = 10


norm_eps = 1e-05
learn_rate = 0.02
small_rate = 1.0
beta_one = 0.9
beta_two = 0.95
adam_eps = 1e-08
weight_decay = 0.1
LANES = 128
bf16 = jnp.bfloat16
f32 = jnp.float32


def from_behind(shard, axis, by):
    peers = lax.axis_size(axis)
    pairs = [(i, i + by) for i in range(peers) if 0 <= i + by < peers]
    return lax.ppermute(shard, axis, pairs)


def to_sibling(block):
    return lax.ppermute(block, "dp", [(i, i ^ 1) for i in range(lax.axis_size("dp"))])


def along_z(block, by):
    count = lax.axis_size("dp")
    return lax.ppermute(block, "dp", [(i, (i + 2 * by) % count) for i in range(count)])


def across_seq(block, by):
    return lax.ppermute(block, "seq", [(i, i ^ by) for i in range(lax.axis_size("seq"))])


def swap_near(block):
    count = lax.axis_size("seq")
    near = (1, 2) if count == 4 else range(1, count)
    return {k: across_seq(block, k) for k in near}


def swap_far(near):
    if lax.axis_size("seq") != 4:
        return {}
    half = near[1].shape[0] // 2
    first, second = across_seq(near[1][:half], 2), across_seq(near[2][half:], 1)
    return {3: jnp.concatenate([first, second], 0)}


def sum_far(halves):
    return across_seq(halves[0], 1), across_seq(halves[1], 2)


def add_far(terms, received):
    if not received:
        return terms
    first, second = received
    half = first.shape[0]
    terms = dict(terms)
    terms[2] = jnp.concatenate([terms[2][:half] + first.astype(f32), terms[2][half:]], 0)
    terms[1] = jnp.concatenate([terms[1][:half], terms[1][half:] + second.astype(f32)], 0)
    return terms


def dot(first, second):
    return jnp.dot(first, second, preferred_element_type=f32)


def left_contract(first, second):
    return lax.dot_general(first, second, (((0,), (0,)), ((), ())), preferred_element_type=f32)


def right_contract(first, second):
    return lax.dot_general(first, second, (((1,), (1,)), ((), ())), preferred_element_type=f32)


def tie(values):
    return lax.optimization_barrier(values)


def pick(stacked, index):
    return lax.dynamic_index_in_dim(stacked, index, 0, keepdims=False)


def place(blocks, slots, chunk, first=0, columns=None):
    outer, depth, width = blocks[0].shape
    columns = width if columns is None else columns
    count = len(blocks)

    def kernel(slots_ref, *refs):
        for k in range(count):
            refs[-1][:, slots_ref[k]] = refs[k][...]

    size = 4 * count * outer * depth * columns
    return pl.pallas_call(
        kernel,
        grid=(columns // chunk,),
        out_shape=jax.ShapeDtypeStruct((outer, count, depth, columns), blocks[0].dtype),
        in_specs=[pl.BlockSpec(memory_space=pltpu.SMEM)]
        + [pl.BlockSpec((outer, depth, chunk), lambda j: (0, 0, j + first // chunk))] * count,
        out_specs=pl.BlockSpec((outer, count, depth, chunk), lambda j: (0, 0, 0, j)),
        compiler_params=pltpu.CompilerParams(vmem_limit_bytes=32 * 2**20),
        cost_estimate=pl.CostEstimate(flops=0, bytes_accessed=size, transcendentals=0),
    )(slots.astype(jnp.int32), *blocks)


def normed(values, gain):
    scale = lax.rsqrt(jnp.mean(values * values, -1, keepdims=True) + norm_eps)
    unit = values * scale
    return (unit, scale, (unit * gain).astype(bf16))


def norm_back(grad_out, unit, scale, gain):
    grad_gain = jnp.sum(grad_out * unit, 0)
    grad_unit = grad_out * gain
    grad_in = scale * (grad_unit - unit * jnp.mean(grad_unit * unit, -1, keepdims=True))
    return (grad_in, grad_gain)


def adamw(master, first, second, grad, rate, decay):
    first_new = beta_one * first + (1.0 - beta_one) * grad
    second_new = beta_two * second + (1.0 - beta_two) * grad * grad
    first_hat = first_new / (1.0 - beta_one**STEP)
    second_hat = second_new / (1.0 - beta_two**STEP)
    master_new = master - rate * (first_hat / (jnp.sqrt(second_hat) + adam_eps) + decay * master)
    return (master_new, first_new, second_new)


def local(
    inputs,
    cotangent,
    segments,
    w_in,
    w_out,
    conv_w,
    w_gate,
    w_up,
    w_down,
    gains,
    m_in,
    m_out,
    m_conv,
    m_gate,
    m_up,
    m_down,
    m_gains,
    v_in,
    v_out,
    v_conv,
    v_gate,
    v_up,
    v_down,
    v_gains,
):
    seqs_here, stretch, width = inputs.shape
    rows = seqs_here * stretch
    n_dp = lax.axis_size("dp")
    n_seq = lax.axis_size("seq")
    n_z = n_dp // 2
    own = w_in.shape[0]
    own_ff = w_down.shape[0]
    ff_part = n_dp * own_ff
    dp = lax.axis_index("dp")
    sq = lax.axis_index("seq")
    z = dp // 2
    core = dp % 2
    first_core = core == 0

    lane = n_seq * own

    def halves(full):
        blocks = [full[:, i * lane : (i + 1) * lane] for i in range(2 * n_z)]
        even = jnp.concatenate(blocks[0::2], 1)
        odd = jnp.concatenate(blocks[1::2], 1)
        return jnp.where(first_core, even, odd), jnp.where(first_core, odd, even)

    def seq_ordered(pieces):
        stacked = jnp.stack(pieces, 0)
        return jnp.stack([pick(stacked, sq ^ j) for j in range(n_seq)], 0)

    def by_part(weight):
        low = weight.astype(bf16).reshape(own, n_dp, n_seq, own_ff)
        return low.transpose(2, 0, 1, 3).reshape(n_seq, own, ff_part)

    smalls = jnp.pad(
        jnp.concatenate([conv_w, gains], 0).astype(bf16), ((0, own - 5), (0, LANES - own))
    )
    mix = jnp.concatenate([w_in.astype(bf16), w_out.astype(bf16), smalls], 1)
    gate_up = jnp.concatenate([by_part(w_gate), by_part(w_up)], 2)

    residual_low = inputs.reshape(rows, width)
    edge_ids = jnp.pad(segments[:, -2:, None].astype(bf16), ((0, 0), (0, 0), (0, LANES - 1)))
    edge = from_behind(jnp.concatenate([inputs[:, -2:, :], edge_ids], 2), "seq", 1)
    z_parts = [along_z(mix, -k) for k in range(1, n_z)]
    gu_parts = [across_seq(pick(gate_up, sq ^ k), k) for k in range(1, n_seq)]
    low_down = w_down.astype(bf16)
    z_parts, gu_parts, edge, low_down = tie((z_parts, gu_parts, edge, low_down))
    gate_up = seq_ordered([pick(gate_up, sq)] + gu_parts)
    mat_gate_up = lax.all_gather(gate_up, "dp", axis=0).reshape(width, 2 * ff_part)
    mat_down = lax.all_gather(low_down, "dp", axis=0, tiled=True)

    columns = mix.shape[1]

    z_slots = (z + jnp.arange(n_z)) % n_z
    seq_slots = sq ^ jnp.arange(n_seq)
    core_slots = core ^ jnp.arange(2)
    order = list(range(n_seq))
    near = order[1:3] if n_seq == 4 else order[1:]
    last = order[-1]
    grad_top = cotangent.reshape(rows, width)
    z_order = place([part[None] for part in [mix] + z_parts], z_slots, columns // 3)[0]
    mix_parts = swap_near(z_order)
    mix_parts = tie(mix_parts)
    mix_parts.update(swap_far(mix_parts))
    mix_parts, top_out = tie((mix_parts, grad_top))
    mix_parts[0] = z_order
    mix_mine = place([mix_parts[k] for k in range(n_seq)], seq_slots, columns // 3)
    mix_mine = mix_mine.reshape(width // 2, columns)

    mix_other = to_sibling(mix_mine)
    tops = swap_near(top_out)

    cut_in, cut_out = 3 * width, 4 * width
    in_mine, in_other = mix_mine[:, :cut_in], mix_other[:, :cut_in]
    out_mine, out_other = mix_mine[:, cut_in:cut_out], mix_other[:, cut_in:cut_out]

    half = width // 2
    feature = lax.broadcasted_iota(jnp.int32, (1, width), 1)
    lane_of = lax.broadcasted_iota(jnp.int32, (LANES, width), 0)
    spread = (lane_of == feature % own).astype(bf16)

    def row_blocks(which):
        row = lax.broadcasted_iota(jnp.int32, (half, 1), 0) // own
        return ((row // n_seq) * 2 + which) * n_seq + row % n_seq

    def small_rows(packed, which):
        wide = jnp.where(row_blocks(which) == feature // own, dot(packed, spread), 0.0)
        chosen = lax.broadcasted_iota(jnp.int32, (8, half), 1) % own
        chosen = chosen == lax.broadcasted_iota(jnp.int32, (8, half), 0)
        return dot(chosen.astype(bf16), wide.astype(bf16))

    small_all = small_rows(mix_mine[:, cut_out:], core) + small_rows(
        mix_other[:, cut_out:], 1 - core
    )
    taps, gain_vals = small_all[:3], small_all[3:5]

    residual = residual_low.astype(f32)
    unit_one, scale_one, norm_one = normed(residual, gain_vals[0])
    edge_rows = jnp.pad(edge[:, :, :width].reshape(2 * seqs_here, width), ((0, 12), (0, 0)))
    edge_norm = normed(edge_rows.astype(f32), gain_vals[0])[2]
    norm_mine, norm_other = halves(norm_one)
    edge_mine, edge_other = halves(edge_norm)
    projected = dot(jnp.concatenate([norm_mine, edge_mine], 0), in_mine) + dot(
        jnp.concatenate([norm_other, edge_other], 0), in_other
    )
    edge_rows = projected[rows : rows + 2 * seqs_here]
    prev_rows = (edge_rows[:, :width] * edge_rows[:, 2 * width :]).astype(bf16)
    prev_rows = prev_rows.reshape(seqs_here, 2, width)
    projected = projected[:rows]
    first_block = sq == 0
    prev_ids = jnp.where(first_block, -1, edge[:, :, width].astype(jnp.int32))
    b_gate = projected[:, :width]
    c_gate = projected[:, width : 2 * width]
    x_part = projected[:, 2 * width :]
    conv_in = (b_gate * x_part).astype(bf16).reshape(seqs_here, stretch, width)
    extended = jnp.concatenate([prev_rows, conv_in], 1).astype(f32)
    ext_ids = jnp.concatenate([prev_ids, segments], 1)
    near_one = (ext_ids[:, 1:-1] == segments).astype(f32)[..., None]
    near_two = (ext_ids[:, :-2] == segments).astype(f32)[..., None]
    tap_now = extended[:, 2:]
    tap_one = extended[:, 1:-1] * near_one
    tap_two = extended[:, :-2] * near_two
    conv_out = (taps[2] * tap_now + taps[1] * tap_one + taps[0] * tap_two).reshape(rows, width)
    mixed_in = (c_gate * conv_out).astype(bf16)
    mixed_in, tops = tie((mixed_in, tops))
    tops.update(swap_far(tops))
    mixed_mine, mixed_other = halves(mixed_in)
    middle = residual + dot(mixed_mine, out_mine) + dot(mixed_other, out_other)
    unit_two, scale_two, norm_two = normed(middle, gain_vals[1])

    norm_two, tops = tie((norm_two, tops))
    tops[0] = grad_top
    norms = swap_near(norm_two)
    hiddens, act_grads, norm_parts, out_parts = {}, {}, {}, {}

    def hidden_block(k):
        both = dot(norms[k], mat_gate_up)
        gate, up_part = both[:, :ff_part], both[:, ff_part:]
        sigma = jax.nn.sigmoid(gate)
        silu_vals = gate * sigma
        grad_hidden = right_contract(tops[k], mat_down)
        hiddens[k] = (silu_vals * up_part).astype(bf16)
        grad_gate_act = (grad_hidden * up_part * sigma * (1.0 + gate * (1.0 - sigma))).astype(bf16)
        grad_up_act = (grad_hidden * silu_vals).astype(bf16)
        act_grads[k] = jnp.concatenate([grad_gate_act, grad_up_act], 1)

    norms[0] = norm_two
    hidden_block(0)
    norm_parts[0] = right_contract(act_grads[0], mat_gate_up)
    out_parts[0] = dot(hiddens[0], mat_down)
    norms, hiddens, act_grads, norm_parts, out_parts = tie(
        (norms, hiddens, act_grads, norm_parts, out_parts)
    )
    norms.update(swap_far(norms))
    norm_sums = {}
    for k in order[1:-1]:
        hidden_block(k)
        norm_parts[k] = right_contract(act_grads[k], mat_gate_up).astype(bf16)
        norm_sums[k] = across_seq(norm_parts[k], k)
        norms, act_grads, norm_parts = tie((norms, act_grads, norm_parts))
    hidden_block(last)
    last_parts = [
        right_contract(act_grads[last][start : start + rows // 2], mat_gate_up).astype(bf16)
        for start in (0, rows // 2)
    ]
    last_sums = [across_seq(part, last) for part in last_parts]
    early = {k: norm_sums[k] for k in order[1:-2]}
    out_far = [
        dot(hiddens[last][start : start + rows // 2], mat_down).astype(bf16)
        for start in (0, rows // 2)
    ]
    last_parts, hiddens, act_grads, early, out_far, mix_mine, mix_other = tie(
        (last_parts, hiddens, act_grads, early, out_far, mix_mine, mix_other)
    )
    norm_sums.update(early)

    def rows_of(blocks):
        return jnp.concatenate([blocks[k] for k in order], 0)

    grad_down = left_contract(rows_of(hiddens), rows_of(tops)).astype(bf16)
    out_parts.update({k: dot(hiddens[k], mat_down) for k in near})
    halves_of = [part.reshape(n_z, -1, columns) for part in (mix_mine, mix_other)]
    in_full = place(halves_of, core_slots, width, 0, cut_in).reshape(width, cut_in)
    out_full = place(halves_of, core_slots, width, cut_in, width).reshape(width, width)
    out_parts, act_grads, grad_down, last_sums[0], in_full, out_full = tie(
        (out_parts, act_grads, grad_down, last_sums[0], in_full, out_full)
    )
    grad_gate_up = left_contract(rows_of(norms), rows_of(act_grads)).astype(bf16)
    last_sums, norm_sums, grad_gate_up, grad_down = tie(
        (last_sums, norm_sums, grad_gate_up, grad_down)
    )
    gu_sum = lax.psum_scatter(grad_gate_up, "dp", scatter_dimension=0, tiled=True)
    sum_down = lax.psum_scatter(grad_down, "dp", scatter_dimension=0, tiled=True)
    norm_sums[last] = jnp.concatenate(last_sums, 0)
    grad_norm_two = norm_parts[0]
    for k in order[1:]:
        grad_norm_two = grad_norm_two + norm_sums[k].astype(f32)

    back_two, gain_two = norm_back(grad_norm_two, unit_two, scale_two, gain_vals[1])
    grad_middle = grad_top.astype(f32) + back_two
    grad_branch = grad_middle.astype(bf16)
    grad_out_mine = left_contract(mixed_mine, grad_branch)
    grad_out_other = left_contract(mixed_other, grad_branch)
    grad_mixed = right_contract(grad_branch, out_full)
    grad_c = grad_mixed * conv_out
    grad_conv = (grad_mixed * c_gate).reshape(seqs_here, stretch, width)
    grad_taps = [
        jnp.sum(tap_two * grad_conv, (0, 1)),
        jnp.sum(tap_one * grad_conv, (0, 1)),
        jnp.sum(tap_now * grad_conv, (0, 1)),
    ]
    term_now = taps[2] * grad_conv
    term_one = taps[1] * grad_conv * near_one
    term_two = taps[0] * grad_conv * near_two
    grad_ext = (
        jnp.pad(term_now, ((0, 0), (2, 0), (0, 0)))
        + jnp.pad(term_one, ((0, 0), (1, 1), (0, 0)))
        + jnp.pad(term_two, ((0, 0), (0, 2), (0, 0)))
    )
    next_terms = from_behind(grad_ext[:, :2, :], "seq", -1)
    next_terms, out_far = tie((next_terms, out_far))
    out_relay = sum_far(out_far) if n_seq == 4 else ()
    grad_conv_in = (
        grad_ext[:, 2:, :] + jnp.pad(next_terms, ((0, 0), (stretch - 2, 0), (0, 0)))
    ).reshape(rows, width)
    grad_proj = jnp.concatenate([grad_conv_in * x_part, grad_c, grad_conv_in * b_gate], -1).astype(
        bf16
    )
    grad_in_mine = left_contract(norm_mine, grad_proj)
    grad_in_other = left_contract(norm_other, grad_proj)
    grad_norm_one = right_contract(grad_proj, in_full)
    back_one, gain_one = norm_back(grad_norm_one, unit_one, scale_one, gain_vals[0])
    input_grad = (grad_middle + back_one).reshape(seqs_here, stretch, width)

    def sum_core(mine, other):
        return mine + to_sibling(other.astype(bf16)).astype(f32)

    small_grads = jnp.stack(grad_taps + [gain_one, gain_two], 0)
    small_grads = (small_grads + to_sibling(small_grads)).astype(bf16)
    small_wide = jnp.tile(jnp.pad(small_grads, ((0, own - 5), (0, 0))), (half // own, 1))
    small_wide = jnp.where(row_blocks(core) == feature // own, small_wide, 0.0).astype(bf16)
    in_received = to_sibling(grad_in_other.astype(bf16))
    mixed = jnp.concatenate(
        [
            grad_in_mine + in_received.astype(f32),
            sum_core(grad_out_mine, grad_out_other),
            right_contract(small_wide, spread),
        ],
        1,
    ).astype(bf16)
    gu_sum = gu_sum.reshape(n_seq, own, 2 * ff_part)
    gu_parts = [across_seq(pick(gu_sum, sq ^ k), k) for k in range(1, n_seq)]
    mixed, out_relay = tie((mixed, out_relay))
    mixed = mixed.reshape(n_z, n_seq, own, -1)

    def seq_block(index):
        return lax.dynamic_index_in_dim(mixed, index, 1, keepdims=False)

    seq_terms = {k: seq_block(sq ^ k) for k in near}
    if n_seq == 4:
        far_block = seq_block(sq ^ last)
        seq_relay = sum_far((far_block[: n_z // 2], far_block[n_z // 2 :]))
        seq_relay = tie(seq_relay)
        seq_terms = {k: term.astype(f32) for k, term in seq_terms.items()}
        seq_terms = {k: term.astype(bf16) for k, term in add_far(seq_terms, seq_relay).items()}
    seq_parts = [across_seq(seq_terms[k], k) for k in near]
    out_low = add_far({k: out_parts[k] for k in near}, out_relay)
    out_low = {k: term.astype(bf16) for k, term in out_low.items()}
    gu_sum = seq_ordered([pick(gu_sum, sq)] + gu_parts)

    def by_row(part):
        return (
            part.reshape(n_seq, own, n_dp, own_ff)
            .transpose(1, 2, 0, 3)
            .reshape(own, n_seq * ff_part)
        )

    def matrix_step(master, first, second, grad):
        return adamw(master, first, second, grad, learn_rate, weight_decay)

    gate_rows, up_rows = by_row(gu_sum[:, :, :ff_part]), by_row(gu_sum[:, :, ff_part:])
    seq_parts, out_low, gate_rows, up_rows = tie((seq_parts, out_low, gate_rows, up_rows))
    total = seq_block(sq).astype(f32)
    for part in seq_parts:
        total = total + part.astype(f32)
    low = total.astype(bf16)
    low, sum_down = tie((low, sum_down))
    z_sums = [along_z(pick(low, (z + k) % n_z), k) for k in range(1, n_z)]
    out_sums = {k: across_seq(out_low[k], k) for k in near}
    step_gate = matrix_step(w_gate, m_gate, v_gate, gate_rows.astype(f32))
    step_up = matrix_step(w_up, m_up, v_up, up_rows.astype(f32))
    z_sums, step_gate, step_up = tie((z_sums, step_gate, step_up))
    total = pick(total, z)
    for part in z_sums:
        total = total + part.astype(f32)
    sum_in, sum_out, small_sum = total[:, :cut_in], total[:, cut_in:cut_out], total[:, cut_out:]

    output = middle + out_parts[0]
    for k in near:
        output = output + out_sums[k].astype(f32)
    output = output.astype(bf16)

    step_down = matrix_step(w_down, m_down, v_down, sum_down.astype(f32))
    step_in = matrix_step(w_in, m_in, v_in, sum_in)
    step_out = matrix_step(w_out, m_out, v_out, sum_out)
    step_conv = adamw(conv_w, m_conv, v_conv, small_sum[:3, :own], small_rate, 0.0)
    step_gains = adamw(gains, m_gains, v_gains, small_sum[3:5, :own], small_rate, 0.0)
    updated = [step_in, step_out, step_conv, step_gate, step_up, step_down, step_gains]
    new_w = [item[0] for item in updated]
    new_m = [item[1] for item in updated]
    new_v = [item[2] for item in updated]
    return (
        output.reshape(seqs_here, stretch, width),
        input_grad,
        *new_w,
        *new_m,
        *new_v,
    )


def solution(mesh):
    tokens = P("dp", "seq", None)
    matrix = P(("dp", "seq"), None)
    vector = P(None, ("dp", "seq"))
    weights = (matrix, matrix, vector, matrix, matrix, matrix, vector)
    return jax.shard_map(
        local,
        mesh=mesh,
        in_specs=(tokens, tokens, P("dp", "seq")) + weights * 3,
        out_specs=(tokens, tokens) + weights * 3,
        check_vma=False,
    )
```
